32 devices in a mesh: grp: 2 (over core), gx: 8 (over z, x), gy: 2 (over y).
Axes of the slice: x: 2, y: 2, z: 4, core: 2. Of those that a mesh axis runs over, the one named last changes fastest.
Arguments:
- les_velocity: float32 [256, 32, 3, 512], P('gx', 'gy', None, 'grp'), may hold values from -6 to 6
- mean_mach: float32 [128, 32], P('gx', 'gy'), may hold values from 0.2 to 0.6
- transfer_tiles: bfloat16 [64, 2, 2, 64, 64], P('gx', 'gy'), may hold values from -0.75 to 0.75
- intersection_offset: int32 [64], P('gx'), may hold values from -1 to 1, as said below
- acoustic_state: float32 [128, 32, 4, 512], P('gx', 'gy', None, 'grp'), may hold values from -6 to 6
Outputs:
- acoustic_out: float32 [128, 32, 4, 512], P('gx', 'gy', None, 'grp')
The draws below stay inside these ranges and needn't reach their ends.
Inputs may be any that keep to these rules, and one draw needn't show every extreme that they name: `intersection_offset`: each value is -1 or 1. The first block of every gx shard has -1 and the last has 1, except that the first two blocks of the grid have 1 and the last two have -1.
All inputs are finite; a program needn't handle non-finite values.
Results may differ from the reference program's by a relative error of at most 0.018.
Values sent between devices are 32-bit elements; how exact they have to be, the bound alone decides.
No kernel may reach another device: no remote copies, remote signals or barrier semaphores. Data moves between devices by JAX's collectives and lax.ppermute only.
A program may use at most 128 MiB of HBM per device.

```python
import jax
import jax.numpy as jnp
from jax import lax

CYL = 16
STEPS = 2
NBL = 8
PLANE = 64
NXL = 256
NXA = 128
NY = 32
NZ = 512
NBX = 64
NBXA = 32
N_GY = 2


def draw_intersection_offset(key, part):
    coins = jax.random.randint(key, (NBX,), 0, 2).astype(jnp.int32) * 2 - 1
    position = jnp.arange(NBX, dtype=jnp.int32)
    local = position % NBL
    offsets = jnp.where(local == 0, -1, jnp.where(local == NBL - 1, 1, coins))
    offsets = jnp.where(position < 2, 1, jnp.where(position >= NBX - 2, -1, offsets))
    return offsets.astype(jnp.int32)


def draw_acoustic_state(key, part):
    shape = (NXA, NY, 4, NZ)
    values = jax.random.normal(key, shape, jnp.float32)
    return jnp.clip(values, -6.0, 6.0).astype(jnp.float32)


def block_scale(key, dims, pieces, smallest, top_value):
    def one(axis_at, parts):
        heights = jax.random.uniform(jax.random.fold_in(jax.random.fold_in(key, 6), axis_at), (parts,), jnp.float32, smallest / len(pieces), top_value / len(pieces))
        return jnp.repeat(jnp.exp(heights), dims[axis_at] // parts).reshape((-1,) + (1,) * (len(dims) - axis_at - 1))

    level = one(*pieces[0])
    for cut in pieces[1:]:
        level = level * one(*cut)
    return level


def normal_values(key, extent, scale, most, split=(), kind=jnp.bfloat16):
    result = scale * jax.random.normal(key, extent, jnp.float32)
    if split:
        result = result * block_scale(key, extent, split, -0.22, 0.18)
    return jnp.clip(result, -most, most).astype(kind)


def setup_inputs(seed: int = 0) -> dict:
    arg_keys = jax.random.split(jax.random.key(seed), 6)
    les_velocity = normal_values(arg_keys[0], (NXL, NY, 3, NZ), 1.0, 6.0, ((0, 8), (1, 2), (3, 2)), jnp.float32)
    mean_mach = jnp.clip(0.2 + 0.400000021 * jax.random.uniform(arg_keys[1], (NXA, NY), jnp.float32) ** block_scale(arg_keys[1], (NXA, NY), ((0, 8), (1, 2)), -0.2, 0.2), 0.2, 0.6)
    transfer_tiles = normal_values(arg_keys[2], (NBX, N_GY, 2, PLANE, PLANE), PLANE ** -0.5, 0.75, ((0, 8), (1, 2)))
    intersection_offset = draw_intersection_offset(jax.random.fold_in(arg_keys[5], 71), 0)
    acoustic_state = draw_acoustic_state(jax.random.fold_in(arg_keys[5], 71), 0)
    return dict(les_velocity=les_velocity, mean_mach=mean_mach, transfer_tiles=transfer_tiles, intersection_offset=intersection_offset, acoustic_state=acoustic_state)


eddy_step = 0.1
viscosity = 0.5
wave_step = 0.2
filter_weight = 0.2
derivative_weights = (0.770882380518, -0.166705904415, 0.020843142770)
filter_taps = (0.287392842460, -0.226146951809, 0.106303578770, -0.023853048191)
unit_moves = ((1, 0, 0), (0, 1, 0), (0, 0, 1))


def window(array, along_x, along_y, along_z, margin):
    return array[margin + along_x: array.shape[0] - margin + along_x,
                 margin + along_y: array.shape[1] - margin + along_y, :,
                 margin + along_z: array.shape[3] - margin + along_z]


def les_terms(padded):
    center = window(padded, 0, 0, 0, 1)
    grads = []
    laplace = -6.0 * center
    for move in unit_moves:
        ahead = window(padded, move[0], move[1], move[2], 1)
        behind = window(padded, -move[0], -move[1], -move[2], 1)
        grads.append(0.5 * (ahead - behind))
        laplace = laplace + ahead + behind
    vort_x = grads[1][:, :, 2] - grads[2][:, :, 1]
    vort_y = grads[2][:, :, 0] - grads[0][:, :, 2]
    vort_z = grads[0][:, :, 1] - grads[1][:, :, 0]
    lamb = jnp.stack([vort_y * center[:, :, 2] - vort_z * center[:, :, 1],
                      vort_z * center[:, :, 0] - vort_x * center[:, :, 2],
                      vort_x * center[:, :, 1] - vort_y * center[:, :, 0]], axis=2)
    return lamb, laplace


def derivative(padded, move):
    total = None
    for index in range(3):
        reach = index + 1
        ahead = window(padded, reach * move[0], reach * move[1], reach * move[2], 3)
        behind = window(padded, -reach * move[0], -reach * move[1], -reach * move[2], 3)
        term = derivative_weights[index] * (ahead - behind)
        total = term if total is None else total + term
    return total


def rate(padded, mach, source):
    grads = [derivative(padded, move) for move in unit_moves]
    convect = mach[:, :, None, None] * grads[0]
    pressure_rate = -(convect[:, :, 0] + grads[0][:, :, 1] + grads[1][:, :, 2] + grads[2][:, :, 3])
    x_rate = -(convect[:, :, 1] + grads[0][:, :, 0]) - source[:, :, 0]
    y_rate = -(convect[:, :, 2] + grads[1][:, :, 0]) - source[:, :, 1]
    z_rate = -(convect[:, :, 3] + grads[2][:, :, 0]) - source[:, :, 2]
    return jnp.stack([pressure_rate, x_rate, y_rate, z_rate], axis=2)


def smooth(padded):
    center = window(padded, 0, 0, 0, 3)
    total = 3.0 * filter_taps[0] * center
    for move in unit_moves:
        for index in range(1, 4):
            ahead = window(padded, index * move[0], index * move[1], index * move[2], 3)
            behind = window(padded, -index * move[0], -index * move[1], -index * move[2], 3)
            total = total + filter_taps[index] * (ahead + behind)
    return center - filter_weight * total


def pad_three(state):
    return jnp.pad(state, ((3, 3), (3, 3), (0, 0), (3, 3)))


def restrict(source, tiles, offsets):
    depth = source.shape[3]
    target = (jnp.arange(NBX, dtype=jnp.int32) // 2 + offsets).astype(jnp.int32)
    slabs = []
    for slab in range(N_GY):
        part = source[:, slab * CYL:(slab + 1) * CYL]
        blocks = part.reshape(NBX, PLANE, 3 * depth)
        terms = jnp.einsum('bkpq,bpc->bkqc', tiles[:, slab].astype(jnp.float32), blocks.astype(jnp.float32),
                           precision=lax.Precision.HIGHEST)
        bricks = terms[:, 0].reshape(NBXA, 2, PLANE, 3 * depth).sum(axis=1)
        bricks = bricks.at[target].add(terms[:, 1])
        slabs.append(bricks.reshape(NXA, CYL, 3, depth))
    return jnp.concatenate(slabs, axis=1)


def reference(les_velocity, mean_mach, transfer_tiles, intersection_offset, acoustic_state):
    velocity = les_velocity
    sources = []
    for step in range(STEPS):
        lamb, laplace = les_terms(jnp.pad(velocity, ((1, 1), (1, 1), (0, 0), (1, 1))))
        sources.append(restrict(lamb, transfer_tiles, intersection_offset))
        if step + 1 < STEPS:
            velocity = velocity + eddy_step * (viscosity * laplace - lamb)
    state = acoustic_state
    for source in sources:
        first = rate(pad_three(state), mean_mach, source)
        middle = state + wave_step * first
        second = rate(pad_three(middle), mean_mach, source)
        updated = state + 0.5 * wave_step * (first + second)
        state = smooth(pad_three(updated))
    return state
```

```python
import functools

import jax
import jax.numpy as jnp
from jax import lax
from jax.experimental import pallas as pl
from jax.experimental.pallas import tpu as pltpu
from jax.sharding import PartitionSpec as P

MOVED = True

eddy_step = 0.1
viscosity = 0.5
wave_step = 0.2
filter_weight = 0.2
deriv = (0.770882380518, -0.166705904415, 0.02084314277)
taps = (0.28739284246, -0.226146951809, 0.10630357877, -0.023853048191)

RATE_Y, RATE_Z = (0, 2), (0, 3)
ALL = (0, 1, 2, 3)
LANES = 128
VMEM = pl.BlockSpec(memory_space=pltpu.VMEM)
SMEM = pl.BlockSpec(memory_space=pltpu.SMEM)


def lane_ids(rows):
    return lax.broadcasted_iota(jnp.int32, (rows, LANES), 1)


def row_ids(lanes):
    return lax.broadcasted_iota(jnp.int32, (8, lanes), 0)


def call(body, outs, ins, scratch=(), smem=1, flops=1000000):
    shapes = [jax.ShapeDtypeStruct(s, jnp.float32) for s in outs]
    size = sum(o.size for o in shapes) + sum(i.size for i in ins)
    return pl.pallas_call(
        body,
        out_shape=shapes,
        in_specs=[SMEM] * smem + [VMEM] * (len(ins) - smem),
        out_specs=[VMEM] * len(shapes),
        scratch_shapes=list(scratch),
        compiler_params=pltpu.CompilerParams(vmem_limit_bytes=24 * 1024 * 1024),
        cost_estimate=pl.CostEstimate(flops=flops, bytes_accessed=4 * size, transcendentals=0),
    )(*ins)


def shift_tiles(tiles, left, right, by, lanes):
    out = []
    row = [left] + tiles + [right]
    for at in range(1, len(tiles) + 1):
        if by > 0:
            mixed = jnp.where(lanes < by, row[at + 1], row[at])
            out.append(pltpu.roll(mixed, LANES - by, 1))
        else:
            mixed = jnp.where(lanes >= LANES + by, row[at - 1], row[at])
            out.append(pltpu.roll(mixed, -by, 1))
    return out


def side_tiles(packed, at, group, reach, half):
    shift = lax.rem(2 * LANES - group * at - jnp.where(half == 1, reach, 0), LANES)
    tile = pltpu.roll(packed, shift, 1)
    zero = jnp.zeros_like(tile)
    return jnp.where(half == 1, tile, zero), jnp.where(half == 0, tile, zero)


def pack_z(src, dst, comps, layers, group, reach, half, put):
    rows, depth = src.shape[2], src.shape[3]
    lanes = lane_ids(rows)
    start = pl.multiple_of(jnp.where(half == 0, depth - LANES, 0), LANES)

    def step(i, acc):
        shift = lax.rem(group * i + jnp.where(half == 0, reach, 0), LANES)
        inside = (lanes >= group * i) & (lanes < group * (i + 1))
        return tuple(
            jnp.where(inside, pltpu.roll(src[put(c, i) + (slice(None), pl.ds(start, LANES))], shift, 1), a)
            for c, a in zip(comps, acc)
        )

    done = lax.fori_loop(0, layers, step, tuple(jnp.zeros((rows, LANES), jnp.float32) for _ in comps))
    for n, value in enumerate(done):
        dst[n] = value


def pack_state(o, inner, outer, ymsg, zmsg, ycomps, zcomps, info):
    pos, row, half = info[0], info[1], info[2]
    X, Y, Z = o.shape[1:]
    si = jnp.where(pos == 0, X - 3, 0)
    so = jnp.where(pos == 0, 0, X - 3)
    for c in range(4):
        for l in range(3):
            inner[3 * c + l] = o[c, si + l]
            outer[3 * c + l] = o[c, so + l]
    rows = row_ids(Z)
    ys = pl.multiple_of(jnp.where(row == 0, Y - 8, 0), 8)

    def normal(c, i):
        tile = o[c, i, pl.ds(ys, 8), :]
        return jnp.where(row == 0, pltpu.roll(tile, 4, 0), tile)

    def step(i, carry):
        for n in range(len(ycomps) // 2):
            first, second = normal(ycomps[2 * n], i), normal(ycomps[2 * n + 1], i)
            ymsg[n, i] = jnp.where(rows < 4, first, pltpu.roll(second, 4, 0))
        return carry

    lax.fori_loop(0, X, step, 0)
    pack_z(o, zmsg, zcomps, X, LANES // X, 3, half, lambda c, i: (c, i))


def fill(F, f, inner, outer, ymsg, ycomps, info):
    pos, row = info[0], info[1]
    X, Y, Z = f.shape[1:]
    hi = jnp.where(pos == 0, X + 3, 0)
    ho = jnp.where(pos == 0, 0, X + 3)
    for c in range(4):
        for l in range(3):
            F[c, hi + l, 8 : 8 + Y, :] = inner[3 * c + l]
            F[c, ho + l, 8 : 8 + Y, :] = outer[3 * c + l]

    def step(i, carry):
        for c in range(4):
            F[c, i + 3, 8 : 8 + Y, :] = f[c, i]
        for n, c in enumerate(ycomps):
            tile = ymsg[n // 2, i]
            turned = pltpu.roll(tile, 4, 0)
            if n % 2:
                tile, turned = turned, tile
            zero = jnp.zeros_like(tile)
            F[c, i + 3, 0:8, :] = jnp.where(row == 1, turned, zero)
            F[c, i + 3, 8 + Y : 16 + Y, :] = jnp.where(row == 0, tile, zero)
        return carry

    lax.fori_loop(0, X, step, 0)


def dx(F, c, i, Y, lane):
    return sum(deriv[j - 1] * (F[c, i + 3 + j, 8 : 8 + Y, lane] - F[c, i + 3 - j, 8 : 8 + Y, lane]) for j in (1, 2, 3))


def dy(F, c, i, Y, lane):
    return sum(
        deriv[j - 1] * (F[c, i + 3, 8 + j : 8 + Y + j, lane] - F[c, i + 3, 8 - j : 8 + Y - j, lane]) for j in (1, 2, 3)
    )


def z_neighbours(F, c, i, Y, Z, packed, half):
    lanes = lane_ids(Y)
    tiles = [F[c, i + 3, 8 : 8 + Y, pl.ds(t * LANES, LANES)] for t in range(Z // LANES)]
    left, right = side_tiles(packed, i, LANES // (F.shape[1] - 6), 3, half)
    return [
        (shift_tiles(tiles, left, right, j, lanes), shift_tiles(tiles, left, right, -j, lanes)) for j in (1, 2, 3)
    ]


def rate_loop(F, mach, source, zmsg, X, Y, Z, half, emit):
    def step(i, carry):
        zs = []
        for n, c in enumerate(RATE_Z):
            pairs = z_neighbours(F, c, i, Y, Z, zmsg[n], half)
            zs.append(
                [sum(deriv[j] * (pairs[j][0][t] - pairs[j][1][t]) for j in range(3)) for t in range(Z // LANES)]
            )
        for t in range(Z // LANES):
            lane = slice(t * LANES, (t + 1) * LANES)
            m = mach[i]
            gp, gu, gv, gw = (dx(F, c, i, Y, lane) for c in range(4))
            emit(0, i, lane, -(m * gp + gu + dy(F, 2, i, Y, lane) + zs[1][t]))
            emit(1, i, lane, -(m * gu + gp) - source(0, i, lane))
            emit(2, i, lane, -(m * gv + dy(F, 0, i, Y, lane)) - source(1, i, lane))
            emit(3, i, lane, -(m * gw + zs[0][t]) - source(2, i, lane))
        return carry

    lax.fori_loop(0, X, step, 0)


def source_of(S, Y):
    brick = S.shape[2] // Y

    def source(c, i, lane):
        return S[i // brick, c, pl.ds(pl.multiple_of(lax.rem(i, brick) * Y, 8), Y), lane]

    return source


def first_body(info, f, inner, outer, ymsg, zmsg, mach, own, t_in, t_out, o, S, n_in, n_out, ny, nz, F):
    X, Y, Z = f.shape[1:]
    bricks = own.shape[0]
    fill(F, f, inner, outer, ymsg, RATE_Y, info)
    at_in = jnp.where(info[0] == 0, bricks - 1, 0)
    at_out = jnp.where(info[0] == 0, 0, bricks - 1)
    S[...] = own[...]
    layers = own.shape[2] // Y
    for ref, at in ((t_in, at_in), (t_out, at_out)):
        for c in range(3):
            for l in range(layers):
                piece = (at, c, slice(l * Y, (l + 1) * Y))
                S[piece] = S[piece] + ref[c * layers + l]

    def emit(c, i, lane, value):
        o[c, i, :, lane] = f[c, i, :, lane] + wave_step * value

    rate_loop(F, mach, source_of(S, Y), zmsg, X, Y, Z, info[2], emit)
    pack_state(o, n_in, n_out, ny, nz, RATE_Y, RATE_Z, info)


def second_body(info, f, inner, outer, ymsg, zmsg, mach, S, state, *rest, extra):
    if extra:
        t_in, t_out, o, n_in, n_out, ny, nz, F = rest
        for n in range(t_in.shape[0]):
            n_in[12 + n] = t_in[n]
            n_out[12 + n] = t_out[n]
    else:
        o, n_in, n_out, ny, nz, F = rest
    X, Y, Z = f.shape[1:]
    fill(F, f, inner, outer, ymsg, RATE_Y, info)

    def emit(c, i, lane, value):
        o[c, i, :, lane] = 0.5 * (state[c, i, :, lane] + f[c, i, :, lane]) + (0.5 * wave_step) * value

    rate_loop(F, mach, source_of(S, Y), zmsg, X, Y, Z, info[2], emit)
    pack_state(o, n_in, n_out, ny, nz, ALL, ALL, info)


def smooth_body(info, f, inner, outer, ymsg, zmsg, o, *rest):
    F = rest[-1]
    X, Y, Z = f.shape[1:]
    fill(F, f, inner, outer, ymsg, ALL, info)

    def step(i, carry):
        for c in range(4):
            pairs = z_neighbours(F, c, i, Y, Z, zmsg[c], info[2])
            for t in range(Z // LANES):
                lane = slice(t * LANES, (t + 1) * LANES)
                center = F[c, i + 3, 8 : 8 + Y, lane]
                total = (1.0 - 3.0 * filter_weight * taps[0]) * center
                for j in (1, 2, 3):
                    beside = (
                        (F[c, i + 3 + j, 8 : 8 + Y, lane] + F[c, i + 3 - j, 8 : 8 + Y, lane])
                        + (F[c, i + 3, 8 + j : 8 + Y + j, lane] + F[c, i + 3, 8 - j : 8 + Y - j, lane])
                        + (pairs[j - 1][0][t] + pairs[j - 1][1][t])
                    )
                    total = total - (filter_weight * taps[j]) * beside
                o[c, i, :, lane] = total
        return carry

    lax.fori_loop(0, X, step, 0)
    if len(rest) > 1:
        pack_state(o, *rest[:4], RATE_Y, RATE_Z, info)


def pack_body(info, f, inner, outer, ymsg, zmsg):
    pack_state(f, inner, outer, ymsg, zmsg, RATE_Y, RATE_Z, info)


def pack_les(v, inner, outer, ymsg, zmsg, base, info):
    pos, row, half = info[0], info[1], info[2]
    X, _, Y, Z = v.shape
    si = jnp.where(pos == 0, X - 1, 0)
    so = jnp.where(pos == 0, 0, X - 1)
    rows = row_ids(Z)
    ys = pl.multiple_of(jnp.where(row == 0, Y - 8, 0), 8)
    for c in range(3):
        inner[base + c] = v[si, c]
        outer[base + c] = v[so, c]
        for n in range(X // 8):
            acc = jnp.zeros((8, Z), jnp.float32)
            for r in range(8):
                tile = v[8 * n + r, c, pl.ds(ys, 8), :]
                moved = jnp.where(row == 0, pltpu.roll(tile, (r + 1) % 8, 0), pltpu.roll(tile, r, 0) if r else tile)
                acc = jnp.where(rows == r, moved, acc)
            ymsg[c, n] = acc
    pack_z(v, zmsg, (0, 1, 2), X, LANES // X, 1, half, lambda c, i: (i, c))


def pack_les_body(info, v, inner, outer, ymsg, zmsg):
    pack_les(v, inner, outer, ymsg, zmsg, 0, info)


def les_body(info, offset, v, inner, outer, ymsg, zmsg, tiles, *rest, base, advance):
    if advance:
        v1, own, n_in, n_out, ny, nz, V, LB, ACC = rest
    else:
        own, n_in, n_out, V, LB, ACC = rest
    pos, row, half = info[0], info[1], info[2]
    X, _, Y, Z = v.shape
    blocks = LB.shape[1]
    wide = X // blocks
    plane = wide * Y
    bricks = own.shape[0]
    hi = jnp.where(pos == 0, X + 1, 0)
    ho = jnp.where(pos == 0, 0, X + 1)
    for c in range(3):
        V[c, hi, 8 : 8 + Y, :] = inner[base + c]
        V[c, ho, 8 : 8 + Y, :] = outer[base + c]
        for n in range(X // 8):
            tile = ymsg[c, n]
            zero = jnp.zeros_like(tile)
            for r in range(8):
                low = pltpu.roll(tile, 7 - r, 0) if r < 7 else tile
                high = pltpu.roll(tile, 8 - r, 0) if r else tile
                V[c, 8 * n + r + 1, 0:8, :] = jnp.where(row == 1, low, zero)
                V[c, 8 * n + r + 1, 8 + Y : 16 + Y, :] = jnp.where(row == 0, high, zero)

    def copy(i, carry):
        for c in range(3):
            V[c, i + 1, 8 : 8 + Y, :] = v[i, c]
        return carry

    lax.fori_loop(0, X, copy, 0)
    ACC[...] = jnp.zeros_like(ACC)
    lanes = lane_ids(Y)
    count = Z // LANES

    def step(i, carry):
        center = [[V[c, i + 1, 8 : 8 + Y, pl.ds(t * LANES, LANES)] for t in range(count)] for c in range(3)]
        ahead, behind = [], []
        for c in range(3 if advance else 2):
            left, right = side_tiles(zmsg[c], i, LANES // X, 1, half)
            ahead.append(shift_tiles(center[c], left, right, 1, lanes))
            behind.append(shift_tiles(center[c], left, right, -1, lanes))
        at = lax.rem(i, wide) * Y
        b = i // wide
        for t in range(count):
            lane = slice(t * LANES, (t + 1) * LANES)
            xa = [V[c, i + 2, 8 : 8 + Y, lane] for c in range(3)]
            xb = [V[c, i, 8 : 8 + Y, lane] for c in range(3)]
            ya = [V[c, i + 1, 9 : 9 + Y, lane] for c in range(3)]
            yb = [V[c, i + 1, 7 : 7 + Y, lane] for c in range(3)]
            u, w, q = center[0][t], center[1][t], center[2][t]
            vx = 0.5 * ((ya[2] - yb[2]) - (ahead[1][t] - behind[1][t]))
            vy = 0.5 * ((ahead[0][t] - behind[0][t]) - (xa[2] - xb[2]))
            vz = 0.5 * ((xa[1] - xb[1]) - (ya[0] - yb[0]))
            lamb = [vy * q - vz * w, vz * u - vx * q, vx * w - vy * u]
            for c in range(3):
                high = lamb[c].astype(jnp.bfloat16)
                low = (lamb[c] - high.astype(jnp.float32)).astype(jnp.bfloat16)
                LB[c, b, pl.ds(pl.multiple_of(at, 16), Y), lane] = high
                LB[c, b, pl.ds(pl.multiple_of(plane + at, 16), Y), lane] = low
                if advance:
                    laplace = -6.0 * center[c][t] + ((xa[c] + xb[c]) + (ya[c] + yb[c]) + (ahead[c][t] + behind[c][t]))
                    v1[i, c, :, lane] = center[c][t] + eddy_step * (viscosity * laplace - lamb[c])
        return carry

    lax.fori_loop(0, X, step, 0)

    def restrict(b, carry):
        tile = tiles[b].astype(jnp.bfloat16)
        m = b // 2 + 1
        to = m + offset[b]
        for c in range(3):
            both = jnp.dot(tile, LB[c, b], preferred_element_type=jnp.float32)
            ACC[m, c] = ACC[m, c] + both[:plane]
            ACC[to, c] = ACC[to, c] + both[plane:]
        return carry

    lax.fori_loop(0, blocks, restrict, 0)
    own[...] = ACC[1 : bricks + 1]
    ti = jnp.where(pos == 0, bricks + 1, 0)
    to = jnp.where(pos == 0, 0, bricks + 1)
    layers = plane // Y
    for c in range(3):
        for l in range(layers):
            n_in[c * layers + l] = ACC[ti, c, l * Y : (l + 1) * Y, :]
            n_out[c * layers + l] = ACC[to, c, l * Y : (l + 1) * Y, :]
    if advance:
        pack_les(v1, n_in, n_out, ny, nz, 3 * layers, info)


def solution(mesh):
    axes = mesh.axis_names
    sizes = [mesh.shape[a] for a in axes]
    gx = mesh.shape["gx"]

    def flat(**at):
        index = 0
        for axis, size in zip(axes, sizes):
            index = index * size + at[axis]
        return index

    cells = [(k, p, y, c) for k in range(gx // 2) for p in (0, 1) for y in range(mesh.shape["gy"]) for c in (0, 1)]

    def home(g, y, a):
        return flat(gx=2 * (g // 2) + a, gy=y, grp=g % 2)

    move = [(flat(gx=2 * k + p, gy=y, grp=c), home(2 * k + p, y, c)) for k, p, y, c in cells]
    back = [(target, source) for source, target in move]
    swap = [(0, 1), (1, 0)]
    even = [pair for k in range(gx // 2) for pair in ((2 * k, 2 * k + 1), (2 * k + 1, 2 * k))]
    odd = [pair for k in range(gx // 2 - 1) for pair in ((2 * k + 1, 2 * k + 2), (2 * k + 2, 2 * k + 1))]
    hop = [(home(s, y, a), home(d, y, a)) for s, d in odd for y in range(mesh.shape["gy"]) for a in (0, 1)]

    def send(inner, outer, ymsg, zmsg):
        if MOVED:
            outer = lax.ppermute(outer, axes, hop)
            zmsg = lax.ppermute(zmsg, "gx", even)
            ymsg = lax.ppermute(ymsg, "gy", swap)
            inner = lax.ppermute(inner, "grp", swap)
        else:
            outer = lax.ppermute(outer, "gx", odd)
            inner = lax.ppermute(inner, "gx", even)
            ymsg = lax.ppermute(ymsg, "gy", swap)
            zmsg = lax.ppermute(zmsg, "grp", swap)
        return inner, outer, ymsg, zmsg

    def body(les_velocity, mean_mach, transfer_tiles, intersection_offset, acoustic_state):
        X2, Y, _, Z = les_velocity.shape
        X = acoustic_state.shape[0]
        blocks, plane = transfer_tiles.shape[0], transfer_tiles.shape[-1]
        bricks = blocks // 2
        layers = plane // Y
        position, parity = lax.axis_index("grp"), lax.axis_index("gx") % 2
        if not MOVED:
            position, parity = parity, position
        info = jnp.stack([position, lax.axis_index("gy"), parity]).astype(jnp.int32)

        v = les_velocity.transpose(0, 2, 1, 3)
        state = acoustic_state.transpose(2, 0, 1, 3)
        tiles = transfer_tiles[:, 0].astype(jnp.float32).swapaxes(2, 3).reshape(blocks, 2 * plane, plane)
        mach, offset = mean_mach, intersection_offset
        if MOVED:
            v = lax.ppermute(v, axes, move)
            small = jnp.concatenate(
                [
                    tiles.reshape(-1, LANES),
                    jnp.pad(mach, ((0, 0), (0, LANES - Y))),
                    jnp.pad(offset.astype(jnp.float32)[None], ((0, 7), (0, LANES - blocks))),
                ]
            )
            small = lax.ppermute(small, axes, move)
            state = lax.ppermute(state, axes, move)
            tall = tiles.size // LANES
            tiles = small[:tall].reshape(blocks, 2 * plane, plane)
            mach = small[tall : tall + X, :Y]
            offset = small[tall + X, :blocks].astype(jnp.int32)
        tiles = jnp.concatenate([tiles, tiles], axis=2)
        mach = jnp.broadcast_to(mach[:, :, None], (X, Y, LANES))

        edge_x = (12, Y, Z)
        edge_y, edge_yy = (1, X, 8, Z), (2, X, 8, Z)
        edge_z, edge_zz = (2, Y, LANES), (4, Y, LANES)
        les_y, les_z = (3, X2 // 8, 8, Z), (3, Y, LANES)
        F = pltpu.VMEM((4, X + 6, Y + 16, Z), jnp.float32)
        les_scratch = [
            pltpu.VMEM((3, X2 + 2, Y + 16, Z), jnp.float32),
            pltpu.VMEM((3, blocks, 2 * plane, Z), jnp.bfloat16),
            pltpu.VMEM((bricks + 2, 3, plane, Z), jnp.float32),
        ]
        grid = state.shape
        own_shape = (bricks, 3, plane, Z)
        term = (3 * layers, Y, Z)

        les_edges = send(*call(pack_les_body, [(3, Y, Z), (3, Y, Z), les_y, les_z], [info, v]))
        state_edges = send(*call(pack_body, [edge_x, edge_x, edge_y, edge_z], [info, state]))
        with_terms = (3 * layers + 3, Y, Z)
        v1, own, *edges = call(
            functools.partial(les_body, base=0, advance=True),
            [v.shape, own_shape, with_terms, with_terms, les_y, les_z],
            [info, offset, v, *les_edges, tiles],
            les_scratch,
            smem=2,
            flops=4000000,
        )
        edges = send(*edges)
        middle, S, *middle_edges = call(
            first_body,
            [grid, own_shape, edge_x, edge_x, edge_y, edge_z],
            [info, state, *state_edges, mach, own, edges[0], edges[1]],
            [F],
            flops=4000000,
        )
        middle_edges = send(*middle_edges)
        own2, up2, down2 = call(
            functools.partial(les_body, base=3 * layers, advance=False),
            [own_shape, term, term],
            [info, offset, v1, *edges, tiles],
            les_scratch,
            smem=2,
            flops=4000000,
        )
        edge_t = (12 + 3 * layers, Y, Z)
        updated, *up_edges = call(
            functools.partial(second_body, extra=True),
            [grid, edge_t, edge_t, edge_yy, edge_zz],
            [info, middle, *middle_edges, mach, S, state, up2, down2],
            [F],
            flops=4000000,
        )
        up_edges = send(*up_edges)
        state, *state_edges = call(
            smooth_body, [grid, edge_x, edge_x, edge_y, edge_z], [info, updated, *up_edges], [F], flops=4000000
        )
        state_edges = send(*state_edges)
        middle, S, *middle_edges = call(
            first_body,
            [grid, own_shape, edge_x, edge_x, edge_y, edge_z],
            [info, state, *state_edges, mach, own2, up_edges[0][12:], up_edges[1][12:]],
            [F],
            flops=4000000,
        )
        middle_edges = send(*middle_edges)
        updated, *up_edges = call(
            functools.partial(second_body, extra=False),
            [grid, edge_x, edge_x, edge_yy, edge_zz],
            [info, middle, *middle_edges, mach, S, state],
            [F],
            flops=4000000,
        )
        up_edges = send(*up_edges)
        (state,) = call(smooth_body, [grid], [info, updated, *up_edges], [F], flops=4000000)
        if MOVED:
            state = lax.ppermute(state, axes, back)
        return state.transpose(1, 2, 0, 3)

    placed = (
        P("gx", "gy", None, "grp"),
        P("gx", "gy"),
        P("gx", "gy", None, None, None),
        P("gx"),
        P("gx", "gy", None, "grp"),
    )
    return jax.shard_map(body, mesh=mesh, in_specs=placed, out_specs=P("gx", "gy", None, "grp"), check_vma=False)
```

```python
import functools

import jax
import jax.numpy as jnp
from jax import lax
from jax.experimental import pallas as pl
from jax.experimental.pallas import tpu as pltpu
from jax.sharding import PartitionSpec as P

MOVED = False

eddy_step = 0.1
viscosity = 0.5
wave_step = 0.2
filter_weight = 0.2
deriv = (0.770882380518, -0.166705904415, 0.02084314277)
taps = (0.28739284246, -0.226146951809, 0.10630357877, -0.023853048191)

RATE_Y, RATE_Z = (0, 2), (0, 3)
ALL = (0, 1, 2, 3)
LANES = 128
VMEM = pl.BlockSpec(memory_space=pltpu.VMEM)
SMEM = pl.BlockSpec(memory_space=pltpu.SMEM)


def lane_ids(rows):
    return lax.broadcasted_iota(jnp.int32, (rows, LANES), 1)


def row_ids(lanes):
    return lax.broadcasted_iota(jnp.int32, (8, lanes), 0)


def call(body, outs, ins, scratch=(), smem=1, flops=1000000):
    shapes = [jax.ShapeDtypeStruct(s, jnp.float32) for s in outs]
    size = sum(o.size for o in shapes) + sum(i.size for i in ins)
    return pl.pallas_call(
        body,
        out_shape=shapes,
        in_specs=[SMEM] * smem + [VMEM] * (len(ins) - smem),
        out_specs=[VMEM] * len(shapes),
        scratch_shapes=list(scratch),
        compiler_params=pltpu.CompilerParams(vmem_limit_bytes=24 * 1024 * 1024),
        cost_estimate=pl.CostEstimate(flops=flops, bytes_accessed=4 * size, transcendentals=0),
    )(*ins)


def shift_tiles(tiles, left, right, by, lanes):
    out = []
    row = [left] + tiles + [right]
    for at in range(1, len(tiles) + 1):
        if by > 0:
            mixed = jnp.where(lanes < by, row[at + 1], row[at])
            out.append(pltpu.roll(mixed, LANES - by, 1))
        else:
            mixed = jnp.where(lanes >= LANES + by, row[at - 1], row[at])
            out.append(pltpu.roll(mixed, -by, 1))
    return out


def side_tiles(packed, at, group, reach, half):
    shift = lax.rem(2 * LANES - group * at - jnp.where(half == 1, reach, 0), LANES)
    tile = pltpu.roll(packed, shift, 1)
    zero = jnp.zeros_like(tile)
    return jnp.where(half == 1, tile, zero), jnp.where(half == 0, tile, zero)


def pack_z(src, dst, comps, layers, group, reach, half, put):
    rows, depth = src.shape[2], src.shape[3]
    lanes = lane_ids(rows)
    start = pl.multiple_of(jnp.where(half == 0, depth - LANES, 0), LANES)

    def step(i, acc):
        shift = lax.rem(group * i + jnp.where(half == 0, reach, 0), LANES)
        inside = (lanes >= group * i) & (lanes < group * (i + 1))
        return tuple(
            jnp.where(inside, pltpu.roll(src[put(c, i) + (slice(None), pl.ds(start, LANES))], shift, 1), a)
            for c, a in zip(comps, acc)
        )

    done = lax.fori_loop(0, layers, step, tuple(jnp.zeros((rows, LANES), jnp.float32) for _ in comps))
    for n, value in enumerate(done):
        dst[n] = value


def pack_state(o, inner, outer, ymsg, zmsg, ycomps, zcomps, info):
    pos, row, half = info[0], info[1], info[2]
    X, Y, Z = o.shape[1:]
    si = jnp.where(pos == 0, X - 3, 0)
    so = jnp.where(pos == 0, 0, X - 3)
    for c in range(4):
        for l in range(3):
            inner[3 * c + l] = o[c, si + l]
            outer[3 * c + l] = o[c, so + l]
    rows = row_ids(Z)
    ys = pl.multiple_of(jnp.where(row == 0, Y - 8, 0), 8)

    def normal(c, i):
        tile = o[c, i, pl.ds(ys, 8), :]
        return jnp.where(row == 0, pltpu.roll(tile, 4, 0), tile)

    def step(i, carry):
        for n in range(len(ycomps) // 2):
            first, second = normal(ycomps[2 * n], i), normal(ycomps[2 * n + 1], i)
            ymsg[n, i] = jnp.where(rows < 4, first, pltpu.roll(second, 4, 0))
        return carry

    lax.fori_loop(0, X, step, 0)
    pack_z(o, zmsg, zcomps, X, LANES // X, 3, half, lambda c, i: (c, i))


def fill(F, f, inner, outer, ymsg, ycomps, info):
    pos, row = info[0], info[1]
    X, Y, Z = f.shape[1:]
    hi = jnp.where(pos == 0, X + 3, 0)
    ho = jnp.where(pos == 0, 0, X + 3)
    for c in range(4):
        for l in range(3):
            F[c, hi + l, 8 : 8 + Y, :] = inner[3 * c + l]
            F[c, ho + l, 8 : 8 + Y, :] = outer[3 * c + l]

    def step(i, carry):
        for c in range(4):
            F[c, i + 3, 8 : 8 + Y, :] = f[c, i]
        for n, c in enumerate(ycomps):
            tile = ymsg[n // 2, i]
            turned = pltpu.roll(tile, 4, 0)
            if n % 2:
                tile, turned = turned, tile
            zero = jnp.zeros_like(tile)
            F[c, i + 3, 0:8, :] = jnp.where(row == 1, turned, zero)
            F[c, i + 3, 8 + Y : 16 + Y, :] = jnp.where(row == 0, tile, zero)
        return carry

    lax.fori_loop(0, X, step, 0)


def dx(F, c, i, Y, lane):
    return sum(deriv[j - 1] * (F[c, i + 3 + j, 8 : 8 + Y, lane] - F[c, i + 3 - j, 8 : 8 + Y, lane]) for j in (1, 2, 3))


def dy(F, c, i, Y, lane):
    return sum(
        deriv[j - 1] * (F[c, i + 3, 8 + j : 8 + Y + j, lane] - F[c, i + 3, 8 - j : 8 + Y - j, lane]) for j in (1, 2, 3)
    )


def z_neighbours(F, c, i, Y, Z, packed, half):
    lanes = lane_ids(Y)
    tiles = [F[c, i + 3, 8 : 8 + Y, pl.ds(t * LANES, LANES)] for t in range(Z // LANES)]
    left, right = side_tiles(packed, i, LANES // (F.shape[1] - 6), 3, half)
    return [
        (shift_tiles(tiles, left, right, j, lanes), shift_tiles(tiles, left, right, -j, lanes)) for j in (1, 2, 3)
    ]


def rate_loop(F, mach, source, zmsg, X, Y, Z, half, emit):
    def step(i, carry):
        zs = []
        for n, c in enumerate(RATE_Z):
            pairs = z_neighbours(F, c, i, Y, Z, zmsg[n], half)
            zs.append(
                [sum(deriv[j] * (pairs[j][0][t] - pairs[j][1][t]) for j in range(3)) for t in range(Z // LANES)]
            )
        for t in range(Z // LANES):
            lane = slice(t * LANES, (t + 1) * LANES)
            m = mach[i]
            gp, gu, gv, gw = (dx(F, c, i, Y, lane) for c in range(4))
            emit(0, i, lane, -(m * gp + gu + dy(F, 2, i, Y, lane) + zs[1][t]))
            emit(1, i, lane, -(m * gu + gp) - source(0, i, lane))
            emit(2, i, lane, -(m * gv + dy(F, 0, i, Y, lane)) - source(1, i, lane))
            emit(3, i, lane, -(m * gw + zs[0][t]) - source(2, i, lane))
        return carry

    lax.fori_loop(0, X, step, 0)


def source_of(S, Y):
    brick = S.shape[2] // Y

    def source(c, i, lane):
        return S[i // brick, c, pl.ds(pl.multiple_of(lax.rem(i, brick) * Y, 8), Y), lane]

    return source


def first_body(info, f, inner, outer, ymsg, zmsg, mach, own, t_in, t_out, o, S, n_in, n_out, ny, nz, F):
    X, Y, Z = f.shape[1:]
    bricks = own.shape[0]
    fill(F, f, inner, outer, ymsg, RATE_Y, info)
    at_in = jnp.where(info[0] == 0, bricks - 1, 0)
    at_out = jnp.where(info[0] == 0, 0, bricks - 1)
    S[...] = own[...]
    layers = own.shape[2] // Y
    for ref, at in ((t_in, at_in), (t_out, at_out)):
        for c in range(3):
            for l in range(layers):
                piece = (at, c, slice(l * Y, (l + 1) * Y))
                S[piece] = S[piece] + ref[c * layers + l]

    def emit(c, i, lane, value):
        o[c, i, :, lane] = f[c, i, :, lane] + wave_step * value

    rate_loop(F, mach, source_of(S, Y), zmsg, X, Y, Z, info[2], emit)
    pack_state(o, n_in, n_out, ny, nz, RATE_Y, RATE_Z, info)


def second_body(info, f, inner, outer, ymsg, zmsg, mach, S, state, *rest, extra):
    if extra:
        t_in, t_out, o, n_in, n_out, ny, nz, F = rest
        for n in range(t_in.shape[0]):
            n_in[12 + n] = t_in[n]
            n_out[12 + n] = t_out[n]
    else:
        o, n_in, n_out, ny, nz, F = rest
    X, Y, Z = f.shape[1:]
    fill(F, f, inner, outer, ymsg, RATE_Y, info)

    def emit(c, i, lane, value):
        o[c, i, :, lane] = 0.5 * (state[c, i, :, lane] + f[c, i, :, lane]) + (0.5 * wave_step) * value

    rate_loop(F, mach, source_of(S, Y), zmsg, X, Y, Z, info[2], emit)
    pack_state(o, n_in, n_out, ny, nz, ALL, ALL, info)


def smooth_body(info, f, inner, outer, ymsg, zmsg, o, *rest):
    F = rest[-1]
    X, Y, Z = f.shape[1:]
    fill(F, f, inner, outer, ymsg, ALL, info)

    def step(i, carry):
        for c in range(4):
            pairs = z_neighbours(F, c, i, Y, Z, zmsg[c], info[2])
            for t in range(Z // LANES):
                lane = slice(t * LANES, (t + 1) * LANES)
                center = F[c, i + 3, 8 : 8 + Y, lane]
                total = (1.0 - 3.0 * filter_weight * taps[0]) * center
                for j in (1, 2, 3):
                    beside = (
                        (F[c, i + 3 + j, 8 : 8 + Y, lane] + F[c, i + 3 - j, 8 : 8 + Y, lane])
                        + (F[c, i + 3, 8 + j : 8 + Y + j, lane] + F[c, i + 3, 8 - j : 8 + Y - j, lane])
                        + (pairs[j - 1][0][t] + pairs[j - 1][1][t])
                    )
                    total = total - (filter_weight * taps[j]) * beside
                o[c, i, :, lane] = total
        return carry

    lax.fori_loop(0, X, step, 0)
    if len(rest) > 1:
        pack_state(o, *rest[:4], RATE_Y, RATE_Z, info)


def pack_body(info, f, inner, outer, ymsg, zmsg):
    pack_state(f, inner, outer, ymsg, zmsg, RATE_Y, RATE_Z, info)


def pack_les(v, inner, outer, ymsg, zmsg, base, info):
    pos, row, half = info[0], info[1], info[2]
    X, _, Y, Z = v.shape
    si = jnp.where(pos == 0, X - 1, 0)
    so = jnp.where(pos == 0, 0, X - 1)
    rows = row_ids(Z)
    ys = pl.multiple_of(jnp.where(row == 0, Y - 8, 0), 8)
    for c in range(3):
        inner[base + c] = v[si, c]
        outer[base + c] = v[so, c]
        for n in range(X // 8):
            acc = jnp.zeros((8, Z), jnp.float32)
            for r in range(8):
                tile = v[8 * n + r, c, pl.ds(ys, 8), :]
                moved = jnp.where(row == 0, pltpu.roll(tile, (r + 1) % 8, 0), pltpu.roll(tile, r, 0) if r else tile)
                acc = jnp.where(rows == r, moved, acc)
            ymsg[c, n] = acc
    pack_z(v, zmsg, (0, 1, 2), X, LANES // X, 1, half, lambda c, i: (i, c))


def pack_les_body(info, v, inner, outer, ymsg, zmsg):
    pack_les(v, inner, outer, ymsg, zmsg, 0, info)


def les_body(info, offset, v, inner, outer, ymsg, zmsg, tiles, *rest, base, advance):
    if advance:
        v1, own, n_in, n_out, ny, nz, V, LB, ACC = rest
    else:
        own, n_in, n_out, V, LB, ACC = rest
    pos, row, half = info[0], info[1], info[2]
    X, _, Y, Z = v.shape
    blocks = LB.shape[1]
    wide = X // blocks
    plane = wide * Y
    bricks = own.shape[0]
    hi = jnp.where(pos == 0, X + 1, 0)
    ho = jnp.where(pos == 0, 0, X + 1)
    for c in range(3):
        V[c, hi, 8 : 8 + Y, :] = inner[base + c]
        V[c, ho, 8 : 8 + Y, :] = outer[base + c]
        for n in range(X // 8):
            tile = ymsg[c, n]
            zero = jnp.zeros_like(tile)
            for r in range(8):
                low = pltpu.roll(tile, 7 - r, 0) if r < 7 else tile
                high = pltpu.roll(tile, 8 - r, 0) if r else tile
                V[c, 8 * n + r + 1, 0:8, :] = jnp.where(row == 1, low, zero)
                V[c, 8 * n + r + 1, 8 + Y : 16 + Y, :] = jnp.where(row == 0, high, zero)

    def copy(i, carry):
        for c in range(3):
            V[c, i + 1, 8 : 8 + Y, :] = v[i, c]
        return carry

    lax.fori_loop(0, X, copy, 0)
    ACC[...] = jnp.zeros_like(ACC)
    lanes = lane_ids(Y)
    count = Z // LANES

    def step(i, carry):
        center = [[V[c, i + 1, 8 : 8 + Y, pl.ds(t * LANES, LANES)] for t in range(count)] for c in range(3)]
        ahead, behind = [], []
        for c in range(3 if advance else 2):
            left, right = side_tiles(zmsg[c], i, LANES // X, 1, half)
            ahead.append(shift_tiles(center[c], left, right, 1, lanes))
            behind.append(shift_tiles(center[c], left, right, -1, lanes))
        at = lax.rem(i, wide) * Y
        b = i // wide
        for t in range(count):
            lane = slice(t * LANES, (t + 1) * LANES)
            xa = [V[c, i + 2, 8 : 8 + Y, lane] for c in range(3)]
            xb = [V[c, i, 8 : 8 + Y, lane] for c in range(3)]
            ya = [V[c, i + 1, 9 : 9 + Y, lane] for c in range(3)]
            yb = [V[c, i + 1, 7 : 7 + Y, lane] for c in range(3)]
            u, w, q = center[0][t], center[1][t], center[2][t]
            vx = 0.5 * ((ya[2] - yb[2]) - (ahead[1][t] - behind[1][t]))
            vy = 0.5 * ((ahead[0][t] - behind[0][t]) - (xa[2] - xb[2]))
            vz = 0.5 * ((xa[1] - xb[1]) - (ya[0] - yb[0]))
            lamb = [vy * q - vz * w, vz * u - vx * q, vx * w - vy * u]
            for c in range(3):
                high = lamb[c].astype(jnp.bfloat16)
                low = (lamb[c] - high.astype(jnp.float32)).astype(jnp.bfloat16)
                LB[c, b, pl.ds(pl.multiple_of(at, 16), Y), lane] = high
                LB[c, b, pl.ds(pl.multiple_of(plane + at, 16), Y), lane] = low
                if advance:
                    laplace = -6.0 * center[c][t] + ((xa[c] + xb[c]) + (ya[c] + yb[c]) + (ahead[c][t] + behind[c][t]))
                    v1[i, c, :, lane] = center[c][t] + eddy_step * (viscosity * laplace - lamb[c])
        return carry

    lax.fori_loop(0, X, step, 0)

    def restrict(b, carry):
        tile = tiles[b].astype(jnp.bfloat16)
        m = b // 2 + 1
        to = m + offset[b]
        for c in range(3):
            both = jnp.dot(tile, LB[c, b], preferred_element_type=jnp.float32)
            ACC[m, c] = ACC[m, c] + both[:plane]
            ACC[to, c] = ACC[to, c] + both[plane:]
        return carry

    lax.fori_loop(0, blocks, restrict, 0)
    own[...] = ACC[1 : bricks + 1]
    ti = jnp.where(pos == 0, bricks + 1, 0)
    to = jnp.where(pos == 0, 0, bricks + 1)
    layers = plane // Y
    for c in range(3):
        for l in range(layers):
            n_in[c * layers + l] = ACC[ti, c, l * Y : (l + 1) * Y, :]
            n_out[c * layers + l] = ACC[to, c, l * Y : (l + 1) * Y, :]
    if advance:
        pack_les(v1, n_in, n_out, ny, nz, 3 * layers, info)


def solution(mesh):
    axes = mesh.axis_names
    sizes = [mesh.shape[a] for a in axes]
    gx = mesh.shape["gx"]

    def flat(**at):
        index = 0
        for axis, size in zip(axes, sizes):
            index = index * size + at[axis]
        return index

    cells = [(k, p, y, c) for k in range(gx // 2) for p in (0, 1) for y in range(mesh.shape["gy"]) for c in (0, 1)]

    def home(g, y, a):
        return flat(gx=2 * (g // 2) + a, gy=y, grp=g % 2)

    move = [(flat(gx=2 * k + p, gy=y, grp=c), home(2 * k + p, y, c)) for k, p, y, c in cells]
    back = [(target, source) for source, target in move]
    swap = [(0, 1), (1, 0)]
    even = [pair for k in range(gx // 2) for pair in ((2 * k, 2 * k + 1), (2 * k + 1, 2 * k))]
    odd = [pair for k in range(gx // 2 - 1) for pair in ((2 * k + 1, 2 * k + 2), (2 * k + 2, 2 * k + 1))]
    hop = [(home(s, y, a), home(d, y, a)) for s, d in odd for y in range(mesh.shape["gy"]) for a in (0, 1)]

    def send(inner, outer, ymsg, zmsg):
        if MOVED:
            outer = lax.ppermute(outer, axes, hop)
            zmsg = lax.ppermute(zmsg, "gx", even)
            ymsg = lax.ppermute(ymsg, "gy", swap)
            inner = lax.ppermute(inner, "grp", swap)
        else:
            outer = lax.ppermute(outer, "gx", odd)
            inner = lax.ppermute(inner, "gx", even)
            ymsg = lax.ppermute(ymsg, "gy", swap)
            zmsg = lax.ppermute(zmsg, "grp", swap)
        return inner, outer, ymsg, zmsg

    def body(les_velocity, mean_mach, transfer_tiles, intersection_offset, acoustic_state):
        X2, Y, _, Z = les_velocity.shape
        X = acoustic_state.shape[0]
        blocks, plane = transfer_tiles.shape[0], transfer_tiles.shape[-1]
        bricks = blocks // 2
        layers = plane // Y
        position, parity = lax.axis_index("grp"), lax.axis_index("gx") % 2
        if not MOVED:
            position, parity = parity, position
        info = jnp.stack([position, lax.axis_index("gy"), parity]).astype(jnp.int32)

        v = les_velocity.transpose(0, 2, 1, 3)
        state = acoustic_state.transpose(2, 0, 1, 3)
        tiles = transfer_tiles[:, 0].astype(jnp.float32).swapaxes(2, 3).reshape(blocks, 2 * plane, plane)
        mach, offset = mean_mach, intersection_offset
        if MOVED:
            v = lax.ppermute(v, axes, move)
            small = jnp.concatenate(
                [
                    tiles.reshape(-1, LANES),
                    jnp.pad(mach, ((0, 0), (0, LANES - Y))),
                    jnp.pad(offset.astype(jnp.float32)[None], ((0, 7), (0, LANES - blocks))),
                ]
            )
            small = lax.ppermute(small, axes, move)
            state = lax.ppermute(state, axes, move)
            tall = tiles.size // LANES
            tiles = small[:tall].reshape(blocks, 2 * plane, plane)
            mach = small[tall : tall + X, :Y]
            offset = small[tall + X, :blocks].astype(jnp.int32)
        tiles = jnp.concatenate([tiles, tiles], axis=2)
        mach = jnp.broadcast_to(mach[:, :, None], (X, Y, LANES))

        edge_x = (12, Y, Z)
        edge_y, edge_yy = (1, X, 8, Z), (2, X, 8, Z)
        edge_z, edge_zz = (2, Y, LANES), (4, Y, LANES)
        les_y, les_z = (3, X2 // 8, 8, Z), (3, Y, LANES)
        F = pltpu.VMEM((4, X + 6, Y + 16, Z), jnp.float32)
        les_scratch = [
            pltpu.VMEM((3, X2 + 2, Y + 16, Z), jnp.float32),
            pltpu.VMEM((3, blocks, 2 * plane, Z), jnp.bfloat16),
            pltpu.VMEM((bricks + 2, 3, plane, Z), jnp.float32),
        ]
        grid = state.shape
        own_shape = (bricks, 3, plane, Z)
        term = (3 * layers, Y, Z)

        les_edges = send(*call(pack_les_body, [(3, Y, Z), (3, Y, Z), les_y, les_z], [info, v]))
        state_edges = send(*call(pack_body, [edge_x, edge_x, edge_y, edge_z], [info, state]))
        with_terms = (3 * layers + 3, Y, Z)
        v1, own, *edges = call(
            functools.partial(les_body, base=0, advance=True),
            [v.shape, own_shape, with_terms, with_terms, les_y, les_z],
            [info, offset, v, *les_edges, tiles],
            les_scratch,
            smem=2,
            flops=4000000,
        )
        edges = send(*edges)
        middle, S, *middle_edges = call(
            first_body,
            [grid, own_shape, edge_x, edge_x, edge_y, edge_z],
            [info, state, *state_edges, mach, own, edges[0], edges[1]],
            [F],
            flops=4000000,
        )
        middle_edges = send(*middle_edges)
        own2, up2, down2 = call(
            functools.partial(les_body, base=3 * layers, advance=False),
            [own_shape, term, term],
            [info, offset, v1, *edges, tiles],
            les_scratch,
            smem=2,
            flops=4000000,
        )
        edge_t = (12 + 3 * layers, Y, Z)
        updated, *up_edges = call(
            functools.partial(second_body, extra=True),
            [grid, edge_t, edge_t, edge_yy, edge_zz],
            [info, middle, *middle_edges, mach, S, state, up2, down2],
            [F],
            flops=4000000,
        )
        up_edges = send(*up_edges)
        state, *state_edges = call(
            smooth_body, [grid, edge_x, edge_x, edge_y, edge_z], [info, updated, *up_edges], [F], flops=4000000
        )
        state_edges = send(*state_edges)
        middle, S, *middle_edges = call(
            first_body,
            [grid, own_shape, edge_x, edge_x, edge_y, edge_z],
            [info, state, *state_edges, mach, own2, up_edges[0][12:], up_edges[1][12:]],
            [F],
            flops=4000000,
        )
        middle_edges = send(*middle_edges)
        updated, *up_edges = call(
            functools.partial(second_body, extra=False),
            [grid, edge_x, edge_x, edge_yy, edge_zz],
            [info, middle, *middle_edges, mach, S, state],
            [F],
            flops=4000000,
        )
        up_edges = send(*up_edges)
        (state,) = call(smooth_body, [grid], [info, updated, *up_edges], [F], flops=4000000)
        if MOVED:
            state = lax.ppermute(state, axes, back)
        return state.transpose(1, 2, 0, 3)

    placed = (
        P("gx", "gy", None, "grp"),
        P("gx", "gy"),
        P("gx", "gy", None, None, None),
        P("gx"),
        P("gx", "gy", None, "grp"),
    )
    return jax.shard_map(body, mesh=mesh, in_specs=placed, out_specs=P("gx", "gy", None, "grp"), check_vma=False)
```

```python
import functools

import jax
import jax.numpy as jnp
import numpy as np
from jax import lax
from jax.experimental import pallas as pl
from jax.experimental.pallas import tpu as pltpu
from jax.sharding import PartitionSpec as P

eddy_step = 0.1
viscosity = 0.5
wave_step = 0.2
filter_weight = 0.2
deriv = (0.770882380518, -0.166705904415, 0.02084314277)
taps = (0.28739284246, -0.226146951809, 0.10630357877, -0.023853048191)

RATE_Y, RATE_Z = (0, 2), (0, 3)
ALL = (0, 1, 2, 3)
LANES = 128
VMEM = pl.BlockSpec(memory_space=pltpu.VMEM)
SMEM = pl.BlockSpec(memory_space=pltpu.SMEM)


def call(body, outs, ins, scratch=(), smem=1, flops=1000000):
    shapes = [jax.ShapeDtypeStruct(s, jnp.float32) for s in outs]
    size = sum(o.size for o in shapes) + sum(i.size for i in ins)
    return pl.pallas_call(
        body,
        out_shape=shapes,
        in_specs=[SMEM] * smem + [VMEM] * (len(ins) - smem),
        out_specs=[VMEM] * len(shapes),
        scratch_shapes=list(scratch),
        compiler_params=pltpu.CompilerParams(vmem_limit_bytes=24 * 1024 * 1024),
        cost_estimate=pl.CostEstimate(flops=flops, bytes_accessed=4 * size, transcendentals=0),
    )(*ins)


def banded(depth, weights, sign, half):
    matrix = np.zeros((depth + LANES, depth), np.float32)
    lane = np.arange(depth)
    for j, weight in enumerate(weights, 1):
        for to, factor in ((lane + j, weight), (lane - j, sign * weight)):
            ok = (to >= 0) & (to < depth)
            matrix[to[ok], lane[ok]] = factor
            beyond = to >= depth if half == 0 else to < 0
            matrix[depth + to[beyond] % LANES, lane[beyond]] = factor
    high = matrix.astype(jnp.bfloat16)
    low = (matrix - high.astype(np.float32)).astype(jnp.bfloat16)
    return np.concatenate([high, high, low])


def z_product(f, zmsg, zmat, comps, G):
    _, T, X, Y, _ = f.shape
    for n, c in enumerate(comps):
        tiles = [f[c, t].reshape(X * Y, LANES) for t in range(T)] + [zmsg[n].reshape(X * Y, LANES)]
        high = [tile.astype(jnp.bfloat16) for tile in tiles]
        low = [(tile - top.astype(jnp.float32)).astype(jnp.bfloat16) for tile, top in zip(tiles, high)]
        out = jnp.dot(jnp.concatenate(high + low + high, axis=1), zmat[...], preferred_element_type=jnp.float32)
        for t in range(T):
            G[n, t] = out[:, t * LANES : (t + 1) * LANES].reshape(X, Y, LANES)


def shift_tiles(tiles, left, right, by, lanes):
    out = []
    row = [left] + tiles + [right]
    for at in range(1, len(tiles) + 1):
        if by > 0:
            mixed = jnp.where(lanes < by, row[at + 1], row[at])
            out.append(pltpu.roll(mixed, LANES - by, 1))
        else:
            mixed = jnp.where(lanes >= LANES + by, row[at - 1], row[at])
            out.append(pltpu.roll(mixed, -by, 1))
    return out


def side_tiles(tile, half):
    zero = jnp.zeros_like(tile)
    return jnp.where(half == 1, tile, zero), jnp.where(half == 0, tile, zero)


def known(value, has):
    return jnp.where(has == 1, value, jnp.zeros_like(value))


def lane_ids(rows):
    return lax.broadcasted_iota(jnp.int32, (rows, LANES), 1)


def pack_state(o, inner, outer, ymsg, zmsg, ycomps, zcomps, info):
    pos, row, half = info[0], info[1], info[2]
    _, T, X, Y, _ = o.shape
    si = jnp.where(pos == 0, X - 3, 0)
    so = jnp.where(pos == 0, 0, X - 3)
    for c in range(4):
        for t in range(T):
            for l in range(3):
                inner[3 * (c * T + t) + l] = o[c, t, si + l]
                outer[3 * (c * T + t) + l] = o[c, t, so + l]
    rows = lax.broadcasted_iota(jnp.int32, (8, LANES), 0)
    ys = pl.multiple_of(jnp.where(row == 0, Y - 8, 0), 8)

    def normal(c, t, i):
        tile = o[c, t, i, pl.ds(ys, 8), :]
        return jnp.where(row == 0, pltpu.roll(tile, 4, 0), tile)

    edge = jnp.where(half == 0, T - 1, 0)

    def step(i, carry):
        for n in range(len(ycomps) // 2):
            for t in range(T):
                first, second = normal(ycomps[2 * n], t, i), normal(ycomps[2 * n + 1], t, i)
                ymsg[n, t, i] = jnp.where(rows < 4, first, pltpu.roll(second, 4, 0))
        for n, c in enumerate(zcomps):
            zmsg[n, i] = o[c, edge, i]
        return carry

    lax.fori_loop(0, X, step, 0, unroll=4)


def fill(F, f, inner, outer, ymsg, ycomps, info):
    pos, row, has = info[0], info[1], info[3]
    _, T, X, Y, _ = f.shape
    hi = jnp.where(pos == 0, X + 3, 0)
    ho = jnp.where(pos == 0, 0, X + 3)
    for c in range(4):
        for t in range(T):
            for l in range(3):
                F[c, t, hi + l, 8 : 8 + Y, :] = inner[3 * (c * T + t) + l]
                F[c, t, ho + l, 8 : 8 + Y, :] = known(outer[3 * (c * T + t) + l], has)

    def step(i, carry):
        for t in range(T):
            for c in range(4):
                F[c, t, i + 3, 8 : 8 + Y, :] = f[c, t, i]
            for n, c in enumerate(ycomps):
                tile = ymsg[n // 2, t, i]
                turned = pltpu.roll(tile, 4, 0)
                if n % 2:
                    tile, turned = turned, tile
                zero = jnp.zeros_like(tile)
                F[c, t, i + 3, 0:8, :] = jnp.where(row == 1, turned, zero)
                F[c, t, i + 3, 8 + Y : 16 + Y, :] = jnp.where(row == 0, tile, zero)
        return carry

    lax.fori_loop(0, X, step, 0, unroll=4)


def dx(F, c, t, i, Y):
    y = slice(8, 8 + Y)
    return sum(deriv[j - 1] * (F[c, t, i + 3 + j, y, :] - F[c, t, i + 3 - j, y, :]) for j in (1, 2, 3))


def dy(F, c, t, i, Y):
    return sum(
        deriv[j - 1] * (F[c, t, i + 3, 8 + j : 8 + Y + j, :] - F[c, t, i + 3, 8 - j : 8 + Y - j, :]) for j in (1, 2, 3)
    )


def rate_loop(F, G, mach, S, emit):
    T, X, Y = F.shape[1], F.shape[2] - 6, F.shape[3] - 16

    def step(i, carry):
        m = mach[i]
        for t in range(T):
            gp, gu, gv, gw = (dx(F, c, t, i, Y) for c in range(4))
            emit(0, t, i, -(m * gp + gu + dy(F, 2, t, i, Y) + G[1, t, i]))
            emit(1, t, i, -(m * gu + gp) - S[0, t, i])
            emit(2, t, i, -(m * gv + dy(F, 0, t, i, Y)) - S[1, t, i])
            emit(3, t, i, -(m * gw + G[0, t, i]) - S[2, t, i])
        return carry

    lax.fori_loop(0, X, step, 0, unroll=4)


def first_body(info, f, inner, outer, ymsg, zmsg, zmat, mach, own, t_in, t_out, o, S, n_in, n_out, ny, nz, F, G, *, layers):
    _, T, X, Y, _ = f.shape
    z_product(f, zmsg, zmat, RATE_Z, G)
    fill(F, f, inner, outer, ymsg, RATE_Y, info)
    at_in = jnp.where(info[0] == 0, X - layers, 0)
    at_out = jnp.where(info[0] == 0, 0, X - layers)
    S[...] = own[...]
    for c in range(3):
        for t in range(T):
            for l in range(layers):
                n = (c * T + t) * layers + l
                S[c, t, at_in + l] = S[c, t, at_in + l] + t_in[n]
                S[c, t, at_out + l] = S[c, t, at_out + l] + known(t_out[n], info[3])

    def emit(c, t, i, value):
        o[c, t, i] = f[c, t, i] + wave_step * value

    rate_loop(F, G, mach, S, emit)
    pack_state(o, n_in, n_out, ny, nz, RATE_Y, RATE_Z, info)


def second_body(info, f, inner, outer, ymsg, zmsg, zmat, mach, S, state, o, n_in, n_out, ny, nz, F, G):
    z_product(f, zmsg, zmat, RATE_Z, G)
    fill(F, f, inner, outer, ymsg, RATE_Y, info)

    def emit(c, t, i, value):
        o[c, t, i] = 0.5 * (state[c, t, i] + f[c, t, i]) + (0.5 * wave_step) * value

    rate_loop(F, G, mach, S, emit)
    pack_state(o, n_in, n_out, ny, nz, ALL, ALL, info)


def smooth_body(info, f, inner, outer, ymsg, zmsg, zmat, o, *rest):
    F, G = rest[-2:]
    _, T, X, Y, _ = f.shape
    z_product(f, zmsg, zmat, ALL, G)
    fill(F, f, inner, outer, ymsg, ALL, info)
    y = slice(8, 8 + Y)

    def step(i, carry):
        for c in range(4):
            for t in range(T):
                total = (1.0 - 3.0 * filter_weight * taps[0]) * F[c, t, i + 3, y, :] + G[c, t, i]
                for j in (1, 2, 3):
                    beside = (F[c, t, i + 3 + j, y, :] + F[c, t, i + 3 - j, y, :]) + (
                        F[c, t, i + 3, 8 + j : 8 + Y + j, :] + F[c, t, i + 3, 8 - j : 8 + Y - j, :]
                    )
                    total = total - (filter_weight * taps[j]) * beside
                if len(rest) > 2:
                    o[c, t, i] = total
                else:
                    o[c, i, :, t * LANES : (t + 1) * LANES] = total
        return carry

    lax.fori_loop(0, X, step, 0, unroll=4)
    if len(rest) > 2:
        pack_state(o, *rest[:4], RATE_Y, RATE_Z, info)


def pack_body(info, f, o, inner, outer, ymsg, zmsg):
    _, T, X, _, _ = o.shape

    def step(i, carry):
        for c in range(4):
            for t in range(T):
                o[c, t, i] = f[c, i, :, t * LANES : (t + 1) * LANES]
        return carry

    lax.fori_loop(0, X, step, 0, unroll=4)
    pack_state(o, inner, outer, ymsg, zmsg, RATE_Y, RATE_Z, info)


def pack_les(get, shape, inner, outer, ymsg, zmsg, base, info):
    pos, row, half = info[0], info[1], info[2]
    _, T, X, Y, _ = shape
    si = jnp.where(pos == 0, X - 1, 0)
    so = jnp.where(pos == 0, 0, X - 1)
    rows = lax.broadcasted_iota(jnp.int32, (8, LANES), 0)
    ys = pl.multiple_of(jnp.where(row == 0, Y - 8, 0), 8)
    for c in range(3):
        for t in range(T):
            inner[base + c * T + t] = get(c, t, si, slice(None))
            outer[base + c * T + t] = get(c, t, so, slice(None))
            for n in range(X // 8):
                acc = jnp.zeros((8, LANES), jnp.float32)
                for r in range(8):
                    tile = get(c, t, 8 * n + r, pl.ds(ys, 8))
                    moved = jnp.where(row == 0, pltpu.roll(tile, (r + 1) % 8, 0), pltpu.roll(tile, r, 0))
                    acc = jnp.where(rows == r, moved, acc)
                ymsg[c, t, n] = acc

    def step(i, carry):
        for c in range(3):
            last, first = get(c, T - 1, i, slice(None)), get(c, 0, i, slice(None))
            zmsg[c, i] = jnp.where(half == 0, last, first)
        return carry

    lax.fori_loop(0, X, step, 0, unroll=4)


def getter(v):
    if len(v.shape) == 4:
        return lambda c, t, i, rows: v[i, c, rows, t * LANES : (t + 1) * LANES]
    return lambda c, t, i, rows: v[c, t, i, rows, :]


def pack_les_body(info, v, inner, outer, ymsg, zmsg):
    X, _, Y, Z = v.shape
    pack_les(getter(v), (3, Z // LANES, X, Y, LANES), inner, outer, ymsg, zmsg, 0, info)


def les_body(info, offset, v, inner, outer, ymsg, zmsg, tiles, *rest, base, advance):
    if advance:
        v1, own, n_in, n_out, ny, nz, V, LB, ACC = rest
    else:
        own, n_in, n_out, V, LB, ACC = rest
    pos, row, half = info[0], info[1], info[2]
    _, T, X, Y, _ = V.shape
    X, Y = X - 2, Y - 16
    get = getter(v)
    blocks = 2 * LB.shape[0]
    wide = X // blocks
    plane = wide * Y
    hi = jnp.where(pos == 0, X + 1, 0)
    ho = jnp.where(pos == 0, 0, X + 1)
    for c in range(3):
        for t in range(T):
            V[c, t, hi, 8 : 8 + Y, :] = inner[base + c * T + t]
            V[c, t, ho, 8 : 8 + Y, :] = known(outer[base + c * T + t], info[3])
            for n in range(X // 8):
                tile = ymsg[c, t, n]
                zero = jnp.zeros_like(tile)
                for r in range(8):
                    low = pltpu.roll(tile, 7 - r, 0) if r < 7 else tile
                    high = pltpu.roll(tile, 8 - r, 0) if r else tile
                    V[c, t, 8 * n + r + 1, 0:8, :] = jnp.where(row == 1, low, zero)
                    V[c, t, 8 * n + r + 1, 8 + Y : 16 + Y, :] = jnp.where(row == 0, high, zero)

    def copy(i, carry):
        for c in range(3):
            for t in range(T):
                V[c, t, i + 1, 8 : 8 + Y, :] = get(c, t, i, slice(None))
        return carry

    lax.fori_loop(0, X, copy, 0, unroll=4)
    ACC[...] = jnp.zeros_like(ACC)
    lanes = lane_ids(Y)
    y = slice(8, 8 + Y)

    def step(i, carry):
        center = [[V[c, t, i + 1, y, :] for t in range(T)] for c in range(3)]
        ahead, behind = [], []
        for c in range(3 if advance else 2):
            left, right = side_tiles(zmsg[c, i], half)
            ahead.append(shift_tiles(center[c], left, right, 1, lanes))
            behind.append(shift_tiles(center[c], left, right, -1, lanes))
        at = lax.rem(i, 2 * wide) * Y
        at = at + jnp.where(at >= plane, plane, 0)
        b = i // (2 * wide)
        for t in range(T):
            xa = [V[c, t, i + 2, y, :] for c in range(3)]
            xb = [V[c, t, i, y, :] for c in range(3)]
            ya = [V[c, t, i + 1, 9 : 9 + Y, :] for c in range(3)]
            yb = [V[c, t, i + 1, 7 : 7 + Y, :] for c in range(3)]
            u, w, q = center[0][t], center[1][t], center[2][t]
            vx = 0.5 * ((ya[2] - yb[2]) - (ahead[1][t] - behind[1][t]))
            vy = 0.5 * ((ahead[0][t] - behind[0][t]) - (xa[2] - xb[2]))
            vz = 0.5 * ((xa[1] - xb[1]) - (ya[0] - yb[0]))
            lamb = [vy * q - vz * w, vz * u - vx * q, vx * w - vy * u]
            for c in range(3):
                high = lamb[c].astype(jnp.bfloat16)
                low = (lamb[c] - high.astype(jnp.float32)).astype(jnp.bfloat16)
                lane = slice((c * T + t) * LANES, (c * T + t + 1) * LANES)
                LB[b, pl.ds(pl.multiple_of(at, 16), Y), lane] = high
                LB[b, pl.ds(pl.multiple_of(plane + at, 16), Y), lane] = low
                if advance:
                    laplace = -6.0 * center[c][t] + ((xa[c] + xb[c]) + (ya[c] + yb[c]) + (ahead[c][t] + behind[c][t]))
                    v1[c, t, i] = center[c][t] + eddy_step * (viscosity * laplace - lamb[c])
        return carry

    lax.fori_loop(0, X, step, 0, unroll=4)

    for m in range(blocks // 2):
        out = jnp.dot(tiles[m].astype(jnp.bfloat16), LB[m], preferred_element_type=jnp.float32)
        at = (m + 1) * wide
        places = [(at, 0), (at + offset[2 * m] * wide, plane), (at + offset[2 * m + 1] * wide, 2 * plane)]
        for c in range(3):
            for t in range(T):
                lane = slice((c * T + t) * LANES, (c * T + t + 1) * LANES)
                for to, row0 in places:
                    for l in range(wide):
                        ACC[c, t, to + l] = ACC[c, t, to + l] + out[row0 + l * Y : row0 + (l + 1) * Y, lane]

    depth = own.shape[2]
    own[...] = ACC[:, :, wide : wide + depth]
    ti = jnp.where(pos == 0, depth + wide, 0)
    to = jnp.where(pos == 0, 0, depth + wide)
    for c in range(3):
        for t in range(T):
            for l in range(wide):
                n_in[(c * T + t) * wide + l] = ACC[c, t, ti + l]
                n_out[(c * T + t) * wide + l] = ACC[c, t, to + l]
    if advance:
        pack_les(getter(v1), v1.shape, n_in, n_out, ny, nz, 3 * T * wide, info)


def solution(mesh):
    gx = mesh.shape["gx"]
    swap = [(0, 1), (1, 0)]
    even = [pair for k in range(gx // 2) for pair in ((2 * k, 2 * k + 1), (2 * k + 1, 2 * k))]
    odd = [pair for k in range(gx // 2 - 1) for pair in ((2 * k + 1, 2 * k + 2), (2 * k + 2, 2 * k + 1))]

    def flat(**at):
        index = 0
        for axis in mesh.axis_names:
            index = index * mesh.shape[axis] + at[axis]
        return index

    ends = [(0, 1), (1, 0)]
    hops = [
        (flat(gx=a, gy=y, grp=c), flat(gx=b, gy=y, grp=c)) for a, b in odd for y in range(mesh.shape["gy"]) for c in (0, 1)
    ] + [
        (flat(gx=g, gy=y, grp=a), flat(gx=g, gy=y, grp=b))
        for g in (0, gx - 1)
        for y in range(mesh.shape["gy"])
        for a, b in ends
    ]

    def send_x(inner, outer):
        return lax.ppermute(inner, "gx", even), lax.ppermute(outer, mesh.axis_names, hops)

    def send(inner, outer, ymsg, zmsg):
        return *send_x(inner, outer), lax.ppermute(ymsg, "gy", swap), lax.ppermute(zmsg, "grp", swap)

    def body(les_velocity, mean_mach, transfer_tiles, intersection_offset, acoustic_state):
        X2, Y, _, Z = les_velocity.shape
        X = acoustic_state.shape[0]
        T = Z // LANES
        blocks, plane = transfer_tiles.shape[0], transfer_tiles.shape[-1]
        wide = plane // Y
        column = lax.axis_index("gx")
        half = lax.axis_index("grp")
        has = (column > 0) & (column < gx - 1)
        info = jnp.stack([column % 2, lax.axis_index("gy"), half, has.astype(jnp.int32)]).astype(jnp.int32)
        v = les_velocity.transpose(0, 2, 1, 3)
        state = acoustic_state.transpose(2, 0, 1, 3)
        rate_z = jnp.where(half == 0, *(banded(Z, deriv, -1, h) for h in (0, 1)))
        smooth_z = jnp.where(half == 0, *(banded(Z, [-filter_weight * w for w in taps[1:]], 1, h) for h in (0, 1)))
        pair = transfer_tiles[:, 0].swapaxes(2, 3).reshape(blocks // 2, 2, 2, plane, plane)
        none = jnp.zeros((blocks // 2, plane, 2 * plane), pair.dtype)
        twice = [[jnp.concatenate([pair[:, n, k]] * 2, axis=2) for k in (0, 1)] for n in (0, 1)]
        tiles = jnp.concatenate(
            [
                jnp.concatenate([twice[0][0], twice[1][0]], axis=2),
                jnp.concatenate([twice[0][1], none], axis=2),
                jnp.concatenate([none, twice[1][1]], axis=2),
            ],
            axis=1,
        )
        mach = jnp.broadcast_to(mean_mach[:, :, None], (X, Y, LANES))

        grid = (4, T, X, Y, LANES)
        source = (3, T, X, Y, LANES)
        edge_x, term = (12 * T, Y, LANES), (3 * T * wide, Y, LANES)
        edge_y, edge_yy = (1, T, X, 8, LANES), (2, T, X, 8, LANES)
        edge_z, edge_zz = (2, X, Y, LANES), (4, X, Y, LANES)
        les_y, les_z = (3, T, X2 // 8, 8, LANES), (3, X2, Y, LANES)
        F = pltpu.VMEM((4, T, X + 6, Y + 16, LANES), jnp.float32)
        G2 = pltpu.VMEM((2, T, X, Y, LANES), jnp.float32)
        G4 = pltpu.VMEM((4, T, X, Y, LANES), jnp.float32)
        les_scratch = [
            pltpu.VMEM((3, T, X2 + 2, Y + 16, LANES), jnp.float32),
            pltpu.VMEM((blocks // 2, 4 * plane, 3 * Z), jnp.bfloat16),
            pltpu.VMEM((3, T, X + 2 * wide, Y, LANES), jnp.float32),
        ]
        les_edges = send(*call(pack_les_body, [(3 * T, Y, LANES), (3 * T, Y, LANES), les_y, les_z], [info, v]))
        state, *state_edges = call(pack_body, [grid, edge_x, edge_x, edge_y, edge_z], [info, state])
        info, *state_edges = lax.optimization_barrier((info, *state_edges))
        state_edges = send(*state_edges)
        with_terms = (term[0] + 3 * T, Y, LANES)
        v1, own, *edges = call(
            functools.partial(les_body, base=0, advance=True),
            [(3, T, X2, Y, LANES), source, with_terms, with_terms, les_y, les_z],
            [info, intersection_offset, v, *les_edges, tiles],
            les_scratch,
            smem=2,
            flops=4000000,
        )
        edges = send(*edges)
        first = functools.partial(first_body, layers=wide)
        outs = [grid, source, edge_x, edge_x, edge_y, edge_z]
        middle, S, *middle_edges = call(
            first, outs, [info, state, *state_edges, rate_z, mach, own, edges[0], edges[1]], [F, G2], flops=4000000
        )
        middle_edges = send(*middle_edges)
        own2, *terms = call(
            functools.partial(les_body, base=term[0], advance=False),
            [source, term, term],
            [info, intersection_offset, v1, *edges, tiles],
            les_scratch,
            smem=2,
            flops=4000000,
        )
        outs = [grid, edge_x, edge_x, edge_yy, edge_zz]
        updated, *up_edges = call(
            second_body, outs, [info, middle, *middle_edges, rate_z, mach, S, state], [F, G2], flops=4000000
        )
        up_edges = send(*up_edges)
        terms = send_x(*terms)
        outs = [grid, edge_x, edge_x, edge_y, edge_z]
        state, *state_edges = call(
            smooth_body, outs, [info, updated, *up_edges, smooth_z], [F, G4], flops=4000000
        )
        state_edges = send(*state_edges)
        outs = [grid, source, edge_x, edge_x, edge_y, edge_z]
        middle, S, *middle_edges = call(
            first, outs, [info, state, *state_edges, rate_z, mach, own2, *terms], [F, G2], flops=4000000
        )
        middle_edges = send(*middle_edges)
        outs = [grid, edge_x, edge_x, edge_yy, edge_zz]
        updated, *up_edges = call(
            second_body, outs, [info, middle, *middle_edges, rate_z, mach, S, state], [F, G2], flops=4000000
        )
        up_edges = send(*up_edges)
        (state,) = call(smooth_body, [(4, X, Y, Z)], [info, updated, *up_edges, smooth_z], [F, G4], flops=4000000)
        return state.transpose(1, 2, 0, 3)

    placed = (
        P("gx", "gy", None, "grp"),
        P("gx", "gy"),
        P("gx", "gy", None, None, None),
        P("gx"),
        P("gx", "gy", None, "grp"),
    )
    return jax.shard_map(body, mesh=mesh, in_specs=placed, out_specs=P("gx", "gy", None, "grp"), check_vma=False)
```

```python
import functools

import jax
import jax.numpy as jnp
import numpy as np
from jax import lax
from jax.experimental import pallas as pl
from jax.experimental.pallas import tpu as pltpu
from jax.sharding import PartitionSpec as P

STEPS = 2
eddy_step = 0.1
viscosity = 0.5
wave_step = 0.2
filter_weight = 0.2
deriv = (0.770882380518, -0.166705904415, 0.02084314277)
taps = (0.28739284246, -0.226146951809, 0.10630357877, -0.023853048191)

RATE_Y, RATE_Z = (0, 2), (0, 3)
ALL = (0, 1, 2, 3)
LANES = 128
VMEM = pl.BlockSpec(memory_space=pltpu.VMEM)
SMEM = pl.BlockSpec(memory_space=pltpu.SMEM)


def call(body, outs, ins, scratch=(), smem=1, flops=1000000):
    shapes = [jax.ShapeDtypeStruct(s, jnp.float32) for s in outs]
    size = sum(o.size for o in shapes) + sum(i.size for i in ins)
    return pl.pallas_call(
        body,
        out_shape=shapes,
        in_specs=[SMEM] * smem + [VMEM] * (len(ins) - smem),
        out_specs=[VMEM] * len(shapes),
        scratch_shapes=list(scratch),
        compiler_params=pltpu.CompilerParams(vmem_limit_bytes=12 * 1024 * 1024),
        cost_estimate=pl.CostEstimate(flops=flops, bytes_accessed=4 * size, transcendentals=0),
    )(*ins)


def banded(depth, weights, sign, half):
    matrix = np.zeros((depth + LANES, depth), np.float32)
    lane = np.arange(depth)
    for j, weight in enumerate(weights, 1):
        for to, factor in ((lane + j, weight), (lane - j, sign * weight)):
            ok = (to >= 0) & (to < depth)
            matrix[to[ok], lane[ok]] = factor
            beyond = to >= depth if half == 0 else to < 0
            matrix[depth + to[beyond] % LANES, lane[beyond]] = factor
    high = matrix.astype(jnp.bfloat16)
    low = (matrix - high.astype(np.float32)).astype(jnp.bfloat16)
    return np.concatenate([high, high, low])


def z_product(F, zmsg, zmat, comps, G):
    _, T, X, Y, _ = F.shape
    X, Y = X - 6, Y - 16
    for n, c in enumerate(comps):
        tiles = [F[c, t, 3 : 3 + X, 8 : 8 + Y, :].reshape(X * Y, LANES) for t in range(T)]
        tiles.append(zmsg[n].reshape(X * Y, LANES))
        high = [tile.astype(jnp.bfloat16) for tile in tiles]
        low = [(tile - top.astype(jnp.float32)).astype(jnp.bfloat16) for tile, top in zip(tiles, high)]
        out = jnp.dot(jnp.concatenate(high + low + high, axis=1), zmat[...], preferred_element_type=jnp.float32)
        for t in range(T):
            G[n, t] = out[:, t * LANES : (t + 1) * LANES].reshape(X, Y, LANES)


def shift_tiles(tiles, left, right, by, lanes):
    out = []
    row = [left] + tiles + [right]
    for at in range(1, len(tiles) + 1):
        if by > 0:
            mixed = jnp.where(lanes < by, row[at + 1], row[at])
            out.append(pltpu.roll(mixed, LANES - by, 1))
        else:
            mixed = jnp.where(lanes >= LANES + by, row[at - 1], row[at])
            out.append(pltpu.roll(mixed, -by, 1))
    return out


def side_tiles(tile, half):
    zero = jnp.zeros_like(tile)
    return jnp.where(half == 1, tile, zero), jnp.where(half == 0, tile, zero)


def known(value, has):
    return jnp.where(has == 1, value, jnp.zeros_like(value))


def lane_ids(rows):
    return lax.broadcasted_iota(jnp.int32, (rows, LANES), 1)


def ends(info, inner, X, deep):
    high = (info[0] == 0) if inner else (info[0] == 1)
    has = jnp.int32(1) if inner else info[3]
    return high, has, lambda d: jnp.where(high, X - 1 - d, d), lambda d: jnp.where(high, 2 - d, d)


def pack_sides(info, get, ymsg, zmsg, ycomps, zcomps, X, Y, T, layers):
    row, half = info[1], info[2]
    rows = lax.broadcasted_iota(jnp.int32, (8, LANES), 0)
    ys = pl.multiple_of(jnp.where(row == 0, Y - 8, 0), 8)
    turn = jnp.where(row == 0, 4, 0)
    edge = jnp.where(half == 0, T - 1, 0)

    def one(i):
        for n in range(len(ycomps) // 2):
            for t in range(T):
                first = pltpu.roll(get(ycomps[2 * n], t, i, pl.ds(ys, 8)), turn, 0)
                second = pltpu.roll(get(ycomps[2 * n + 1], t, i, pl.ds(ys, 8)), 4 - turn, 0)
                ymsg[n, t, i] = jnp.where(rows < 4, first, second)
        for n, c in enumerate(zcomps):
            zmsg[n, i] = get(c, edge, i, slice(None))

    if layers is None:
        lax.fori_loop(0, X, lambda i, carry: (one(i), carry)[1], 0, unroll=4)
    else:
        for i in layers:
            one(i)


def fill(F, f, nears, fars, ymsg, ycomps, info, halos=None):
    row = info[1]
    _, T, X, Y, _ = f.shape
    y = slice(8, 8 + Y)

    def step(i, carry):
        for t in range(T):
            for c in range(4):
                F[c, t, i + 3, y, :] = f[c, t, i]
            for n, c in enumerate(ycomps):
                tile = ymsg[n // 2, t, i]
                turned = pltpu.roll(tile, 4, 0)
                if n % 2:
                    tile, turned = turned, tile
                zero = jnp.zeros_like(tile)
                F[c, t, i + 3, 0:8, :] = jnp.where(row == 1, turned, zero)
                F[c, t, i + 3, 8 + Y : 16 + Y, :] = jnp.where(row == 0, tile, zero)
        return carry

    lax.fori_loop(0, X, step, 0, unroll=4)
    zero = jnp.zeros((Y, LANES), jnp.float32)
    for side, near in enumerate(nears):
        high, has, layer, place = ends(info, side == 0, X, 3)
        for c in range(4):
            for t in range(T):
                for d in range(3):
                    F[c, t, 3 + layer(d), y, :] = near[3 * (c * T + t) + place(d)]
                    beyond = zero
                    if halos is not None:
                        beyond = known(halos[side][3 * (c * T + t) + place(2 - d)], has)
                    F[c, t, jnp.where(high, X + 3 + d, 2 - d), y, :] = beyond
                if fars:
                    far = fars[side]
                    count = far.shape[0] // (4 * T)
                    for d in range(count):
                        F[c, t, 3 + layer(3 + d), y, :] = far[count * (c * T + t) + d]


def dx(F, c, t, i, Y):
    y = slice(8, 8 + Y)
    return sum(deriv[j - 1] * (F[c, t, i + 3 + j, y, :] - F[c, t, i + 3 - j, y, :]) for j in (1, 2, 3))


def dy(F, c, t, i, Y):
    return sum(
        deriv[j - 1] * (F[c, t, i + 3, 8 + j : 8 + Y + j, :] - F[c, t, i + 3, 8 - j : 8 + Y - j, :]) for j in (1, 2, 3)
    )


def rate_loop(F, G, mach, S, emit):
    T, X, Y = F.shape[1], F.shape[2] - 6, F.shape[3] - 16

    def step(i, carry):
        m = mach[i]
        for t in range(T):
            gp, gu, gv, gw = (dx(F, c, t, i, Y) for c in range(4))
            emit(0, t, i, -(m * gp + gu + dy(F, 2, t, i, Y) + G[1, t, i]))
            emit(1, t, i, -(m * gu + gp) - S[0, t, i])
            emit(2, t, i, -(m * gv + dy(F, 0, t, i, Y)) - S[1, t, i])
            emit(3, t, i, -(m * gw + G[0, t, i]) - S[2, t, i])
        return carry

    lax.fori_loop(0, X, step, 0, unroll=4)


def first_main(info, f, near_in, near_out, ymsg, zmsg, zmat, mach, S, o, base, F, G):
    Y = f.shape[3]
    fill(F, f, (near_in, near_out), (), ymsg, RATE_Y, info)
    z_product(F, zmsg, zmat, RATE_Z, G)

    def emit(c, t, i, value):
        center = F[c, t, i + 3, 8 : 8 + Y, :]
        base[c, t, i] = center
        o[c, t, i] = center + wave_step * value

    rate_loop(F, G, mach, S, emit)


def second_main(info, f, near_in, near_out, far_in, far_out, ymsg, zmsg, zmat, mach, S, base, o, F, G):
    Y = f.shape[3]
    fill(F, f, (near_in, near_out), (far_in, far_out), ymsg, RATE_Y, info)
    z_product(F, zmsg, zmat, RATE_Z, G)

    def emit(c, t, i, value):
        o[c, t, i] = 0.5 * (base[c, t, i] + F[c, t, i + 3, 8 : 8 + Y, :]) + (0.5 * wave_step) * value

    rate_loop(F, G, mach, S, emit)


def smooth_main(info, f, near_in, near_out, far_in, far_out, ymsg, zmsg, zmat, *rest, last):
    *halos, o, F, G = rest
    _, T, X, Y, _ = f.shape
    fill(F, f, (near_in, near_out), (far_in, far_out), ymsg, ALL, info, halos if last else None)
    z_product(F, zmsg, zmat, ALL, G)
    y = slice(8, 8 + Y)

    def step(i, carry):
        for c in range(4):
            for t in range(T):
                total = (1.0 - 3.0 * filter_weight * taps[0]) * F[c, t, i + 3, y, :] + G[c, t, i]
                for j in (1, 2, 3):
                    beside = (F[c, t, i + 3 + j, y, :] + F[c, t, i + 3 - j, y, :]) + (
                        F[c, t, i + 3, 8 + j : 8 + Y + j, :] + F[c, t, i + 3, 8 - j : 8 + Y - j, :]
                    )
                    total = total - (filter_weight * taps[j]) * beside
                if last:
                    o[c, i, :, t * LANES : (t + 1) * LANES] = total
                else:
                    o[c, t, i] = total
        return carry

    lax.fori_loop(0, X, step, 0, unroll=4)


def edge_body(info, f, halo_in, halo_out, *rest, smooth, scale, ycomps, zcomps):
    rest = list(rest)
    mach, *terms = (None, None, None) if smooth else [rest.pop(0) for _ in range(3)]
    *done, ymsg, zmsg = rest
    sides = [done[:1], done[1:]] if smooth else [done[:2], done[2:]]
    _, T, X, Y, _ = f.shape
    deep = 3 if smooth else 3 + sides[0][1].shape[0] // (4 * T)
    for side, halo in enumerate((halo_in, halo_out)):
        near = sides[side][0]
        high, has, layer, place = ends(info, side == 0, X, deep)
        sign = (jnp.where(high, scale, -scale) * has).astype(jnp.float32)
        weight = has.astype(jnp.float32)
        for t in range(T):
            for d in range(deep):
                at = layer(d)
                values = [f[c, t, at] for c in range(4)]
                if d < 3:
                    beyond = [[halo[3 * (c * T + t) + place(2 - e)] for e in range(3 - d)] for c in range(4)]
                    coefs = taps[1:] if smooth else deriv
                    parts = [sum(coefs[d + e] * value for e, value in enumerate(column)) for column in beyond]
                    if smooth:
                        values = [value - (filter_weight * weight) * part for value, part in zip(values, parts)]
                    else:
                        m, (gp, gu, gv, gw) = mach[at], parts
                        change = (m * gp + gu, m * gu + gp, m * gv, m * gw)
                        values = [value - sign * part for value, part in zip(values, change)]
                if not smooth:
                    index = jnp.where(high, deep - 1 - d, d)
                    for c in range(3):
                        term = terms[side][(c * T + t) * deep + index]
                        values[1 + c] = values[1 + c] - (scale * weight) * term
                for c in range(4):
                    if d < 3:
                        near[3 * (c * T + t) + place(d)] = values[c]
                    else:
                        sides[side][1][(deep - 3) * (c * T + t) + d - 3] = values[c]
    pack_sides(info, lambda c, t, i, rows: f[c, t, i, rows, :], ymsg, zmsg, ycomps, zcomps, X, Y, T, None)
    for side, (near, *far) in enumerate(sides):
        _, _, layer, place = ends(info, side == 0, X, deep)
        for d in range(deep):

            def get(c, t, i, rows):
                if d < 3:
                    return near[3 * (c * T + t) + place(d), rows, :]
                return far[0][(deep - 3) * (c * T + t) + d - 3, rows, :]

            pack_sides(info, get, ymsg, zmsg, ycomps, zcomps, X, Y, T, [layer(d)])


def pack_whole(info, f, o, near_in, near_out, start, ymsg, zmsg):
    _, T, X, Y, _ = o.shape

    def step(i, carry):
        for c in range(4):
            for t in range(T):
                o[c, t, i] = f[c, i, :, t * LANES : (t + 1) * LANES]
        return carry

    lax.fori_loop(0, X, step, 0, unroll=4)
    for side, near in enumerate((near_in, near_out)):
        _, _, layer, place = ends(info, side == 0, X, 3)
        for c in range(4):
            for t in range(T):
                for d in range(3):
                    near[start + 3 * (c * T + t) + place(d)] = o[c, t, layer(d)]
    pack_sides(info, lambda c, t, i, rows: o[c, t, i, rows, :], ymsg, zmsg, RATE_Y, RATE_Z, X, Y, T, None)


def pack_les(get, shape, inner, outer, ymsg, zmsg, info, base=0):
    pos, row, half = info[0], info[1], info[2]
    _, T, X, Y, _ = shape
    si = jnp.where(pos == 0, X - 1, 0)
    so = jnp.where(pos == 0, 0, X - 1)
    rows = lax.broadcasted_iota(jnp.int32, (8, LANES), 0)
    ys = pl.multiple_of(jnp.where(row == 0, Y - 8, 0), 8)
    turn = [jnp.where(row == 0, (r + 1) % 8, r) for r in range(8)]
    for c in range(3):
        for t in range(T):
            inner[base + c * T + t] = get(c, t, si, slice(None))
            outer[base + c * T + t] = get(c, t, so, slice(None))
            for n in range(X // 8):
                acc = jnp.zeros((8, LANES), jnp.float32)
                for r in range(8):
                    tile = get(c, t, 8 * n + r, pl.ds(ys, 8))
                    acc = jnp.where(rows == r, pltpu.roll(tile, turn[r], 0), acc)
                ymsg[c, t, n] = acc

    def step(i, carry):
        for c in range(3):
            last, first = get(c, T - 1, i, slice(None)), get(c, 0, i, slice(None))
            zmsg[c, i] = jnp.where(half == 0, last, first)
        return carry

    lax.fori_loop(0, X, step, 0, unroll=4)


def getter(v):
    if len(v.shape) == 4:
        return lambda c, t, i, rows: v[i, c, rows, t * LANES : (t + 1) * LANES]
    return lambda c, t, i, rows: v[c, t, i, rows, :]


def pack_les_body(info, v, inner, outer, ymsg, zmsg):
    X, _, Y, Z = v.shape
    pack_les(getter(v), (3, Z // LANES, X, Y, LANES), inner, outer, ymsg, zmsg, info)


def les_body(info, offset, v, inner, outer, ymsg, zmsg, tiles, *rest, base, advance):
    if advance:
        state, v1, own, n_in, n_out, ny, nz, f, fy, fz, V, LB, ACC = rest
    else:
        own, n_in, n_out, V, LB, ACC = rest
    pos, row, half = info[0], info[1], info[2]
    _, T, X, Y, _ = V.shape
    X, Y = X - 2, Y - 16
    get = getter(v)
    blocks = 2 * LB.shape[0]
    wide = X // blocks
    plane = wide * Y
    hi = jnp.where(pos == 0, X + 1, 0)
    ho = jnp.where(pos == 0, 0, X + 1)
    for c in range(3):
        for t in range(T):
            V[c, t, hi, 8 : 8 + Y, :] = inner[base + c * T + t]
            V[c, t, ho, 8 : 8 + Y, :] = known(outer[base + c * T + t], info[3])
            for n in range(X // 8):
                tile = ymsg[c, t, n]
                zero = jnp.zeros_like(tile)
                for r in range(8):
                    low = pltpu.roll(tile, 7 - r, 0) if r < 7 else tile
                    high = pltpu.roll(tile, 8 - r, 0) if r else tile
                    V[c, t, 8 * n + r + 1, 0:8, :] = jnp.where(row == 1, low, zero)
                    V[c, t, 8 * n + r + 1, 8 + Y : 16 + Y, :] = jnp.where(row == 0, high, zero)

    def copy(i, carry):
        for c in range(3):
            for t in range(T):
                V[c, t, i + 1, 8 : 8 + Y, :] = get(c, t, i, slice(None))
        return carry

    lax.fori_loop(0, X, copy, 0, unroll=4)
    ACC[...] = jnp.zeros_like(ACC)
    lanes = lane_ids(Y)
    y = slice(8, 8 + Y)

    def step(i, carry):
        center = [[V[c, t, i + 1, y, :] for t in range(T)] for c in range(3)]
        ahead, behind = [], []
        for c in range(3 if advance else 2):
            left, right = side_tiles(zmsg[c, i], half)
            ahead.append(shift_tiles(center[c], left, right, 1, lanes))
            behind.append(shift_tiles(center[c], left, right, -1, lanes))
        at = lax.rem(i, 2 * wide) * Y
        at = at + jnp.where(at >= plane, plane, 0)
        b = i // (2 * wide)
        for t in range(T):
            xa = [V[c, t, i + 2, y, :] for c in range(3)]
            xb = [V[c, t, i, y, :] for c in range(3)]
            ya = [V[c, t, i + 1, 9 : 9 + Y, :] for c in range(3)]
            yb = [V[c, t, i + 1, 7 : 7 + Y, :] for c in range(3)]
            u, w, q = center[0][t], center[1][t], center[2][t]
            vx = 0.5 * ((ya[2] - yb[2]) - (ahead[1][t] - behind[1][t]))
            vy = 0.5 * ((ahead[0][t] - behind[0][t]) - (xa[2] - xb[2]))
            vz = 0.5 * ((xa[1] - xb[1]) - (ya[0] - yb[0]))
            lamb = [vy * q - vz * w, vz * u - vx * q, vx * w - vy * u]
            for c in range(3):
                high = lamb[c].astype(jnp.bfloat16)
                low = (lamb[c] - high.astype(jnp.float32)).astype(jnp.bfloat16)
                lane = slice((c * T + t) * LANES, (c * T + t + 1) * LANES)
                LB[b, pl.ds(pl.multiple_of(at, 16), Y), lane] = high
                LB[b, pl.ds(pl.multiple_of(plane + at, 16), Y), lane] = low
                if advance:
                    laplace = -6.0 * center[c][t] + ((xa[c] + xb[c]) + (ya[c] + yb[c]) + (ahead[c][t] + behind[c][t]))
                    v1[c, t, i] = center[c][t] + eddy_step * (viscosity * laplace - lamb[c])
        return carry

    lax.fori_loop(0, X, step, 0, unroll=4)

    for m in range(blocks // 2):
        a, b = tiles[2 * m], tiles[2 * m + 1]
        none = jnp.zeros((plane, 2 * plane), jnp.bfloat16)
        rows = [(a[:plane], b[:plane]), (a[plane:], none), (none, b[plane:])]
        weights = jnp.concatenate([jnp.concatenate(pair, axis=1) for pair in rows], axis=0)
        out = jnp.dot(weights, LB[m], preferred_element_type=jnp.float32)
        at = (m + 1) * wide
        places = [(at, 0), (at + offset[2 * m] * wide, plane), (at + offset[2 * m + 1] * wide, 2 * plane)]
        for c in range(3):
            for t in range(T):
                lane = slice((c * T + t) * LANES, (c * T + t + 1) * LANES)
                for to, row0 in places:
                    for l in range(wide):
                        ACC[c, t, to + l] = ACC[c, t, to + l] + out[row0 + l * Y : row0 + (l + 1) * Y, lane]

    depth = own.shape[2]
    own[...] = ACC[:, :, wide : wide + depth]
    ti = jnp.where(pos == 0, depth + wide, 0)
    to = jnp.where(pos == 0, 0, depth + wide)
    for c in range(3):
        for t in range(T):
            for l in range(wide):
                n_in[(c * T + t) * wide + l] = ACC[c, t, ti + l]
                n_out[(c * T + t) * wide + l] = ACC[c, t, to + l]
    if advance:
        pack_les(getter(v1), v1.shape, n_in, n_out, ny, nz, info, 3 * T * wide)
        pack_whole(info, state, f, n_in, n_out, 3 * T * (wide + 1), fy, fz)


def solution(mesh):
    gx = mesh.shape["gx"]
    swap = [(0, 1), (1, 0)]
    even = [pair for k in range(gx // 2) for pair in ((2 * k, 2 * k + 1), (2 * k + 1, 2 * k))]
    odd = [pair for k in range(gx // 2 - 1) for pair in ((2 * k + 1, 2 * k + 2), (2 * k + 2, 2 * k + 1))]

    def flat(**at):
        index = 0
        for axis in mesh.axis_names:
            index = index * mesh.shape[axis] + at[axis]
        return index

    ends = [(0, 1), (1, 0)]
    hops = [
        (flat(gx=a, gy=y, grp=c), flat(gx=b, gy=y, grp=c)) for a, b in odd for y in range(mesh.shape["gy"]) for c in (0, 1)
    ] + [
        (flat(gx=g, gy=y, grp=a), flat(gx=g, gy=y, grp=b))
        for g in (0, gx - 1)
        for y in range(mesh.shape["gy"])
        for a, b in ends
    ]

    def send_in(message):
        return lax.ppermute(message, "gx", even)

    def send_out(message):
        return lax.ppermute(message, mesh.axis_names, hops)

    def send_sides(ymsg, zmsg):
        return lax.ppermute(ymsg, "gy", swap), lax.ppermute(zmsg, "grp", swap)

    def body(les_velocity, mean_mach, transfer_tiles, intersection_offset, acoustic_state):
        X2, Y, _, Z = les_velocity.shape
        X = acoustic_state.shape[0]
        T = Z // LANES
        blocks, plane = transfer_tiles.shape[0], transfer_tiles.shape[-1]
        wide = plane // Y
        column = lax.axis_index("gx")
        half = lax.axis_index("grp")
        has = (column > 0) & (column < gx - 1)
        info = jnp.stack([column % 2, lax.axis_index("gy"), half, has.astype(jnp.int32)]).astype(jnp.int32)
        v = les_velocity.transpose(0, 2, 1, 3)
        state = acoustic_state.transpose(2, 0, 1, 3)
        rate_z = jnp.where(half == 0, *(banded(Z, deriv, -1, h) for h in (0, 1)))
        smooth_z = jnp.where(half == 0, *(banded(Z, [-filter_weight * w for w in taps[1:]], 1, h) for h in (0, 1)))
        mach = jnp.broadcast_to(mean_mach[:, :, None], (X, Y, LANES))

        grid = (4, T, X, Y, LANES)
        source = (3, T, X, Y, LANES)
        near, far = (12 * T, Y, LANES), (4 * T * (wide - 3), Y, LANES)
        term = (3 * T * wide, Y, LANES)
        edge_y, edge_yy = (1, T, X, 8, LANES), (2, T, X, 8, LANES)
        edge_z, edge_zz = (2, X, Y, LANES), (4, X, Y, LANES)
        les_x, les_y, les_z = (3 * T, Y, LANES), (3, T, X2 // 8, 8, LANES), (3, X2, Y, LANES)
        F = pltpu.VMEM((4, T, X + 6, Y + 16, LANES), jnp.float32)
        G2 = pltpu.VMEM((2, T, X, Y, LANES), jnp.float32)
        G4 = pltpu.VMEM((4, T, X, Y, LANES), jnp.float32)
        les_scratch = [
            pltpu.VMEM((3, T, X2 + 2, Y + 16, LANES), jnp.float32),
            pltpu.VMEM((blocks // 2, 4 * plane, 3 * Z), jnp.bfloat16),
            pltpu.VMEM((3, T, X + 2 * wide, Y, LANES), jnp.float32),
        ]
        def complete(part, halos, shared, scale, next_y, next_z):
            smooth = not shared
            shapes = [near, near] if smooth else [near, far, near, far]
            sides = [edge_y, edge_z] if next_y == RATE_Y else [edge_yy, edge_zz]
            *done, ymsg, zmsg = call(
                functools.partial(edge_body, smooth=smooth, scale=scale, ycomps=next_y, zcomps=next_z),
                [*shapes, *sides],
                [info, part, *halos, *([shared[0], *shared[1]] if shared else [])],
            )
            nears, fars = (done, []) if smooth else (done[::2], done[1::2])
            return [part, *nears], fars, send_sides(ymsg, zmsg), (send_in(nears[0]), send_out(nears[1]))

        v_in, v_out, *sides = call(pack_les_body, [les_x, les_x, les_y, les_z], [info, v])
        les_edges = [send_in(v_in), send_out(v_out), *send_sides(*sides)]
        les_edges[3], tiles = lax.optimization_barrier((les_edges[3], transfer_tiles))
        tiles = tiles[:, 0].swapaxes(2, 3).reshape(blocks, 2 * plane, plane)
        tiles = jnp.concatenate([tiles, tiles], axis=2)
        at = term[0] + 3 * T
        joint = (at + near[0], Y, LANES)
        v1, S, *own, les_ym, les_zm, state, ym, zm = call(
            functools.partial(les_body, base=0, advance=True),
            [(3, T, X2, Y, LANES), source, joint, joint, les_y, les_z, grid, edge_y, edge_z],
            [info, intersection_offset, v, *les_edges, tiles, state],
            les_scratch,
            smem=2,
            flops=4000000,
        )
        terms = (send_in(own[0]), send_out(own[1]))
        sides = send_sides(ym, zm)
        les_edges = [*terms, *send_sides(les_ym, les_zm)]
        near_in, near_out = (message[at:] for message in own)
        halos = [message[at:] for message in terms]
        whole = [state, near_in, near_out]
        for step in range(STEPS):
            if step:
                whole[1], terms = lax.optimization_barrier((whole[1], terms))
            part, base = call(
                first_main, [grid, grid], [info, *whole, *sides, rate_z, mach, S], [F, G2], flops=4000000
            )
            whole, fars, sides, halos = complete(part, halos, (mach, terms), wave_step, RATE_Y, RATE_Z)
            if step + 1 < STEPS:
                S2, *terms2 = call(
                    functools.partial(les_body, base=term[0], advance=False),
                    [source, term, term],
                    [info, intersection_offset, v1, *les_edges, tiles],
                    les_scratch,
                    smem=2,
                    flops=4000000,
                )
                info, S2, *terms2 = lax.optimization_barrier((info, S2, *terms2))
                terms2 = (send_in(terms2[0]), send_out(terms2[1]))
            (part,) = call(
                second_main, [grid], [info, *whole, *fars, *sides, rate_z, mach, S, base], [F, G2], flops=4000000
            )
            whole, fars, sides, halos = complete(part, halos, (mach, terms), 0.5 * wave_step, ALL, ALL)
            if step + 1 < STEPS:
                terms, S = terms2, S2
                (part,) = call(
                    functools.partial(smooth_main, last=False),
                    [grid],
                    [info, *whole, *fars, *sides, smooth_z],
                    [F, G4],
                    flops=4000000,
                )
                whole, _, sides, halos = complete(part, halos, None, 0.0, RATE_Y, RATE_Z)
        (state,) = call(
            functools.partial(smooth_main, last=True),
            [(4, X, Y, Z)],
            [info, *whole, *fars, *sides, smooth_z, *halos],
            [F, G4],
            flops=4000000,
        )
        return state.transpose(1, 2, 0, 3)

    placed = (
        P("gx", "gy", None, "grp"),
        P("gx", "gy"),
        P("gx", "gy", None, None, None),
        P("gx"),
        P("gx", "gy", None, "grp"),
    )
    return jax.shard_map(body, mesh=mesh, in_specs=placed, out_specs=P("gx", "gy", None, "grp"), check_vma=False)
```

```python
import functools

import jax
import jax.numpy as jnp
import numpy as np
from jax import lax
from jax.experimental import pallas as pl
from jax.experimental.pallas import tpu as pltpu
from jax.sharding import PartitionSpec as P

STEPS = 2
eddy_step = 0.1
viscosity = 0.5
wave_step = 0.2
filter_weight = 0.2
deriv = (0.770882380518, -0.166705904415, 0.02084314277)
taps = (0.28739284246, -0.226146951809, 0.10630357877, -0.023853048191)

RATE_Y, RATE_Z = (0, 2), (0, 3)
ALL = (0, 1, 2, 3)
LANES = 128
VMEM = pl.BlockSpec(memory_space=pltpu.VMEM)
SMEM = pl.BlockSpec(memory_space=pltpu.SMEM)


def call(body, outs, ins, scratch=(), smem=1, flops=1000000, alias=None):
    shapes = [jax.ShapeDtypeStruct(s, jnp.float32) for s in outs]
    size = sum(o.size for o in shapes) + sum(i.size for i in ins)
    return pl.pallas_call(
        body,
        out_shape=shapes,
        in_specs=[SMEM] * smem + [VMEM] * (len(ins) - smem),
        out_specs=[VMEM] * len(shapes),
        scratch_shapes=list(scratch),
        input_output_aliases=alias or {},
        compiler_params=pltpu.CompilerParams(vmem_limit_bytes=12 * 1024 * 1024),
        cost_estimate=pl.CostEstimate(flops=flops, bytes_accessed=4 * size, transcendentals=0),
    )(*ins)


def banded(depth, weights, sign, half):
    matrix = np.zeros((depth + LANES, depth), np.float32)
    lane = np.arange(depth)
    for j, weight in enumerate(weights, 1):
        for to, factor in ((lane + j, weight), (lane - j, sign * weight)):
            ok = (to >= 0) & (to < depth)
            matrix[to[ok], lane[ok]] = factor
            beyond = to >= depth if half == 0 else to < 0
            matrix[depth + to[beyond] % LANES, lane[beyond]] = factor
    high = matrix.astype(jnp.bfloat16)
    low = (matrix - high.astype(np.float32)).astype(jnp.bfloat16)
    return np.concatenate([high, high, low])


def z_product(F, zmsg, zmat, comps, G):
    _, T, X, Y, _ = F.shape
    X, Y = X - 6, Y - 16
    for n, c in enumerate(comps):
        tiles = [F[c, t, 3 : 3 + X, 8 : 8 + Y, :].reshape(X * Y, LANES) for t in range(T)]
        tiles.append(zmsg[n].reshape(X * Y, LANES))
        high = [tile.astype(jnp.bfloat16) for tile in tiles]
        low = [(tile - top.astype(jnp.float32)).astype(jnp.bfloat16) for tile, top in zip(tiles, high)]
        out = jnp.dot(jnp.concatenate(high + low + high, axis=1), zmat[...], preferred_element_type=jnp.float32)
        for t in range(T):
            G[n, t] = out[:, t * LANES : (t + 1) * LANES].reshape(X, Y, LANES)


def shift_tiles(tiles, left, right, by, lanes):
    out = []
    row = [left] + tiles + [right]
    for at in range(1, len(tiles) + 1):
        if by > 0:
            mixed = jnp.where(lanes < by, row[at + 1], row[at])
            out.append(pltpu.roll(mixed, LANES - by, 1))
        else:
            mixed = jnp.where(lanes >= LANES + by, row[at - 1], row[at])
            out.append(pltpu.roll(mixed, -by, 1))
    return out


def side_tiles(tile, half):
    zero = jnp.zeros_like(tile)
    return jnp.where(half == 1, tile, zero), jnp.where(half == 0, tile, zero)


def known(value, has):
    return jnp.where(has == 1, value, jnp.zeros_like(value))


def lane_ids(rows):
    return lax.broadcasted_iota(jnp.int32, (rows, LANES), 1)


def ends(info, inner, X, deep):
    high = (info[0] == 0) if inner else (info[0] == 1)
    has = jnp.int32(1) if inner else info[3]
    return high, has, lambda d: jnp.where(high, X - 1 - d, d), lambda d: jnp.where(high, 2 - d, d)


def pack_sides(info, get, ymsg, zmsg, ycomps, zcomps, X, Y, T, layers):
    row, half = info[1], info[2]
    rows = lax.broadcasted_iota(jnp.int32, (8, LANES), 0)
    ys = pl.multiple_of(jnp.where(row == 0, Y - 8, 0), 8)
    turn = jnp.where(row == 0, 4, 0)
    edge = jnp.where(half == 0, T - 1, 0)

    def one(i):
        for n in range(len(ycomps) // 2):
            for t in range(T):
                first = pltpu.roll(get(ycomps[2 * n], t, i, pl.ds(ys, 8)), turn, 0)
                second = pltpu.roll(get(ycomps[2 * n + 1], t, i, pl.ds(ys, 8)), 4 - turn, 0)
                ymsg[n, t, i] = jnp.where(rows < 4, first, second)
        for n, c in enumerate(zcomps):
            zmsg[n, i] = get(c, edge, i, slice(None))

    if layers is None:
        lax.fori_loop(0, X, lambda i, carry: (one(i), carry)[1], 0, unroll=4)
    else:
        for i in layers:
            one(i)


def fill(F, f, nears, fars, ymsg, ycomps, info):
    row = info[1]
    _, T, X, Y, _ = f.shape
    y = slice(8, 8 + Y)

    def step(i, carry):
        for t in range(T):
            for c in range(4):
                F[c, t, i + 3, y, :] = f[c, t, i]
            for n, c in enumerate(ycomps):
                tile = ymsg[n // 2, t, i]
                turned = pltpu.roll(tile, 4, 0)
                if n % 2:
                    tile, turned = turned, tile
                zero = jnp.zeros_like(tile)
                F[c, t, i + 3, 0:8, :] = jnp.where(row == 1, turned, zero)
                F[c, t, i + 3, 8 + Y : 16 + Y, :] = jnp.where(row == 0, tile, zero)
        return carry

    lax.fori_loop(0, X, step, 0, unroll=4)
    zero = jnp.zeros((Y, LANES), jnp.float32)
    for side, near in enumerate(nears):
        high, _, layer, place = ends(info, side == 0, X, 3)
        for c in range(4):
            for t in range(T):
                for d in range(3):
                    F[c, t, 3 + layer(d), y, :] = near[3 * (c * T + t) + place(d)]
                    F[c, t, jnp.where(high, X + 3 + d, 2 - d), y, :] = zero
                if fars:
                    far = fars[side]
                    count = far.shape[0] // (4 * T)
                    for d in range(count):
                        F[c, t, 3 + layer(3 + d), y, :] = far[count * (c * T + t) + d]


def dx(F, c, t, i, Y):
    y = slice(8, 8 + Y)
    return sum(deriv[j - 1] * (F[c, t, i + 3 + j, y, :] - F[c, t, i + 3 - j, y, :]) for j in (1, 2, 3))


def dy(F, c, t, i, Y):
    return sum(
        deriv[j - 1] * (F[c, t, i + 3, 8 + j : 8 + Y + j, :] - F[c, t, i + 3, 8 - j : 8 + Y - j, :]) for j in (1, 2, 3)
    )


def rate_loop(F, G, mach, S, emit):
    T, X, Y = F.shape[1], F.shape[2] - 6, F.shape[3] - 16

    def step(i, carry):
        m = mach[i]
        for t in range(T):
            gp, gu, gv, gw = (dx(F, c, t, i, Y) for c in range(4))
            emit(0, t, i, -(m * gp + gu + dy(F, 2, t, i, Y) + G[1, t, i]))
            emit(1, t, i, -(m * gu + gp) - S[0, t, i])
            emit(2, t, i, -(m * gv + dy(F, 0, t, i, Y)) - S[1, t, i])
            emit(3, t, i, -(m * gw + G[0, t, i]) - S[2, t, i])
        return carry

    lax.fori_loop(0, X, step, 0, unroll=4)


def first_main(info, f, near_in, near_out, ymsg, zmsg, zmat, mach, S, o, base, F, G):
    Y = f.shape[3]
    fill(F, f, (near_in, near_out), (), ymsg, RATE_Y, info)
    z_product(F, zmsg, zmat, RATE_Z, G)

    def emit(c, t, i, value):
        center = F[c, t, i + 3, 8 : 8 + Y, :]
        base[c, t, i] = center
        o[c, t, i] = center + wave_step * value

    rate_loop(F, G, mach, S, emit)


def second_main(info, f, near_in, near_out, far_in, far_out, ymsg, zmsg, zmat, mach, S, base, o, F, G):
    Y = f.shape[3]
    fill(F, f, (near_in, near_out), (far_in, far_out), ymsg, RATE_Y, info)
    z_product(F, zmsg, zmat, RATE_Z, G)

    def emit(c, t, i, value):
        o[c, t, i] = 0.5 * (base[c, t, i] + F[c, t, i + 3, 8 : 8 + Y, :]) + (0.5 * wave_step) * value

    rate_loop(F, G, mach, S, emit)


def smooth_main(info, f, near_in, near_out, far_in, far_out, ymsg, zmsg, zmat, o, F, G, *, last):
    _, T, X, Y, _ = f.shape
    fill(F, f, (near_in, near_out), (far_in, far_out), ymsg, ALL, info)
    z_product(F, zmsg, zmat, ALL, G)
    y = slice(8, 8 + Y)

    def step(i, carry):
        for c in range(4):
            for t in range(T):
                total = (1.0 - 3.0 * filter_weight * taps[0]) * F[c, t, i + 3, y, :] + G[c, t, i]
                for j in (1, 2, 3):
                    beside = (F[c, t, i + 3 + j, y, :] + F[c, t, i + 3 - j, y, :]) + (
                        F[c, t, i + 3, 8 + j : 8 + Y + j, :] + F[c, t, i + 3, 8 - j : 8 + Y - j, :]
                    )
                    total = total - (filter_weight * taps[j]) * beside
                if last:
                    o[c, i, :, t * LANES : (t + 1) * LANES] = total
                else:
                    o[c, t, i] = total
        return carry

    lax.fori_loop(0, X, step, 0, unroll=4)


def last_body(info, f, halo_in, halo_out, o):
    _, X, Y, Z = f.shape
    T = Z // LANES
    for side, halo in enumerate((halo_in, halo_out)):
        _, has, layer, place = ends(info, side == 0, X, 3)
        weight = filter_weight * has.astype(jnp.float32)
        for c in range(4):
            for t in range(T):
                lane = slice(t * LANES, (t + 1) * LANES)
                beyond = [halo[3 * (c * T + t) + place(2 - e)] for e in range(3)]
                for d in range(3):
                    part = sum(taps[1 + d + e] * beyond[e] for e in range(3 - d))
                    o[c, layer(d), :, lane] = f[c, layer(d), :, lane] - weight * part


def edge_body(info, f, halo_in, halo_out, *rest, smooth, scale, ycomps, zcomps):
    rest = list(rest)
    mach, *terms = (None, None, None) if smooth else [rest.pop(0) for _ in range(3)]
    *done, ymsg, zmsg = rest
    sides = [done[:1], done[1:]] if smooth else [done[:2], done[2:]]
    _, T, X, Y, _ = f.shape
    deep = 3 if smooth else 3 + sides[0][1].shape[0] // (4 * T)
    for side, halo in enumerate((halo_in, halo_out)):
        near = sides[side][0]
        high, has, layer, place = ends(info, side == 0, X, deep)
        sign = (jnp.where(high, scale, -scale) * has).astype(jnp.float32)
        weight = has.astype(jnp.float32)
        for t in range(T):
            for d in range(deep):
                at = layer(d)
                values = [f[c, t, at] for c in range(4)]
                if d < 3:
                    beyond = [[halo[3 * (c * T + t) + place(2 - e)] for e in range(3 - d)] for c in range(4)]
                    coefs = taps[1:] if smooth else deriv
                    parts = [sum(coefs[d + e] * value for e, value in enumerate(column)) for column in beyond]
                    if smooth:
                        values = [value - (filter_weight * weight) * part for value, part in zip(values, parts)]
                    else:
                        m, (gp, gu, gv, gw) = mach[at], parts
                        change = (m * gp + gu, m * gu + gp, m * gv, m * gw)
                        values = [value - sign * part for value, part in zip(values, change)]
                if not smooth:
                    index = jnp.where(high, deep - 1 - d, d)
                    for c in range(3):
                        term = terms[side][(c * T + t) * deep + index]
                        values[1 + c] = values[1 + c] - (scale * weight) * term
                for c in range(4):
                    if d < 3:
                        near[3 * (c * T + t) + place(d)] = values[c]
                    else:
                        sides[side][1][(deep - 3) * (c * T + t) + d - 3] = values[c]
    pack_sides(info, lambda c, t, i, rows: f[c, t, i, rows, :], ymsg, zmsg, ycomps, zcomps, X, Y, T, None)
    for side, (near, *far) in enumerate(sides):
        _, _, layer, place = ends(info, side == 0, X, deep)
        for d in range(deep):

            def get(c, t, i, rows):
                if d < 3:
                    return near[3 * (c * T + t) + place(d), rows, :]
                return far[0][(deep - 3) * (c * T + t) + d - 3, rows, :]

            pack_sides(info, get, ymsg, zmsg, ycomps, zcomps, X, Y, T, [layer(d)])


def pack_whole(info, f, o, near_in, near_out, start, ymsg, zmsg):
    _, T, X, Y, _ = o.shape

    def step(i, carry):
        for c in range(4):
            for t in range(T):
                o[c, t, i] = f[c, i, :, t * LANES : (t + 1) * LANES]
        return carry

    lax.fori_loop(0, X, step, 0, unroll=4)
    for side, near in enumerate((near_in, near_out)):
        _, _, layer, place = ends(info, side == 0, X, 3)
        for c in range(4):
            for t in range(T):
                for d in range(3):
                    near[start + 3 * (c * T + t) + place(d)] = o[c, t, layer(d)]
    pack_sides(info, lambda c, t, i, rows: o[c, t, i, rows, :], ymsg, zmsg, RATE_Y, RATE_Z, X, Y, T, None)


def pack_les(get, shape, inner, outer, ymsg, zmsg, info, base=0):
    pos, row, half = info[0], info[1], info[2]
    _, T, X, Y, _ = shape
    si = jnp.where(pos == 0, X - 1, 0)
    so = jnp.where(pos == 0, 0, X - 1)
    rows = lax.broadcasted_iota(jnp.int32, (8, LANES), 0)
    ys = pl.multiple_of(jnp.where(row == 0, Y - 8, 0), 8)
    turn = [jnp.where(row == 0, (r + 1) % 8, r) for r in range(8)]
    for c in range(3):
        for t in range(T):
            inner[base + c * T + t] = get(c, t, si, slice(None))
            outer[base + c * T + t] = get(c, t, so, slice(None))
            for n in range(X // 8):
                acc = jnp.zeros((8, LANES), jnp.float32)
                for r in range(8):
                    tile = get(c, t, 8 * n + r, pl.ds(ys, 8))
                    acc = jnp.where(rows == r, pltpu.roll(tile, turn[r], 0), acc)
                ymsg[c, t, n] = acc

    def step(i, carry):
        for c in range(3):
            last, first = get(c, T - 1, i, slice(None)), get(c, 0, i, slice(None))
            zmsg[c, i] = jnp.where(half == 0, last, first)
        return carry

    lax.fori_loop(0, X, step, 0, unroll=4)


def getter(v):
    if len(v.shape) == 4:
        return lambda c, t, i, rows: v[i, c, rows, t * LANES : (t + 1) * LANES]
    return lambda c, t, i, rows: v[c, t, i, rows, :]


def pack_les_body(info, v, inner, outer, ymsg, zmsg):
    X, _, Y, Z = v.shape
    pack_les(getter(v), (3, Z // LANES, X, Y, LANES), inner, outer, ymsg, zmsg, info)


def les_body(info, offset, v, inner, outer, ymsg, zmsg, tiles, *rest, base, advance):
    if advance:
        state, v1, own, n_in, n_out, ny, nz, f, fy, fz, V, LB, ACC = rest
    else:
        own, n_in, n_out, V, LB, ACC = rest
    pos, row, half = info[0], info[1], info[2]
    _, T, X, Y, _ = V.shape
    X, Y = X - 2, Y - 16
    get = getter(v)
    blocks = 2 * LB.shape[0]
    wide = X // blocks
    plane = wide * Y
    hi = jnp.where(pos == 0, X + 1, 0)
    ho = jnp.where(pos == 0, 0, X + 1)
    for c in range(3):
        for t in range(T):
            V[c, t, hi, 8 : 8 + Y, :] = inner[base + c * T + t]
            V[c, t, ho, 8 : 8 + Y, :] = known(outer[base + c * T + t], info[3])
            for n in range(X // 8):
                tile = ymsg[c, t, n]
                zero = jnp.zeros_like(tile)
                for r in range(8):
                    low = pltpu.roll(tile, 7 - r, 0) if r < 7 else tile
                    high = pltpu.roll(tile, 8 - r, 0) if r else tile
                    V[c, t, 8 * n + r + 1, 0:8, :] = jnp.where(row == 1, low, zero)
                    V[c, t, 8 * n + r + 1, 8 + Y : 16 + Y, :] = jnp.where(row == 0, high, zero)

    def copy(i, carry):
        for c in range(3):
            for t in range(T):
                V[c, t, i + 1, 8 : 8 + Y, :] = get(c, t, i, slice(None))
        return carry

    lax.fori_loop(0, X, copy, 0, unroll=4)
    ACC[...] = jnp.zeros_like(ACC)
    lanes = lane_ids(Y)
    y = slice(8, 8 + Y)

    def step(i, carry):
        center = [[V[c, t, i + 1, y, :] for t in range(T)] for c in range(3)]
        ahead, behind = [], []
        for c in range(3 if advance else 2):
            left, right = side_tiles(zmsg[c, i], half)
            ahead.append(shift_tiles(center[c], left, right, 1, lanes))
            behind.append(shift_tiles(center[c], left, right, -1, lanes))
        at = lax.rem(i, 2 * wide) * Y
        at = at + jnp.where(at >= plane, plane, 0)
        b = i // (2 * wide)
        for t in range(T):
            xa = [V[c, t, i + 2, y, :] for c in range(3)]
            xb = [V[c, t, i, y, :] for c in range(3)]
            ya = [V[c, t, i + 1, 9 : 9 + Y, :] for c in range(3)]
            yb = [V[c, t, i + 1, 7 : 7 + Y, :] for c in range(3)]
            u, w, q = center[0][t], center[1][t], center[2][t]
            vx = 0.5 * ((ya[2] - yb[2]) - (ahead[1][t] - behind[1][t]))
            vy = 0.5 * ((ahead[0][t] - behind[0][t]) - (xa[2] - xb[2]))
            vz = 0.5 * ((xa[1] - xb[1]) - (ya[0] - yb[0]))
            lamb = [vy * q - vz * w, vz * u - vx * q, vx * w - vy * u]
            for c in range(3):
                high = lamb[c].astype(jnp.bfloat16)
                low = (lamb[c] - high.astype(jnp.float32)).astype(jnp.bfloat16)
                lane = slice((c * T + t) * LANES, (c * T + t + 1) * LANES)
                LB[b, pl.ds(pl.multiple_of(at, 16), Y), lane] = high
                LB[b, pl.ds(pl.multiple_of(plane + at, 16), Y), lane] = low
                if advance:
                    laplace = -6.0 * center[c][t] + ((xa[c] + xb[c]) + (ya[c] + yb[c]) + (ahead[c][t] + behind[c][t]))
                    v1[c, t, i] = center[c][t] + eddy_step * (viscosity * laplace - lamb[c])
        return carry

    lax.fori_loop(0, X, step, 0, unroll=4)

    for m in range(blocks // 2):
        a, b = [[tiles[2 * m + n, k] for k in (0, 1)] for n in (0, 1)]
        parts = [
            (jnp.concatenate([a[0], a[0], b[0], b[0]]), LB[m]),
            (jnp.concatenate([a[1], a[1]]), LB[m, : 2 * plane]),
            (jnp.concatenate([b[1], b[1]]), LB[m, 2 * plane :]),
        ]
        out = [
            lax.dot_general(w, x, (((0,), (0,)), ((), ())), preferred_element_type=jnp.float32) for w, x in parts
        ]
        at = (m + 1) * wide
        places = [at, at + offset[2 * m] * wide, at + offset[2 * m + 1] * wide]
        for c in range(3):
            for t in range(T):
                lane = slice((c * T + t) * LANES, (c * T + t + 1) * LANES)
                for to, value in zip(places, out):
                    for l in range(wide):
                        ACC[c, t, to + l] = ACC[c, t, to + l] + value[l * Y : (l + 1) * Y, lane]

    depth = own.shape[2]
    own[...] = ACC[:, :, wide : wide + depth]
    ti = jnp.where(pos == 0, depth + wide, 0)
    to = jnp.where(pos == 0, 0, depth + wide)
    for c in range(3):
        for t in range(T):
            for l in range(wide):
                n_in[(c * T + t) * wide + l] = ACC[c, t, ti + l]
                n_out[(c * T + t) * wide + l] = ACC[c, t, to + l]
    if advance:
        pack_les(getter(v1), v1.shape, n_in, n_out, ny, nz, info, 3 * T * wide)
        pack_whole(info, state, f, n_in, n_out, 3 * T * (wide + 1), fy, fz)


def solution(mesh):
    gx = mesh.shape["gx"]
    swap = [(0, 1), (1, 0)]
    even = [pair for k in range(gx // 2) for pair in ((2 * k, 2 * k + 1), (2 * k + 1, 2 * k))]
    odd = [pair for k in range(gx // 2 - 1) for pair in ((2 * k + 1, 2 * k + 2), (2 * k + 2, 2 * k + 1))]

    def flat(**at):
        index = 0
        for axis in mesh.axis_names:
            index = index * mesh.shape[axis] + at[axis]
        return index

    ends = [(0, 1), (1, 0)]
    hops = [
        (flat(gx=a, gy=y, grp=c), flat(gx=b, gy=y, grp=c)) for a, b in odd for y in range(mesh.shape["gy"]) for c in (0, 1)
    ] + [
        (flat(gx=g, gy=y, grp=a), flat(gx=g, gy=y, grp=b))
        for g in (0, gx - 1)
        for y in range(mesh.shape["gy"])
        for a, b in ends
    ]

    def send_in(message):
        return lax.ppermute(message, "gx", even)

    def send_out(message):
        return lax.ppermute(message, mesh.axis_names, hops)

    def send_sides(ymsg, zmsg):
        return lax.ppermute(ymsg, "gy", swap), lax.ppermute(zmsg, "grp", swap)

    def body(les_velocity, mean_mach, transfer_tiles, intersection_offset, acoustic_state):
        X2, Y, _, Z = les_velocity.shape
        X = acoustic_state.shape[0]
        T = Z // LANES
        blocks, plane = transfer_tiles.shape[0], transfer_tiles.shape[-1]
        wide = plane // Y
        column = lax.axis_index("gx")
        half = lax.axis_index("grp")
        has = (column > 0) & (column < gx - 1)
        info = jnp.stack([column % 2, lax.axis_index("gy"), half, has.astype(jnp.int32)]).astype(jnp.int32)
        v = les_velocity.transpose(0, 2, 1, 3)
        state = acoustic_state.transpose(2, 0, 1, 3)
        rate_z = jnp.where(half == 0, *(banded(Z, deriv, -1, h) for h in (0, 1)))
        smooth_z = jnp.where(half == 0, *(banded(Z, [-filter_weight * w for w in taps[1:]], 1, h) for h in (0, 1)))
        mach = jnp.broadcast_to(mean_mach[:, :, None], (X, Y, LANES))

        grid = (4, T, X, Y, LANES)
        source = (3, T, X, Y, LANES)
        near, far = (12 * T, Y, LANES), (4 * T * (wide - 3), Y, LANES)
        term = (3 * T * wide, Y, LANES)
        edge_y, edge_yy = (1, T, X, 8, LANES), (2, T, X, 8, LANES)
        edge_z, edge_zz = (2, X, Y, LANES), (4, X, Y, LANES)
        les_x, les_y, les_z = (3 * T, Y, LANES), (3, T, X2 // 8, 8, LANES), (3, X2, Y, LANES)
        F = pltpu.VMEM((4, T, X + 6, Y + 16, LANES), jnp.float32)
        G2 = pltpu.VMEM((2, T, X, Y, LANES), jnp.float32)
        G4 = pltpu.VMEM((4, T, X, Y, LANES), jnp.float32)
        les_scratch = [
            pltpu.VMEM((3, T, X2 + 2, Y + 16, LANES), jnp.float32),
            pltpu.VMEM((blocks // 2, 4 * plane, 3 * Z), jnp.bfloat16),
            pltpu.VMEM((3, T, X + 2 * wide, Y, LANES), jnp.float32),
        ]
        def complete(part, halos, shared, scale, next_y, next_z):
            smooth = not shared
            shapes = [near, near] if smooth else [near, far, near, far]
            sides = [edge_y, edge_z] if next_y == RATE_Y else [edge_yy, edge_zz]
            *done, ymsg, zmsg = call(
                functools.partial(edge_body, smooth=smooth, scale=scale, ycomps=next_y, zcomps=next_z),
                [*shapes, *sides],
                [info, part, *halos, *([shared[0], *shared[1]] if shared else [])],
            )
            nears, fars = (done, []) if smooth else (done[::2], done[1::2])
            return [part, *nears], fars, send_sides(ymsg, zmsg), (send_in(nears[0]), send_out(nears[1]))

        v_in, v_out, *sides = call(pack_les_body, [les_x, les_x, les_y, les_z], [info, v])
        les_edges = [send_in(v_in), send_out(v_out), *send_sides(*sides)]
        tiles = transfer_tiles[:, 0]
        at = term[0] + 3 * T
        joint = (at + near[0], Y, LANES)
        v1, S, *own, les_ym, les_zm, state, ym, zm = call(
            functools.partial(les_body, base=0, advance=True),
            [(3, T, X2, Y, LANES), source, joint, joint, les_y, les_z, grid, edge_y, edge_z],
            [info, intersection_offset, v, *les_edges, tiles, state],
            les_scratch,
            smem=2,
            flops=4000000,
        )
        terms = (send_in(own[0]), send_out(own[1]))
        sides = send_sides(ym, zm)
        les_edges = [*terms, *send_sides(les_ym, les_zm)]
        near_in, near_out = (message[at:] for message in own)
        halos = [message[at:] for message in terms]
        whole = [state, near_in, near_out]
        for step in range(STEPS):
            if step:
                whole[1], terms = lax.optimization_barrier((whole[1], terms))
            part, base = call(
                first_main, [grid, grid], [info, *whole, *sides, rate_z, mach, S], [F, G2], flops=4000000
            )
            whole, fars, sides, halos = complete(part, halos, (mach, terms), wave_step, RATE_Y, RATE_Z)
            if step + 1 < STEPS:
                S2, *terms2 = call(
                    functools.partial(les_body, base=term[0], advance=False),
                    [source, term, term],
                    [info, intersection_offset, v1, *les_edges, tiles],
                    les_scratch,
                    smem=2,
                    flops=4000000,
                )
                info, S2, *terms2 = lax.optimization_barrier((info, S2, *terms2))
                terms2 = (send_in(terms2[0]), send_out(terms2[1]))
            (part,) = call(
                second_main, [grid], [info, *whole, *fars, *sides, rate_z, mach, S, base], [F, G2], flops=4000000
            )
            whole, fars, sides, halos = complete(part, halos, (mach, terms), 0.5 * wave_step, ALL, ALL)
            if step + 1 < STEPS:
                terms, S = terms2, S2
                (part,) = call(
                    functools.partial(smooth_main, last=False),
                    [grid],
                    [info, *whole, *fars, *sides, smooth_z],
                    [F, G4],
                    flops=4000000,
                )
                whole, _, sides, halos = complete(part, halos, None, 0.0, RATE_Y, RATE_Z)
        (part,) = call(
            functools.partial(smooth_main, last=True),
            [(4, X, Y, Z)],
            [info, *whole, *fars, *sides, smooth_z],
            [F, G4],
            flops=4000000,
        )
        (state,) = call(last_body, [(4, X, Y, Z)], [info, part, *halos], alias={1: 0})
        return state.transpose(1, 2, 0, 3)

    placed = (
        P("gx", "gy", None, "grp"),
        P("gx", "gy"),
        P("gx", "gy", None, None, None),
        P("gx"),
        P("gx", "gy", None, "grp"),
    )
    return jax.shard_map(body, mesh=mesh, in_specs=placed, out_specs=P("gx", "gy", None, "grp"), check_vma=False)
```

```python
import functools

import jax
import jax.numpy as jnp
import numpy as np
from jax import lax
from jax.experimental import pallas as pl
from jax.experimental.pallas import tpu as pltpu
from jax.sharding import PartitionSpec as P

STEPS = 2
eddy_step = 0.1
viscosity = 0.5
wave_step = 0.2
filter_weight = 0.2
deriv = (0.770882380518, -0.166705904415, 0.02084314277)
taps = (0.28739284246, -0.226146951809, 0.10630357877, -0.023853048191)

RATE_Y, RATE_Z = (0, 2), (0, 3)
ALL = (0, 1, 2, 3)
LANES = 128
VMEM = pl.BlockSpec(memory_space=pltpu.VMEM)
ANY = pl.BlockSpec(memory_space=pl.ANY)


def place():
    column = lax.axis_index("gx")
    inside = (column > 0) & (column < lax.axis_size("gx") - 1)
    return lax.rem(column, 2), lax.axis_index("gy"), lax.axis_index("grp"), inside.astype(jnp.int32)


def call(body, outs, ins, scratch=(), away=0, flops=1000000, alias=None):
    shapes = [jax.ShapeDtypeStruct(s, jnp.float32) for s in outs]
    size = sum(o.size for o in shapes) + sum(i.size for i in ins)
    return pl.pallas_call(
        lambda *refs: body(place(), *refs),
        out_shape=shapes,
        in_specs=[ANY] * away + [VMEM] * (len(ins) - away),
        out_specs=[VMEM] * len(shapes),
        scratch_shapes=list(scratch),
        input_output_aliases=alias or {},
        compiler_params=pltpu.CompilerParams(vmem_limit_bytes=12 * 1024 * 1024),
        cost_estimate=pl.CostEstimate(flops=flops, bytes_accessed=4 * size, transcendentals=0),
    )(*ins)


def banded(depth, weights, sign, half):
    matrix = np.zeros((depth + LANES, depth), np.float32)
    lane = np.arange(depth)
    for j, weight in enumerate(weights, 1):
        for to, factor in ((lane + j, weight), (lane - j, sign * weight)):
            ok = (to >= 0) & (to < depth)
            matrix[to[ok], lane[ok]] = factor
            beyond = to >= depth if half == 0 else to < 0
            matrix[depth + to[beyond] % LANES, lane[beyond]] = factor
    high = matrix.astype(jnp.bfloat16)
    low = (matrix - high.astype(np.float32)).astype(jnp.bfloat16)
    return np.concatenate([high, high, low])


def z_product(F, zmsg, zmat, comps, G, half):
    _, T, X, Y, _ = F.shape
    X, Y = X - 6, Y - 16
    for n, c in enumerate(comps):
        tiles = [F[c, t, 3 : 3 + X, 8 : 8 + Y, :].reshape(X * Y, LANES) for t in range(T)]
        tiles.append(zmsg[n * X : (n + 1) * X].reshape(X * Y, LANES))
        high = [tile.astype(jnp.bfloat16) for tile in tiles]
        low = [(tile - top.astype(jnp.float32)).astype(jnp.bfloat16) for tile, top in zip(tiles, high)]
        out = jnp.dot(jnp.concatenate(high + low + high, axis=1), zmat[half], preferred_element_type=jnp.float32)
        for t in range(T):
            G[n, t] = out[:, t * LANES : (t + 1) * LANES].reshape(X, Y, LANES)


def shift_tiles(tiles, left, right, by, lanes):
    out = []
    row = [left] + tiles + [right]
    for at in range(1, len(tiles) + 1):
        if by > 0:
            mixed = jnp.where(lanes < by, row[at + 1], row[at])
            out.append(pltpu.roll(mixed, LANES - by, 1))
        else:
            mixed = jnp.where(lanes >= LANES + by, row[at - 1], row[at])
            out.append(pltpu.roll(mixed, -by, 1))
    return out


def side_tiles(tile, half):
    zero = jnp.zeros_like(tile)
    return jnp.where(half == 1, tile, zero), jnp.where(half == 0, tile, zero)


def known(value, has):
    return jnp.where(has == 1, value, jnp.zeros_like(value))


def lane_ids(rows):
    return lax.broadcasted_iota(jnp.int32, (rows, LANES), 1)


def ends(info, inner, X, deep):
    high = (info[0] == 0) if inner else (info[0] == 1)
    has = jnp.int32(1) if inner else info[3]
    return high, has, lambda d: jnp.where(high, X - 1 - d, d), lambda d: jnp.where(high, 2 - d, d)


def pack_sides(info, get, ymsg, zmsg, ycomps, zcomps, X, Y, T, layers):
    row, half = info[1], info[2]
    rows = lax.broadcasted_iota(jnp.int32, (8, LANES), 0)
    ys = pl.multiple_of(jnp.where(row == 0, Y - 8, 0), 8)
    turn = jnp.where(row == 0, 4, 0)
    edge = jnp.where(half == 0, T - 1, 0)

    def one(i):
        for n in range(len(ycomps) // 2):
            for t in range(T):
                first = pltpu.roll(get(ycomps[2 * n], t, i, pl.ds(ys, 8)), turn, 0)
                second = pltpu.roll(get(ycomps[2 * n + 1], t, i, pl.ds(ys, 8)), 4 - turn, 0)
                ymsg[(n * T + t) * X + i] = jnp.where(rows < 4, first, second)
        for n, c in enumerate(zcomps):
            zmsg[n * X + i] = get(c, edge, i, slice(None))

    if layers is None:
        lax.fori_loop(0, X, lambda i, carry: (one(i), carry)[1], 0, unroll=4)
    else:
        for i in layers:
            one(i)


def fill(F, f, nears, fars, ymsg, ycomps, info):
    row = info[1]
    _, T, X, Y, _ = f.shape
    y = slice(8, 8 + Y)

    def step(i, carry):
        for t in range(T):
            for c in range(4):
                F[c, t, i + 3, y, :] = f[c, t, i]
            for n, c in enumerate(ycomps):
                tile = ymsg[(n // 2 * T + t) * X + i]
                turned = pltpu.roll(tile, 4, 0)
                if n % 2:
                    tile, turned = turned, tile
                zero = jnp.zeros_like(tile)
                F[c, t, i + 3, 0:8, :] = jnp.where(row == 1, turned, zero)
                F[c, t, i + 3, 8 + Y : 16 + Y, :] = jnp.where(row == 0, tile, zero)
        return carry

    lax.fori_loop(0, X, step, 0, unroll=4)
    zero = jnp.zeros((Y, LANES), jnp.float32)
    for side, near in enumerate(nears):
        high, _, layer, place = ends(info, side == 0, X, 3)
        for c in range(4):
            for t in range(T):
                for d in range(3):
                    F[c, t, 3 + layer(d), y, :] = near[3 * (c * T + t) + place(d)]
                    F[c, t, jnp.where(high, X + 3 + d, 2 - d), y, :] = zero
                if fars:
                    far = fars[side]
                    count = far.shape[0] // (4 * T)
                    for d in range(count):
                        F[c, t, 3 + layer(3 + d), y, :] = far[count * (c * T + t) + d]


def dx(F, c, t, i, Y):
    y = slice(8, 8 + Y)
    return sum(deriv[j - 1] * (F[c, t, i + 3 + j, y, :] - F[c, t, i + 3 - j, y, :]) for j in (1, 2, 3))


def dy(F, c, t, i, Y):
    return sum(
        deriv[j - 1] * (F[c, t, i + 3, 8 + j : 8 + Y + j, :] - F[c, t, i + 3, 8 - j : 8 + Y - j, :]) for j in (1, 2, 3)
    )


def rate_loop(F, G, mach, S, emit):
    T, X, Y = F.shape[1], F.shape[2] - 6, F.shape[3] - 16

    def step(i, carry):
        m = mach[i]
        for t in range(T):
            gp, gu, gv, gw = (dx(F, c, t, i, Y) for c in range(4))
            emit(0, t, i, -(m * gp + gu + dy(F, 2, t, i, Y) + G[1, t, i]))
            emit(1, t, i, -(m * gu + gp) - S[0, t, i])
            emit(2, t, i, -(m * gv + dy(F, 0, t, i, Y)) - S[1, t, i])
            emit(3, t, i, -(m * gw + G[0, t, i]) - S[2, t, i])
        return carry

    lax.fori_loop(0, X, step, 0, unroll=4)


def first_main(info, f, near_in, near_out, ymsg, zmsg, zmat, mach, S, o, base, F, G, *, near_base):
    Y = f.shape[3]
    fill(F, f, (near_in.at[near_base:], near_out.at[near_base:]), (), ymsg, RATE_Y, info)
    z_product(F, zmsg, zmat, RATE_Z, G, info[2])

    def emit(c, t, i, value):
        center = F[c, t, i + 3, 8 : 8 + Y, :]
        base[c, t, i] = center
        o[c, t, i] = center + wave_step * value

    rate_loop(F, G, mach, S, emit)


def second_main(info, f, near_in, near_out, far_in, far_out, ymsg, zmsg, zmat, mach, S, base, o, F, G):
    Y = f.shape[3]
    fill(F, f, (near_in, near_out), (far_in, far_out), ymsg, RATE_Y, info)
    z_product(F, zmsg, zmat, RATE_Z, G, info[2])

    def emit(c, t, i, value):
        o[c, t, i] = 0.5 * (base[c, t, i] + F[c, t, i + 3, 8 : 8 + Y, :]) + (0.5 * wave_step) * value

    rate_loop(F, G, mach, S, emit)


def smooth_main(info, f, near_in, near_out, far_in, far_out, ymsg, zmsg, zmat, o, F, G, *, last):
    _, T, X, Y, _ = f.shape
    fill(F, f, (near_in, near_out), (far_in, far_out), ymsg, ALL, info)
    z_product(F, zmsg, zmat, ALL, G, info[2])
    y = slice(8, 8 + Y)

    def step(i, carry):
        for c in range(4):
            for t in range(T):
                total = (1.0 - 3.0 * filter_weight * taps[0]) * F[c, t, i + 3, y, :] + G[c, t, i]
                for j in (1, 2, 3):
                    beside = (F[c, t, i + 3 + j, y, :] + F[c, t, i + 3 - j, y, :]) + (
                        F[c, t, i + 3, 8 + j : 8 + Y + j, :] + F[c, t, i + 3, 8 - j : 8 + Y - j, :]
                    )
                    total = total - (filter_weight * taps[j]) * beside
                if last:
                    o[c, i, :, t * LANES : (t + 1) * LANES] = total
                else:
                    o[c, t, i] = total
        return carry

    lax.fori_loop(0, X, step, 0, unroll=4)


def last_body(info, f, halo_in, halo_out, o):
    _, X, Y, Z = f.shape
    T = Z // LANES
    for side, halo in enumerate((halo_in, halo_out)):
        _, has, layer, place = ends(info, side == 0, X, 3)
        weight = filter_weight * has.astype(jnp.float32)
        for c in range(4):
            for t in range(T):
                lane = slice(t * LANES, (t + 1) * LANES)
                beyond = [halo[3 * (c * T + t) + place(2 - e)] for e in range(3)]
                for d in range(3):
                    part = sum(taps[1 + d + e] * beyond[e] for e in range(3 - d))
                    o[c, layer(d), :, lane] = f[c, layer(d), :, lane] - weight * part


def edge_body(info, f, halo_in, halo_out, *rest, smooth, scale, ycomps, zcomps, halo_base):
    rest = list(rest)
    mach, *terms = (None, None, None) if smooth else [rest.pop(0) for _ in range(3)]
    *done, ymsg, zmsg = rest
    sides = [done[:1], done[1:]] if smooth else [done[:2], done[2:]]
    _, T, X, Y, _ = f.shape
    deep = 3 if smooth else 3 + sides[0][1].shape[0] // (4 * T)
    for side, halo in enumerate((halo_in.at[halo_base:], halo_out.at[halo_base:])):
        near = sides[side][0]
        high, has, layer, place = ends(info, side == 0, X, deep)
        sign = (jnp.where(high, scale, -scale) * has).astype(jnp.float32)
        weight = has.astype(jnp.float32)
        for t in range(T):
            for d in range(deep):
                at = layer(d)
                values = [f[c, t, at] for c in range(4)]
                if d < 3:
                    beyond = [[halo[3 * (c * T + t) + place(2 - e)] for e in range(3 - d)] for c in range(4)]
                    coefs = taps[1:] if smooth else deriv
                    parts = [sum(coefs[d + e] * value for e, value in enumerate(column)) for column in beyond]
                    if smooth:
                        values = [value - (filter_weight * weight) * part for value, part in zip(values, parts)]
                    else:
                        m, (gp, gu, gv, gw) = mach[at], parts
                        change = (m * gp + gu, m * gu + gp, m * gv, m * gw)
                        values = [value - sign * part for value, part in zip(values, change)]
                if not smooth:
                    index = jnp.where(high, deep - 1 - d, d)
                    for c in range(3):
                        term = terms[side][(c * T + t) * deep + index]
                        values[1 + c] = values[1 + c] - (scale * weight) * term
                for c in range(4):
                    if d < 3:
                        near[3 * (c * T + t) + place(d)] = values[c]
                    else:
                        sides[side][1][(deep - 3) * (c * T + t) + d - 3] = values[c]
    pack_sides(info, lambda c, t, i, rows: f[c, t, i, rows, :], ymsg, zmsg, ycomps, zcomps, X, Y, T, None)
    for side, (near, *far) in enumerate(sides):
        _, _, layer, place = ends(info, side == 0, X, deep)
        for d in range(deep):

            def get(c, t, i, rows):
                if d < 3:
                    return near[3 * (c * T + t) + place(d), rows, :]
                return far[0][(deep - 3) * (c * T + t) + d - 3, rows, :]

            pack_sides(info, get, ymsg, zmsg, ycomps, zcomps, X, Y, T, [layer(d)])


def pack_whole(info, f, o, near_in, near_out, start, ymsg, zmsg):
    _, T, X, Y, _ = o.shape

    def step(i, carry):
        for c in range(4):
            for t in range(T):
                o[c, t, i] = f[c, i, :, t * LANES : (t + 1) * LANES]
        return carry

    lax.fori_loop(0, X, step, 0, unroll=4)
    for side, near in enumerate((near_in, near_out)):
        _, _, layer, place = ends(info, side == 0, X, 3)
        for c in range(4):
            for t in range(T):
                for d in range(3):
                    near[start + 3 * (c * T + t) + place(d)] = o[c, t, layer(d)]
    pack_sides(info, lambda c, t, i, rows: o[c, t, i, rows, :], ymsg, zmsg, RATE_Y, RATE_Z, X, Y, T, None)


def pack_les(get, shape, inner, outer, ymsg, zmsg, info, base=0, ybase=0, zbase=0):
    pos, row, half = info[0], info[1], info[2]
    _, T, X, Y, _ = shape
    si = jnp.where(pos == 0, X - 1, 0)
    so = jnp.where(pos == 0, 0, X - 1)
    rows = lax.broadcasted_iota(jnp.int32, (8, LANES), 0)
    ys = pl.multiple_of(jnp.where(row == 0, Y - 8, 0), 8)
    turn = [jnp.where(row == 0, (r + 1) % 8, r) for r in range(8)]
    for c in range(3):
        for t in range(T):
            inner[base + c * T + t] = get(c, t, si, slice(None))
            outer[base + c * T + t] = get(c, t, so, slice(None))
            for n in range(X // 8):
                acc = jnp.zeros((8, LANES), jnp.float32)
                for r in range(8):
                    tile = get(c, t, 8 * n + r, pl.ds(ys, 8))
                    acc = jnp.where(rows == r, pltpu.roll(tile, turn[r], 0), acc)
                ymsg[ybase + (c * T + t) * (X // 8) + n] = acc

    def step(i, carry):
        for c in range(3):
            last, first = get(c, T - 1, i, slice(None)), get(c, 0, i, slice(None))
            zmsg[zbase + c * X + i] = jnp.where(half == 0, last, first)
        return carry

    lax.fori_loop(0, X, step, 0, unroll=4)


def getter(v):
    if len(v.shape) == 4:
        return lambda c, t, i, rows: v[i, c, rows, t * LANES : (t + 1) * LANES]
    return lambda c, t, i, rows: v[c, t, i, rows, :]


def pack_les_body(info, v, inner, outer, ymsg, zmsg):
    X, _, Y, Z = v.shape
    pack_les(getter(v), (3, Z // LANES, X, Y, LANES), inner, outer, ymsg, zmsg, info)


def les_body(info, offsets, v, inner, outer, ymsg, zmsg, tiles, *rest, base, ybase, zbase, advance):
    if advance:
        state, v1, own, n_in, n_out, f, ny, nz, V, LB, ACC, offset, sem = rest
    else:
        own, n_in, n_out, V, LB, ACC, offset, sem = rest
    copy_in = pltpu.make_async_copy(offsets, offset, sem)
    copy_in.start()
    pos, row, half = info[0], info[1], info[2]
    _, T, X, Y, _ = V.shape
    X, Y = X - 2, Y - 16
    get = getter(v)
    blocks = 2 * LB.shape[0]
    wide = X // blocks
    plane = wide * Y
    hi = jnp.where(pos == 0, X + 1, 0)
    ho = jnp.where(pos == 0, 0, X + 1)
    for c in range(3):
        for t in range(T):
            V[c, t, hi, 8 : 8 + Y, :] = inner[base + c * T + t]
            V[c, t, ho, 8 : 8 + Y, :] = known(outer[base + c * T + t], info[3])
            for n in range(X // 8):
                tile = ymsg[ybase + (c * T + t) * (X // 8) + n]
                zero = jnp.zeros_like(tile)
                for r in range(8):
                    low = pltpu.roll(tile, 7 - r, 0) if r < 7 else tile
                    high = pltpu.roll(tile, 8 - r, 0) if r else tile
                    V[c, t, 8 * n + r + 1, 0:8, :] = jnp.where(row == 1, low, zero)
                    V[c, t, 8 * n + r + 1, 8 + Y : 16 + Y, :] = jnp.where(row == 0, high, zero)

    def copy(i, carry):
        for c in range(3):
            for t in range(T):
                V[c, t, i + 1, 8 : 8 + Y, :] = get(c, t, i, slice(None))
        return carry

    lax.fori_loop(0, X, copy, 0, unroll=4)
    ACC[...] = jnp.zeros_like(ACC)
    lanes = lane_ids(Y)
    y = slice(8, 8 + Y)

    def step(i, carry):
        center = [[V[c, t, i + 1, y, :] for t in range(T)] for c in range(3)]
        ahead, behind = [], []
        for c in range(3 if advance else 2):
            left, right = side_tiles(zmsg[zbase + c * X + i], half)
            ahead.append(shift_tiles(center[c], left, right, 1, lanes))
            behind.append(shift_tiles(center[c], left, right, -1, lanes))
        at = lax.rem(i, 2 * wide) * Y
        at = at + jnp.where(at >= plane, plane, 0)
        b = i // (2 * wide)
        for t in range(T):
            xa = [V[c, t, i + 2, y, :] for c in range(3)]
            xb = [V[c, t, i, y, :] for c in range(3)]
            ya = [V[c, t, i + 1, 9 : 9 + Y, :] for c in range(3)]
            yb = [V[c, t, i + 1, 7 : 7 + Y, :] for c in range(3)]
            u, w, q = center[0][t], center[1][t], center[2][t]
            vx = 0.5 * ((ya[2] - yb[2]) - (ahead[1][t] - behind[1][t]))
            vy = 0.5 * ((ahead[0][t] - behind[0][t]) - (xa[2] - xb[2]))
            vz = 0.5 * ((xa[1] - xb[1]) - (ya[0] - yb[0]))
            lamb = [vy * q - vz * w, vz * u - vx * q, vx * w - vy * u]
            for c in range(3):
                high = lamb[c].astype(jnp.bfloat16)
                low = (lamb[c] - high.astype(jnp.float32)).astype(jnp.bfloat16)
                lane = slice((c * T + t) * LANES, (c * T + t + 1) * LANES)
                LB[b, pl.ds(pl.multiple_of(at, 16), Y), lane] = high
                LB[b, pl.ds(pl.multiple_of(plane + at, 16), Y), lane] = low
                if advance:
                    laplace = -6.0 * center[c][t] + ((xa[c] + xb[c]) + (ya[c] + yb[c]) + (ahead[c][t] + behind[c][t]))
                    v1[c, t, i] = center[c][t] + eddy_step * (viscosity * laplace - lamb[c])
        return carry

    lax.fori_loop(0, X, step, 0, unroll=4)

    copy_in.wait()
    for m in range(blocks // 2):
        a, b = [[tiles[2 * m + n, k] for k in (0, 1)] for n in (0, 1)]
        parts = [
            (jnp.concatenate([a[0], a[0], b[0], b[0]]), LB[m]),
            (jnp.concatenate([a[1], a[1]]), LB[m, : 2 * plane]),
            (jnp.concatenate([b[1], b[1]]), LB[m, 2 * plane :]),
        ]
        out = [
            lax.dot_general(w, x, (((0,), (0,)), ((), ())), preferred_element_type=jnp.float32) for w, x in parts
        ]
        at = (m + 1) * wide
        places = [at, at + offset[2 * m] * wide, at + offset[2 * m + 1] * wide]
        for c in range(3):
            for t in range(T):
                lane = slice((c * T + t) * LANES, (c * T + t + 1) * LANES)
                for to, value in zip(places, out):
                    for l in range(wide):
                        ACC[c, t, to + l] = ACC[c, t, to + l] + value[l * Y : (l + 1) * Y, lane]

    depth = own.shape[2]
    own[...] = ACC[:, :, wide : wide + depth]
    ti = jnp.where(pos == 0, depth + wide, 0)
    to = jnp.where(pos == 0, 0, depth + wide)
    for c in range(3):
        for t in range(T):
            for l in range(wide):
                n_in[(c * T + t) * wide + l] = ACC[c, t, ti + l]
                n_out[(c * T + t) * wide + l] = ACC[c, t, to + l]
    if advance:
        pack_whole(info, state, f, n_in, n_out, 3 * T * (wide + 1), ny, nz)
        pack_les(getter(v1), v1.shape, n_in, n_out, ny, nz, info, 3 * T * wide, T * f.shape[2], 2 * f.shape[2])


def solution(mesh):
    gx = mesh.shape["gx"]
    swap = [(0, 1), (1, 0)]
    even = [pair for k in range(gx // 2) for pair in ((2 * k, 2 * k + 1), (2 * k + 1, 2 * k))]
    odd = [pair for k in range(gx // 2 - 1) for pair in ((2 * k + 1, 2 * k + 2), (2 * k + 2, 2 * k + 1))]

    def flat(**at):
        index = 0
        for axis in mesh.axis_names:
            index = index * mesh.shape[axis] + at[axis]
        return index

    ends = [(0, 1), (1, 0)]
    hops = [
        (flat(gx=a, gy=y, grp=c), flat(gx=b, gy=y, grp=c)) for a, b in odd for y in range(mesh.shape["gy"]) for c in (0, 1)
    ] + [
        (flat(gx=g, gy=y, grp=a), flat(gx=g, gy=y, grp=b))
        for g in (0, gx - 1)
        for y in range(mesh.shape["gy"])
        for a, b in ends
    ]

    def send_in(message):
        return lax.ppermute(message, "gx", even)

    def send_out(message):
        return lax.ppermute(message, mesh.axis_names, hops)

    def send_sides(ymsg, zmsg):
        return lax.ppermute(ymsg, "gy", swap), lax.ppermute(zmsg, "grp", swap)

    def body(les_velocity, mean_mach, transfer_tiles, intersection_offset, acoustic_state):
        X2, Y, _, Z = les_velocity.shape
        X = acoustic_state.shape[0]
        T = Z // LANES
        blocks, plane = transfer_tiles.shape[0], transfer_tiles.shape[-1]
        wide = plane // Y
        v = les_velocity.transpose(0, 2, 1, 3)
        state = acoustic_state.transpose(2, 0, 1, 3)
        rate_z, smooth_z = (
            jnp.asarray(np.stack([banded(Z, weights, sign, h) for h in (0, 1)]))
            for weights, sign in ((deriv, -1), ([-filter_weight * w for w in taps[1:]], 1))
        )
        mach = jnp.broadcast_to(mean_mach[:, :, None], (X, Y, LANES))

        grid = (4, T, X, Y, LANES)
        source = (3, T, X, Y, LANES)
        near, far = (12 * T, Y, LANES), (4 * T * (wide - 3), Y, LANES)
        term = (3 * T * wide, Y, LANES)
        edge_y, edge_yy = (T * X, 8, LANES), (2 * T * X, 8, LANES)
        edge_z, edge_zz = (2 * X, Y, LANES), (4 * X, Y, LANES)
        les_x, les_y, les_z = (3 * T, Y, LANES), (3 * T * X2 // 8, 8, LANES), (3 * X2, Y, LANES)
        both_y, both_z = [(a[0] + b[0], *a[1:]) for a, b in ((edge_y, les_y), (edge_z, les_z))]
        F = pltpu.VMEM((4, T, X + 6, Y + 16, LANES), jnp.float32)
        G2 = pltpu.VMEM((2, T, X, Y, LANES), jnp.float32)
        G4 = pltpu.VMEM((4, T, X, Y, LANES), jnp.float32)
        les_scratch = [
            pltpu.VMEM((3, T, X2 + 2, Y + 16, LANES), jnp.float32),
            pltpu.VMEM((blocks // 2, 4 * plane, 3 * Z), jnp.bfloat16),
            pltpu.VMEM((3, T, X + 2 * wide, Y, LANES), jnp.float32),
            pltpu.SMEM((blocks,), jnp.int32),
            pltpu.SemaphoreType.DMA(()),
        ]
        def complete(part, halos, shared, scale, next_y, next_z, halo_base=0):
            smooth = not shared
            shapes = [near, near] if smooth else [near, far, near, far]
            sides = [edge_y, edge_z] if next_y == RATE_Y else [edge_yy, edge_zz]
            *done, ymsg, zmsg = call(
                functools.partial(
                    edge_body, smooth=smooth, scale=scale, ycomps=next_y, zcomps=next_z, halo_base=halo_base
                ),
                [*shapes, *sides],
                [part, *halos, *([shared[0], *shared[1]] if shared else [])],
            )
            nears, fars = (done, []) if smooth else (done[::2], done[1::2])
            return [part, *nears], fars, send_sides(ymsg, zmsg), (send_in(nears[0]), send_out(nears[1]))

        v_in, v_out, *sides = call(pack_les_body, [les_x, les_x, les_y, les_z], [v])
        les_edges = [send_in(v_in), send_out(v_out), *send_sides(*sides)]
        tiles = transfer_tiles[:, 0]
        at = term[0] + 3 * T
        joint = (at + near[0], Y, LANES)
        v1, S, *own, state, ym, zm = call(
            functools.partial(les_body, base=0, ybase=0, zbase=0, advance=True),
            [(3, T, X2, Y, LANES), source, joint, joint, grid, both_y, both_z],
            [intersection_offset, v, *les_edges, tiles, state],
            les_scratch,
            away=1,
            flops=4000000,
        )
        terms = (send_in(own[0]), send_out(own[1]))
        sides = send_sides(ym, zm)
        les_edges = [*terms, *sides]
        near_in, near_out = own
        halos = terms
        whole = [state, near_in, near_out]
        for step in range(STEPS):
            if step:
                whole[1], terms = lax.optimization_barrier((whole[1], terms))
            part, base = call(
                functools.partial(first_main, near_base=at if step == 0 else 0), [grid, grid], [*whole, *sides, rate_z, mach, S], [F, G2], flops=4000000
            )
            whole, fars, sides, halos = complete(
                part, halos, (mach, terms), wave_step, RATE_Y, RATE_Z, at if step == 0 else 0
            )
            if step + 1 < STEPS:
                S2, *terms2 = call(
                    functools.partial(les_body, base=term[0], ybase=edge_y[0], zbase=edge_z[0], advance=False),
                    [source, term, term],
                    [intersection_offset, v1, *les_edges, tiles],
                    les_scratch,
                    away=1,
                    flops=4000000,
                )
                whole[1], S2, *terms2 = lax.optimization_barrier((whole[1], S2, *terms2))
                terms2 = (send_in(terms2[0]), send_out(terms2[1]))
            (part,) = call(
                second_main, [grid], [*whole, *fars, *sides, rate_z, mach, S, base], [F, G2], flops=4000000
            )
            whole, fars, sides, halos = complete(part, halos, (mach, terms), 0.5 * wave_step, ALL, ALL)
            if step + 1 < STEPS:
                terms, S = terms2, S2
                (part,) = call(
                    functools.partial(smooth_main, last=False),
                    [grid],
                    [*whole, *fars, *sides, smooth_z],
                    [F, G4],
                    flops=4000000,
                )
                whole, _, sides, halos = complete(part, halos, None, 0.0, RATE_Y, RATE_Z)
        (part,) = call(
            functools.partial(smooth_main, last=True),
            [(4, X, Y, Z)],
            [*whole, *fars, *sides, smooth_z],
            [F, G4],
            flops=4000000,
        )
        (state,) = call(last_body, [(4, X, Y, Z)], [part, *halos], alias={0: 0})
        return state.transpose(1, 2, 0, 3)

    placed = (
        P("gx", "gy", None, "grp"),
        P("gx", "gy"),
        P("gx", "gy", None, None, None),
        P("gx"),
        P("gx", "gy", None, "grp"),
    )
    return jax.shard_map(body, mesh=mesh, in_specs=placed, out_specs=P("gx", "gy", None, "grp"), check_vma=False)
```

```python
import functools

import jax
import jax.numpy as jnp
import numpy as np
from jax import lax
from jax.experimental import pallas as pl
from jax.experimental.pallas import tpu as pltpu
from jax.sharding import PartitionSpec as P

STEPS = 2
eddy_step = 0.1
viscosity = 0.5
wave_step = 0.2
filter_weight = 0.2
deriv = (0.770882380518, -0.166705904415, 0.02084314277)
taps = (0.28739284246, -0.226146951809, 0.10630357877, -0.023853048191)

RATE_Y, RATE_Z = (0, 2), (0, 3)
ALL = (0, 1, 2, 3)
LANES = 128
VMEM = pl.BlockSpec(memory_space=pltpu.VMEM)
ANY = pl.BlockSpec(memory_space=pl.ANY)


def place():
    column = lax.axis_index("gx")
    inside = (column > 0) & (column < lax.axis_size("gx") - 1)
    return lax.rem(column, 2), lax.axis_index("gy"), lax.axis_index("grp"), inside.astype(jnp.int32)


def call(body, outs, ins, scratch=(), away=0, flops=1000000):
    shapes = [jax.ShapeDtypeStruct(s, jnp.float32) for s in outs]
    size = sum(o.size for o in shapes) + sum(i.size for i in ins)
    return pl.pallas_call(
        lambda *refs: body(place(), *refs),
        out_shape=shapes,
        in_specs=[ANY] * away + [VMEM] * (len(ins) - away),
        out_specs=[VMEM] * len(shapes),
        scratch_shapes=list(scratch),
        compiler_params=pltpu.CompilerParams(vmem_limit_bytes=12 * 1024 * 1024),
        cost_estimate=pl.CostEstimate(flops=flops, bytes_accessed=4 * size, transcendentals=0),
    )(*ins)


def banded(depth, weights, sign, half):
    matrix = np.zeros((depth + LANES, depth), np.float32)
    lane = np.arange(depth)
    for j, weight in enumerate(weights, 1):
        for to, factor in ((lane + j, weight), (lane - j, sign * weight)):
            ok = (to >= 0) & (to < depth)
            matrix[to[ok], lane[ok]] = factor
            beyond = to >= depth if half == 0 else to < 0
            matrix[depth + to[beyond] % LANES, lane[beyond]] = factor
    high = matrix.astype(jnp.bfloat16)
    low = (matrix - high.astype(np.float32)).astype(jnp.bfloat16)
    return np.concatenate([high, high, low])


def z_product(F, zmsg, zmat, comps, G, half):
    _, T, X, Y, _ = F.shape
    X, Y = X - 6, Y - 16
    for n, c in enumerate(comps):
        tiles = [F[c, t, 3 : 3 + X, 8 : 8 + Y, :].reshape(X * Y, LANES) for t in range(T)]
        tiles.append(zmsg[n * X : (n + 1) * X].reshape(X * Y, LANES))
        high = [tile.astype(jnp.bfloat16) for tile in tiles]
        low = [(tile - top.astype(jnp.float32)).astype(jnp.bfloat16) for tile, top in zip(tiles, high)]
        out = jnp.dot(jnp.concatenate(high + low + high, axis=1), zmat[half], preferred_element_type=jnp.float32)
        for t in range(T):
            G[n, t] = out[:, t * LANES : (t + 1) * LANES].reshape(X, Y, LANES)


def shift_tiles(tiles, left, right, by, lanes):
    out = []
    row = [left] + tiles + [right]
    for at in range(1, len(tiles) + 1):
        if by > 0:
            mixed = jnp.where(lanes < by, row[at + 1], row[at])
            out.append(pltpu.roll(mixed, LANES - by, 1))
        else:
            mixed = jnp.where(lanes >= LANES + by, row[at - 1], row[at])
            out.append(pltpu.roll(mixed, -by, 1))
    return out


def side_tiles(tile, half):
    zero = jnp.zeros_like(tile)
    return jnp.where(half == 1, tile, zero), jnp.where(half == 0, tile, zero)


def known(value, has):
    return jnp.where(has == 1, value, jnp.zeros_like(value))


def lane_ids(rows):
    return lax.broadcasted_iota(jnp.int32, (rows, LANES), 1)


def ends(info, inner, X, deep):
    high = (info[0] == 0) if inner else (info[0] == 1)
    has = jnp.int32(1) if inner else info[3]
    return high, has, lambda d: jnp.where(high, X - 1 - d, d), lambda d: jnp.where(high, 2 - d, d)


def pack_sides(info, get, ymsg, zmsg, ycomps, zcomps, X, Y, T, layers):
    row, half = info[1], info[2]
    rows = lax.broadcasted_iota(jnp.int32, (8, LANES), 0)
    ys = pl.multiple_of(jnp.where(row == 0, Y - 8, 0), 8)
    turn = jnp.where(row == 0, 4, 0)
    edge = jnp.where(half == 0, T - 1, 0)

    def one(i):
        for n in range(len(ycomps) // 2):
            for t in range(T):
                first = pltpu.roll(get(ycomps[2 * n], t, i, pl.ds(ys, 8)), turn, 0)
                second = pltpu.roll(get(ycomps[2 * n + 1], t, i, pl.ds(ys, 8)), 4 - turn, 0)
                ymsg[(n * T + t) * X + i] = jnp.where(rows < 4, first, second)
        for n, c in enumerate(zcomps):
            zmsg[n * X + i] = get(c, edge, i, slice(None))

    if layers is None:
        lax.fori_loop(0, X, lambda i, carry: (one(i), carry)[1], 0, unroll=4)
    else:
        for i in layers:
            one(i)


def fill(F, f, nears, fars, ymsg, ycomps, info):
    row = info[1]
    _, T, X, Y, _ = f.shape
    y = slice(8, 8 + Y)

    def step(i, carry):
        for t in range(T):
            for c in range(4):
                F[c, t, i + 3, y, :] = f[c, t, i]
            for n, c in enumerate(ycomps):
                tile = ymsg[(n // 2 * T + t) * X + i]
                turned = pltpu.roll(tile, 4, 0)
                if n % 2:
                    tile, turned = turned, tile
                zero = jnp.zeros_like(tile)
                F[c, t, i + 3, 0:8, :] = jnp.where(row == 1, turned, zero)
                F[c, t, i + 3, 8 + Y : 16 + Y, :] = jnp.where(row == 0, tile, zero)
        return carry

    lax.fori_loop(0, X, step, 0, unroll=4)
    zero = jnp.zeros((Y, LANES), jnp.float32)
    for side, near in enumerate(nears):
        high, _, layer, place = ends(info, side == 0, X, 3)
        for c in range(4):
            for t in range(T):
                for d in range(3):
                    F[c, t, 3 + layer(d), y, :] = near[3 * (c * T + t) + place(d)]
                    F[c, t, jnp.where(high, X + 3 + d, 2 - d), y, :] = zero
                if fars:
                    far = fars[side]
                    count = far.shape[0] // (4 * T)
                    for d in range(count):
                        F[c, t, 3 + layer(3 + d), y, :] = far[count * (c * T + t) + d]


def dx(F, c, t, i, Y):
    y = slice(8, 8 + Y)
    return sum(deriv[j - 1] * (F[c, t, i + 3 + j, y, :] - F[c, t, i + 3 - j, y, :]) for j in (1, 2, 3))


def dy(F, c, t, i, Y):
    return sum(
        deriv[j - 1] * (F[c, t, i + 3, 8 + j : 8 + Y + j, :] - F[c, t, i + 3, 8 - j : 8 + Y - j, :]) for j in (1, 2, 3)
    )


def rate_loop(F, G, mach, S, emit):
    T, X, Y = F.shape[1], F.shape[2] - 6, F.shape[3] - 16

    def step(i, carry):
        m = mach[i]
        for t in range(T):
            gp, gu, gv, gw = (dx(F, c, t, i, Y) for c in range(4))
            emit(0, t, i, -(m * gp + gu + dy(F, 2, t, i, Y) + G[1, t, i]))
            emit(1, t, i, -(m * gu + gp) - S[0, t, i])
            emit(2, t, i, -(m * gv + dy(F, 0, t, i, Y)) - S[1, t, i])
            emit(3, t, i, -(m * gw + G[0, t, i]) - S[2, t, i])
        return carry

    lax.fori_loop(0, X, step, 0, unroll=4)


def first_main(info, f, near_in, near_out, ymsg, zmsg, zmat, mach, S, o, base, F, G, *, near_base):
    Y = f.shape[3]
    fill(F, f, (near_in.at[near_base:], near_out.at[near_base:]), (), ymsg, RATE_Y, info)
    z_product(F, zmsg, zmat, RATE_Z, G, info[2])

    def emit(c, t, i, value):
        center = F[c, t, i + 3, 8 : 8 + Y, :]
        base[c, t, i] = center
        o[c, t, i] = center + wave_step * value

    rate_loop(F, G, mach, S, emit)


def second_main(info, f, near_in, near_out, far_in, far_out, ymsg, zmsg, zmat, mach, S, base, o, F, G):
    Y = f.shape[3]
    fill(F, f, (near_in, near_out), (far_in, far_out), ymsg, RATE_Y, info)
    z_product(F, zmsg, zmat, RATE_Z, G, info[2])

    def emit(c, t, i, value):
        o[c, t, i] = 0.5 * (base[c, t, i] + F[c, t, i + 3, 8 : 8 + Y, :]) + (0.5 * wave_step) * value

    rate_loop(F, G, mach, S, emit)


def smooth_main(info, f, near_in, near_out, far_in, far_out, ymsg, zmsg, zmat, o, F, G, *, last):
    _, T, X, Y, _ = f.shape
    fill(F, f, (near_in, near_out), (far_in, far_out), ymsg, ALL, info)
    z_product(F, zmsg, zmat, ALL, G, info[2])
    y = slice(8, 8 + Y)

    def step(i, carry):
        for c in range(4):
            for t in range(T):
                total = (1.0 - 3.0 * filter_weight * taps[0]) * F[c, t, i + 3, y, :] + G[c, t, i]
                for j in (1, 2, 3):
                    beside = (F[c, t, i + 3 + j, y, :] + F[c, t, i + 3 - j, y, :]) + (
                        F[c, t, i + 3, 8 + j : 8 + Y + j, :] + F[c, t, i + 3, 8 - j : 8 + Y - j, :]
                    )
                    total = total - (filter_weight * taps[j]) * beside
                if last:
                    o[c, i, :, t * LANES : (t + 1) * LANES] = total
                else:
                    o[c, t, i] = total
        return carry

    lax.fori_loop(0, X, step, 0, unroll=4)


def last_body(info, f, halo_in, halo_out, o):
    _, X, Y, Z = f.shape
    T = Z // LANES

    def copy(i, carry):
        for c in range(4):
            o[c, i] = f[c, i]
        return carry

    lax.fori_loop(0, X, copy, 0, unroll=4)
    for side, halo in enumerate((halo_in, halo_out)):
        _, has, layer, place = ends(info, side == 0, X, 3)
        weight = filter_weight * has.astype(jnp.float32)
        for c in range(4):
            for t in range(T):
                lane = slice(t * LANES, (t + 1) * LANES)
                beyond = [halo[3 * (c * T + t) + place(2 - e)] for e in range(3)]
                for d in range(3):
                    part = sum(taps[1 + d + e] * beyond[e] for e in range(3 - d))
                    o[c, layer(d), :, lane] = f[c, layer(d), :, lane] - weight * part


def edge_body(info, f, halo_in, halo_out, *rest, smooth, scale, ycomps, zcomps, halo_base):
    rest = list(rest)
    mach, *terms = (None, None, None) if smooth else [rest.pop(0) for _ in range(3)]
    *done, ymsg, zmsg = rest
    sides = [done[:1], done[1:]] if smooth else [done[:2], done[2:]]
    _, T, X, Y, _ = f.shape
    deep = 3 if smooth else 3 + sides[0][1].shape[0] // (4 * T)
    for side, halo in enumerate((halo_in.at[halo_base:], halo_out.at[halo_base:])):
        near = sides[side][0]
        high, has, layer, place = ends(info, side == 0, X, deep)
        sign = (jnp.where(high, scale, -scale) * has).astype(jnp.float32)
        weight = has.astype(jnp.float32)
        for t in range(T):
            for d in range(deep):
                at = layer(d)
                values = [f[c, t, at] for c in range(4)]
                if d < 3:
                    beyond = [[halo[3 * (c * T + t) + place(2 - e)] for e in range(3 - d)] for c in range(4)]
                    coefs = taps[1:] if smooth else deriv
                    parts = [sum(coefs[d + e] * value for e, value in enumerate(column)) for column in beyond]
                    if smooth:
                        values = [value - (filter_weight * weight) * part for value, part in zip(values, parts)]
                    else:
                        m, (gp, gu, gv, gw) = mach[at], parts
                        change = (m * gp + gu, m * gu + gp, m * gv, m * gw)
                        values = [value - sign * part for value, part in zip(values, change)]
                if not smooth:
                    index = jnp.where(high, deep - 1 - d, d)
                    for c in range(3):
                        term = terms[side][(c * T + t) * deep + index]
                        values[1 + c] = values[1 + c] - (scale * weight) * term
                for c in range(4):
                    if d < 3:
                        near[3 * (c * T + t) + place(d)] = values[c]
                    else:
                        sides[side][1][(deep - 3) * (c * T + t) + d - 3] = values[c]
    pack_sides(info, lambda c, t, i, rows: f[c, t, i, rows, :], ymsg, zmsg, ycomps, zcomps, X, Y, T, None)
    for side, (near, *far) in enumerate(sides):
        _, _, layer, place = ends(info, side == 0, X, deep)
        for d in range(deep):

            def get(c, t, i, rows):
                if d < 3:
                    return near[3 * (c * T + t) + place(d), rows, :]
                return far[0][(deep - 3) * (c * T + t) + d - 3, rows, :]

            pack_sides(info, get, ymsg, zmsg, ycomps, zcomps, X, Y, T, [layer(d)])


def pack_whole(info, f, o, near_in, near_out, start, ymsg, zmsg):
    _, T, X, Y, _ = o.shape

    def step(i, carry):
        for c in range(4):
            for t in range(T):
                o[c, t, i] = f[c, i, :, t * LANES : (t + 1) * LANES]
        return carry

    lax.fori_loop(0, X, step, 0, unroll=4)
    for side, near in enumerate((near_in, near_out)):
        _, _, layer, place = ends(info, side == 0, X, 3)
        for c in range(4):
            for t in range(T):
                for d in range(3):
                    near[start + 3 * (c * T + t) + place(d)] = o[c, t, layer(d)]
    pack_sides(info, lambda c, t, i, rows: o[c, t, i, rows, :], ymsg, zmsg, RATE_Y, RATE_Z, X, Y, T, None)


def pack_les(get, shape, inner, outer, ymsg, zmsg, info, base=0, ybase=0, zbase=0):
    pos, row, half = info[0], info[1], info[2]
    _, T, X, Y, _ = shape
    si = jnp.where(pos == 0, X - 1, 0)
    so = jnp.where(pos == 0, 0, X - 1)
    rows = lax.broadcasted_iota(jnp.int32, (8, LANES), 0)
    ys = pl.multiple_of(jnp.where(row == 0, Y - 8, 0), 8)
    turn = [jnp.where(row == 0, (r + 1) % 8, r) for r in range(8)]
    for c in range(3):
        for t in range(T):
            inner[base + c * T + t] = get(c, t, si, slice(None))
            outer[base + c * T + t] = get(c, t, so, slice(None))
            for n in range(X // 8):
                acc = jnp.zeros((8, LANES), jnp.float32)
                for r in range(8):
                    tile = get(c, t, 8 * n + r, pl.ds(ys, 8))
                    acc = jnp.where(rows == r, pltpu.roll(tile, turn[r], 0), acc)
                ymsg[ybase + (c * T + t) * (X // 8) + n] = acc

    def step(i, carry):
        for c in range(3):
            last, first = get(c, T - 1, i, slice(None)), get(c, 0, i, slice(None))
            zmsg[zbase + c * X + i] = jnp.where(half == 0, last, first)
        return carry

    lax.fori_loop(0, X, step, 0, unroll=4)


def getter(v):
    if len(v.shape) == 4:
        return lambda c, t, i, rows: v[i, c, rows, t * LANES : (t + 1) * LANES]
    return lambda c, t, i, rows: v[c, t, i, rows, :]


def pack_les_body(info, v, inner, outer, ymsg, zmsg):
    X, _, Y, Z = v.shape
    pack_les(getter(v), (3, Z // LANES, X, Y, LANES), inner, outer, ymsg, zmsg, info)


def les_body(info, offsets, v, inner, outer, ymsg, zmsg, tiles, *rest, base, ybase, zbase, advance):
    if advance:
        state, v1, own, n_in, n_out, f, ny, nz, V, LB, ACC, offset, sem = rest
    else:
        own, n_in, n_out, V, LB, ACC, offset, sem = rest
    copy_in = pltpu.make_async_copy(offsets, offset, sem)
    copy_in.start()
    pos, row, half = info[0], info[1], info[2]
    _, T, X, Y, _ = V.shape
    X, Y = X - 2, Y - 16
    get = getter(v)
    blocks = 2 * LB.shape[0]
    wide = X // blocks
    plane = wide * Y
    hi = jnp.where(pos == 0, X + 1, 0)
    ho = jnp.where(pos == 0, 0, X + 1)
    for c in range(3):
        for t in range(T):
            V[c, t, hi, 8 : 8 + Y, :] = inner[base + c * T + t]
            V[c, t, ho, 8 : 8 + Y, :] = known(outer[base + c * T + t], info[3])
            for n in range(X // 8):
                tile = ymsg[ybase + (c * T + t) * (X // 8) + n]
                zero = jnp.zeros_like(tile)
                for r in range(8):
                    low = pltpu.roll(tile, 7 - r, 0) if r < 7 else tile
                    high = pltpu.roll(tile, 8 - r, 0) if r else tile
                    V[c, t, 8 * n + r + 1, 0:8, :] = jnp.where(row == 1, low, zero)
                    V[c, t, 8 * n + r + 1, 8 + Y : 16 + Y, :] = jnp.where(row == 0, high, zero)

    def copy(i, carry):
        for c in range(3):
            for t in range(T):
                V[c, t, i + 1, 8 : 8 + Y, :] = get(c, t, i, slice(None))
        return carry

    lax.fori_loop(0, X, copy, 0, unroll=4)
    ACC[...] = jnp.zeros_like(ACC)
    lanes = lane_ids(Y)
    y = slice(8, 8 + Y)

    def step(i, carry):
        center = [[V[c, t, i + 1, y, :] for t in range(T)] for c in range(3)]
        ahead, behind = [], []
        for c in range(3 if advance else 2):
            left, right = side_tiles(zmsg[zbase + c * X + i], half)
            ahead.append(shift_tiles(center[c], left, right, 1, lanes))
            behind.append(shift_tiles(center[c], left, right, -1, lanes))
        at = lax.rem(i, 2 * wide) * Y
        at = at + jnp.where(at >= plane, plane, 0)
        b = i // (2 * wide)
        for t in range(T):
            xa = [V[c, t, i + 2, y, :] for c in range(3)]
            xb = [V[c, t, i, y, :] for c in range(3)]
            ya = [V[c, t, i + 1, 9 : 9 + Y, :] for c in range(3)]
            yb = [V[c, t, i + 1, 7 : 7 + Y, :] for c in range(3)]
            u, w, q = center[0][t], center[1][t], center[2][t]
            vx = 0.5 * ((ya[2] - yb[2]) - (ahead[1][t] - behind[1][t]))
            vy = 0.5 * ((ahead[0][t] - behind[0][t]) - (xa[2] - xb[2]))
            vz = 0.5 * ((xa[1] - xb[1]) - (ya[0] - yb[0]))
            lamb = [vy * q - vz * w, vz * u - vx * q, vx * w - vy * u]
            for c in range(3):
                high = lamb[c].astype(jnp.bfloat16)
                low = (lamb[c] - high.astype(jnp.float32)).astype(jnp.bfloat16)
                lane = slice((c * T + t) * LANES, (c * T + t + 1) * LANES)
                LB[b, pl.ds(pl.multiple_of(at, 16), Y), lane] = high
                LB[b, pl.ds(pl.multiple_of(plane + at, 16), Y), lane] = low
                if advance:
                    laplace = -6.0 * center[c][t] + ((xa[c] + xb[c]) + (ya[c] + yb[c]) + (ahead[c][t] + behind[c][t]))
                    v1[c, t, i] = center[c][t] + eddy_step * (viscosity * laplace - lamb[c])
        return carry

    lax.fori_loop(0, X, step, 0, unroll=4)

    copy_in.wait()
    for m in range(blocks // 2):
        a, b = [[tiles[2 * m + n, k] for k in (0, 1)] for n in (0, 1)]
        parts = [
            (jnp.concatenate([a[0], a[0], b[0], b[0]]), LB[m]),
            (jnp.concatenate([a[1], a[1]]), LB[m, : 2 * plane]),
            (jnp.concatenate([b[1], b[1]]), LB[m, 2 * plane :]),
        ]
        out = [
            lax.dot_general(w, x, (((0,), (0,)), ((), ())), preferred_element_type=jnp.float32) for w, x in parts
        ]
        at = (m + 1) * wide
        places = [at, at + offset[2 * m] * wide, at + offset[2 * m + 1] * wide]
        for c in range(3):
            for t in range(T):
                lane = slice((c * T + t) * LANES, (c * T + t + 1) * LANES)
                for to, value in zip(places, out):
                    for l in range(wide):
                        ACC[c, t, to + l] = ACC[c, t, to + l] + value[l * Y : (l + 1) * Y, lane]

    depth = own.shape[2]
    own[...] = ACC[:, :, wide : wide + depth]
    ti = jnp.where(pos == 0, depth + wide, 0)
    to = jnp.where(pos == 0, 0, depth + wide)
    for c in range(3):
        for t in range(T):
            for l in range(wide):
                n_in[(c * T + t) * wide + l] = ACC[c, t, ti + l]
                n_out[(c * T + t) * wide + l] = ACC[c, t, to + l]
    if advance:
        pack_whole(info, state, f, n_in, n_out, 3 * T * (wide + 1), ny, nz)
        pack_les(getter(v1), v1.shape, n_in, n_out, ny, nz, info, 3 * T * wide, T * f.shape[2], 2 * f.shape[2])


def solution(mesh):
    gx = mesh.shape["gx"]
    swap = [(0, 1), (1, 0)]
    even = [pair for k in range(gx // 2) for pair in ((2 * k, 2 * k + 1), (2 * k + 1, 2 * k))]
    odd = [pair for k in range(gx // 2 - 1) for pair in ((2 * k + 1, 2 * k + 2), (2 * k + 2, 2 * k + 1))]

    def flat(**at):
        index = 0
        for axis in mesh.axis_names:
            index = index * mesh.shape[axis] + at[axis]
        return index

    ends = [(0, 1), (1, 0)]
    hops = [
        (flat(gx=a, gy=y, grp=c), flat(gx=b, gy=y, grp=c)) for a, b in odd for y in range(mesh.shape["gy"]) for c in (0, 1)
    ] + [
        (flat(gx=g, gy=y, grp=a), flat(gx=g, gy=y, grp=b))
        for g in (0, gx - 1)
        for y in range(mesh.shape["gy"])
        for a, b in ends
    ]

    def send_in(message):
        return lax.ppermute(message, "gx", even)

    def send_out(message):
        return lax.ppermute(message, mesh.axis_names, hops)

    def send_sides(ymsg, zmsg):
        return lax.ppermute(ymsg, "gy", swap), lax.ppermute(zmsg, "grp", swap)

    def body(les_velocity, mean_mach, transfer_tiles, intersection_offset, acoustic_state):
        X2, Y, _, Z = les_velocity.shape
        X = acoustic_state.shape[0]
        T = Z // LANES
        blocks, plane = transfer_tiles.shape[0], transfer_tiles.shape[-1]
        wide = plane // Y
        v = les_velocity.transpose(0, 2, 1, 3)
        state = acoustic_state.transpose(2, 0, 1, 3)
        rate_z, smooth_z = (
            jnp.asarray(np.stack([banded(Z, weights, sign, h) for h in (0, 1)]))
            for weights, sign in ((deriv, -1), ([-filter_weight * w for w in taps[1:]], 1))
        )
        mach = jnp.broadcast_to(mean_mach[:, :, None], (X, Y, LANES))

        grid = (4, T, X, Y, LANES)
        source = (3, T, X, Y, LANES)
        near, far = (12 * T, Y, LANES), (4 * T * (wide - 3), Y, LANES)
        term = (3 * T * wide, Y, LANES)
        edge_y, edge_yy = (T * X, 8, LANES), (2 * T * X, 8, LANES)
        edge_z, edge_zz = (2 * X, Y, LANES), (4 * X, Y, LANES)
        les_x, les_y, les_z = (3 * T, Y, LANES), (3 * T * X2 // 8, 8, LANES), (3 * X2, Y, LANES)
        both_y, both_z = [(a[0] + b[0], *a[1:]) for a, b in ((edge_y, les_y), (edge_z, les_z))]
        F = pltpu.VMEM((4, T, X + 6, Y + 16, LANES), jnp.float32)
        G2 = pltpu.VMEM((2, T, X, Y, LANES), jnp.float32)
        G4 = pltpu.VMEM((4, T, X, Y, LANES), jnp.float32)
        les_scratch = [
            pltpu.VMEM((3, T, X2 + 2, Y + 16, LANES), jnp.float32),
            pltpu.VMEM((blocks // 2, 4 * plane, 3 * Z), jnp.bfloat16),
            pltpu.VMEM((3, T, X + 2 * wide, Y, LANES), jnp.float32),
            pltpu.SMEM((blocks,), jnp.int32),
            pltpu.SemaphoreType.DMA(()),
        ]
        def complete(part, halos, shared, scale, next_y, next_z, halo_base=0):
            smooth = not shared
            shapes = [near, near] if smooth else [near, far, near, far]
            sides = [edge_y, edge_z] if next_y == RATE_Y else [edge_yy, edge_zz]
            *done, ymsg, zmsg = call(
                functools.partial(
                    edge_body, smooth=smooth, scale=scale, ycomps=next_y, zcomps=next_z, halo_base=halo_base
                ),
                [*shapes, *sides],
                [part, *halos, *([shared[0], *shared[1]] if shared else [])],
            )
            nears, fars = (done, []) if smooth else (done[::2], done[1::2])
            return [part, *nears], fars, send_sides(ymsg, zmsg), (send_in(nears[0]), send_out(nears[1]))

        v_in, v_out, *sides = call(pack_les_body, [les_x, les_x, les_y, les_z], [v])
        les_edges = [send_in(v_in), send_out(v_out), *send_sides(*sides)]
        tiles = transfer_tiles[:, 0]
        at = term[0] + 3 * T
        joint = (at + near[0], Y, LANES)
        v1, S, *own, state, ym, zm = call(
            functools.partial(les_body, base=0, ybase=0, zbase=0, advance=True),
            [(3, T, X2, Y, LANES), source, joint, joint, grid, both_y, both_z],
            [intersection_offset, v, *les_edges, tiles, state],
            les_scratch,
            away=1,
            flops=4000000,
        )
        terms = (send_in(own[0]), send_out(own[1]))
        sides = send_sides(ym, zm)
        les_edges = [*terms, *sides]
        near_in, near_out = own
        halos = terms
        whole = [state, near_in, near_out]
        for step in range(STEPS):
            if step:
                whole[1], terms = lax.optimization_barrier((whole[1], terms))
            part, base = call(
                functools.partial(first_main, near_base=at if step == 0 else 0), [grid, grid], [*whole, *sides, rate_z, mach, S], [F, G2], flops=4000000
            )
            whole, fars, sides, halos = complete(
                part, halos, (mach, terms), wave_step, RATE_Y, RATE_Z, at if step == 0 else 0
            )
            if step + 1 < STEPS:
                S2, *terms2 = call(
                    functools.partial(les_body, base=term[0], ybase=edge_y[0], zbase=edge_z[0], advance=False),
                    [source, term, term],
                    [intersection_offset, v1, *les_edges, tiles],
                    les_scratch,
                    away=1,
                    flops=4000000,
                )
                whole[1], S2, *terms2 = lax.optimization_barrier((whole[1], S2, *terms2))
                terms2 = (send_in(terms2[0]), send_out(terms2[1]))
            (part,) = call(
                second_main, [grid], [*whole, *fars, *sides, rate_z, mach, S, base], [F, G2], flops=4000000
            )
            whole, fars, sides, halos = complete(part, halos, (mach, terms), 0.5 * wave_step, ALL, ALL)
            if step + 1 < STEPS:
                terms, S = terms2, S2
                (part,) = call(
                    functools.partial(smooth_main, last=False),
                    [grid],
                    [*whole, *fars, *sides, smooth_z],
                    [F, G4],
                    flops=4000000,
                )
                whole, _, sides, halos = complete(part, halos, None, 0.0, RATE_Y, RATE_Z)
        (part,) = call(
            functools.partial(smooth_main, last=True),
            [(4, X, Y, Z)],
            [*whole, *fars, *sides, smooth_z],
            [F, G4],
            flops=4000000,
        )
        (state,) = call(last_body, [(4, X, Y, Z)], [part, *halos])
        return state.transpose(1, 2, 0, 3)

    placed = (
        P("gx", "gy", None, "grp"),
        P("gx", "gy"),
        P("gx", "gy", None, None, None),
        P("gx"),
        P("gx", "gy", None, "grp"),
    )
    return jax.shard_map(body, mesh=mesh, in_specs=placed, out_specs=P("gx", "gy", None, "grp"), check_vma=False)
```

```python
import functools

import jax
import jax.numpy as jnp
import numpy as np
from jax import lax
from jax.experimental import pallas as pl
from jax.experimental.pallas import tpu as pltpu
from jax.sharding import PartitionSpec as P

STEPS = 2
eddy_step = 0.1
viscosity = 0.5
wave_step = 0.2
filter_weight = 0.2
deriv = (0.770882380518, -0.166705904415, 0.02084314277)
taps = (0.28739284246, -0.226146951809, 0.10630357877, -0.023853048191)

RATE_Y, RATE_Z = (0, 2), (0, 3)
ALL = (0, 1, 2, 3)
LANES = 128
VMEM = pl.BlockSpec(memory_space=pltpu.VMEM)
ANY = pl.BlockSpec(memory_space=pl.ANY)


def place():
    column = lax.axis_index("gx")
    inside = (column > 0) & (column < lax.axis_size("gx") - 1)
    return lax.rem(column, 2), lax.axis_index("gy"), lax.axis_index("grp"), inside.astype(jnp.int32)


def call(body, outs, ins, scratch=(), away=0, flops=1000000):
    shapes = [jax.ShapeDtypeStruct(s, jnp.float32) for s in outs]
    size = sum(o.size for o in shapes) + sum(i.size for i in ins)
    return pl.pallas_call(
        lambda *refs: body(place(), *refs),
        out_shape=shapes,
        in_specs=[ANY] * away + [VMEM] * (len(ins) - away),
        out_specs=[VMEM] * len(shapes),
        scratch_shapes=list(scratch),
        compiler_params=pltpu.CompilerParams(vmem_limit_bytes=12 * 1024 * 1024),
        cost_estimate=pl.CostEstimate(flops=flops, bytes_accessed=4 * size, transcendentals=0),
    )(*ins)


def banded(depth, weights, sign, half):
    matrix = np.zeros((depth + LANES, depth), np.float32)
    lane = np.arange(depth)
    for j, weight in enumerate(weights, 1):
        for to, factor in ((lane + j, weight), (lane - j, sign * weight)):
            ok = (to >= 0) & (to < depth)
            matrix[to[ok], lane[ok]] = factor
            beyond = to >= depth if half == 0 else to < 0
            matrix[depth + to[beyond] % LANES, lane[beyond]] = factor
    high = matrix.astype(jnp.bfloat16)
    low = (matrix - high.astype(np.float32)).astype(jnp.bfloat16)
    return np.concatenate([high, high, low])


def z_product(F, zmsg, zmat, comps, G, half):
    _, T, X, Y, _ = F.shape
    X, Y = X - 6, Y - 16
    for n, c in enumerate(comps):
        tiles = [F[c, t, 3 : 3 + X, 8 : 8 + Y, :].reshape(X * Y, LANES) for t in range(T)]
        tiles.append(zmsg[n * X : (n + 1) * X].reshape(X * Y, LANES))
        high = [tile.astype(jnp.bfloat16) for tile in tiles]
        low = [(tile - top.astype(jnp.float32)).astype(jnp.bfloat16) for tile, top in zip(tiles, high)]
        out = jnp.dot(jnp.concatenate(high + low + high, axis=1), zmat[half], preferred_element_type=jnp.float32)
        for t in range(T):
            G[n, t] = out[:, t * LANES : (t + 1) * LANES].reshape(X, Y, LANES)


def shift_tiles(tiles, left, right, by, lanes):
    out = []
    row = [left] + tiles + [right]
    for at in range(1, len(tiles) + 1):
        if by > 0:
            mixed = jnp.where(lanes < by, row[at + 1], row[at])
            out.append(pltpu.roll(mixed, LANES - by, 1))
        else:
            mixed = jnp.where(lanes >= LANES + by, row[at - 1], row[at])
            out.append(pltpu.roll(mixed, -by, 1))
    return out


def side_tiles(tile, half):
    zero = jnp.zeros_like(tile)
    return jnp.where(half == 1, tile, zero), jnp.where(half == 0, tile, zero)


def known(value, has):
    return jnp.where(has == 1, value, jnp.zeros_like(value))


def lane_ids(rows):
    return lax.broadcasted_iota(jnp.int32, (rows, LANES), 1)


def ends(info, inner, X, deep):
    high = (info[0] == 0) if inner else (info[0] == 1)
    has = jnp.int32(1) if inner else info[3]
    return high, has, lambda d: jnp.where(high, X - 1 - d, d), lambda d: jnp.where(high, 2 - d, d)


def pack_sides(info, get, ymsg, zmsg, ycomps, zcomps, X, Y, T, layers):
    row, half = info[1], info[2]
    rows = lax.broadcasted_iota(jnp.int32, (8, LANES), 0)
    ys = pl.multiple_of(jnp.where(row == 0, Y - 8, 0), 8)
    turn = jnp.where(row == 0, 4, 0)
    edge = jnp.where(half == 0, T - 1, 0)

    def one(i):
        for n in range(len(ycomps) // 2):
            for t in range(T):
                first = pltpu.roll(get(ycomps[2 * n], t, i, pl.ds(ys, 8)), turn, 0)
                second = pltpu.roll(get(ycomps[2 * n + 1], t, i, pl.ds(ys, 8)), 4 - turn, 0)
                ymsg[(n * T + t) * X + i] = jnp.where(rows < 4, first, second)
        for n, c in enumerate(zcomps):
            zmsg[n * X + i] = get(c, edge, i, slice(None))

    if layers is None:
        lax.fori_loop(0, X, lambda i, carry: (one(i), carry)[1], 0, unroll=16)
    else:
        for i in layers:
            one(i)


def fill(F, f, nears, fars, ymsg, ycomps, info):
    row = info[1]
    _, T, X, Y, _ = f.shape
    y = slice(8, 8 + Y)

    def step(i, carry):
        for t in range(T):
            for c in range(4):
                F[c, t, i + 3, y, :] = f[c, t, i]
            for n, c in enumerate(ycomps):
                tile = ymsg[(n // 2 * T + t) * X + i]
                turned = pltpu.roll(tile, 4, 0)
                if n % 2:
                    tile, turned = turned, tile
                zero = jnp.zeros_like(tile)
                F[c, t, i + 3, 0:8, :] = jnp.where(row == 1, turned, zero)
                F[c, t, i + 3, 8 + Y : 16 + Y, :] = jnp.where(row == 0, tile, zero)
        return carry

    lax.fori_loop(0, X, step, 0, unroll=16)
    zero = jnp.zeros((Y, LANES), jnp.float32)
    for side, near in enumerate(nears):
        high, _, layer, place = ends(info, side == 0, X, 3)
        for c in range(4):
            for t in range(T):
                for d in range(3):
                    F[c, t, 3 + layer(d), y, :] = near[3 * (c * T + t) + place(d)]
                    F[c, t, jnp.where(high, X + 3 + d, 2 - d), y, :] = zero
                if fars:
                    far = fars[side]
                    count = far.shape[0] // (4 * T)
                    for d in range(count):
                        F[c, t, 3 + layer(3 + d), y, :] = far[count * (c * T + t) + d]


def dx(F, c, t, i, Y):
    y = slice(8, 8 + Y)
    return sum(deriv[j - 1] * (F[c, t, i + 3 + j, y, :] - F[c, t, i + 3 - j, y, :]) for j in (1, 2, 3))


def dy(F, c, t, i, Y):
    return sum(
        deriv[j - 1] * (F[c, t, i + 3, 8 + j : 8 + Y + j, :] - F[c, t, i + 3, 8 - j : 8 + Y - j, :]) for j in (1, 2, 3)
    )


def rate_loop(F, G, mach, S, emit):
    T, X, Y = F.shape[1], F.shape[2] - 6, F.shape[3] - 16

    def step(i, carry):
        m = mach[i]
        for t in range(T):
            gp, gu, gv, gw = (dx(F, c, t, i, Y) for c in range(4))
            emit(0, t, i, -(m * gp + gu + dy(F, 2, t, i, Y) + G[1, t, i]))
            emit(1, t, i, -(m * gu + gp) - S[0, t, i])
            emit(2, t, i, -(m * gv + dy(F, 0, t, i, Y)) - S[1, t, i])
            emit(3, t, i, -(m * gw + G[0, t, i]) - S[2, t, i])
        return carry

    lax.fori_loop(0, X, step, 0, unroll=16)


def first_main(info, f, near_in, near_out, ymsg, zmsg, zmat, mach, S, o, base, F, G, *, near_base):
    Y = f.shape[3]
    fill(F, f, (near_in.at[near_base:], near_out.at[near_base:]), (), ymsg, RATE_Y, info)
    z_product(F, zmsg, zmat, RATE_Z, G, info[2])

    def emit(c, t, i, value):
        center = F[c, t, i + 3, 8 : 8 + Y, :]
        base[c, t, i] = center
        o[c, t, i] = center + wave_step * value

    rate_loop(F, G, mach, S, emit)


def second_main(info, f, near_in, near_out, far_in, far_out, ymsg, zmsg, zmat, mach, S, base, o, F, G):
    Y = f.shape[3]
    fill(F, f, (near_in, near_out), (far_in, far_out), ymsg, RATE_Y, info)
    z_product(F, zmsg, zmat, RATE_Z, G, info[2])

    def emit(c, t, i, value):
        o[c, t, i] = 0.5 * (base[c, t, i] + F[c, t, i + 3, 8 : 8 + Y, :]) + (0.5 * wave_step) * value

    rate_loop(F, G, mach, S, emit)


def smooth_main(info, f, near_in, near_out, far_in, far_out, ymsg, zmsg, zmat, o, F, G, *, last):
    _, T, X, Y, _ = f.shape
    fill(F, f, (near_in, near_out), (far_in, far_out), ymsg, ALL, info)
    z_product(F, zmsg, zmat, ALL, G, info[2])
    y = slice(8, 8 + Y)

    def step(i, carry):
        for c in range(4):
            for t in range(T):
                total = (1.0 - 3.0 * filter_weight * taps[0]) * F[c, t, i + 3, y, :] + G[c, t, i]
                for j in (1, 2, 3):
                    beside = (F[c, t, i + 3 + j, y, :] + F[c, t, i + 3 - j, y, :]) + (
                        F[c, t, i + 3, 8 + j : 8 + Y + j, :] + F[c, t, i + 3, 8 - j : 8 + Y - j, :]
                    )
                    total = total - (filter_weight * taps[j]) * beside
                if last:
                    o[c, i, :, t * LANES : (t + 1) * LANES] = total
                else:
                    o[c, t, i] = total
        return carry

    lax.fori_loop(0, X, step, 0, unroll=16)


def last_body(info, f, halo_in, halo_out, o):
    _, X, Y, Z = f.shape
    T = Z // LANES

    def copy(i, carry):
        for c in range(4):
            o[c, i] = f[c, i]
        return carry

    lax.fori_loop(0, X, copy, 0, unroll=16)
    for side, halo in enumerate((halo_in, halo_out)):
        _, has, layer, place = ends(info, side == 0, X, 3)
        weight = filter_weight * has.astype(jnp.float32)
        for c in range(4):
            for t in range(T):
                lane = slice(t * LANES, (t + 1) * LANES)
                beyond = [halo[3 * (c * T + t) + place(2 - e)] for e in range(3)]
                for d in range(3):
                    part = sum(taps[1 + d + e] * beyond[e] for e in range(3 - d))
                    o[c, layer(d), :, lane] = f[c, layer(d), :, lane] - weight * part


def edge_body(info, f, halo_in, halo_out, *rest, smooth, scale, ycomps, zcomps, halo_base):
    rest = list(rest)
    mach, *terms = (None, None, None) if smooth else [rest.pop(0) for _ in range(3)]
    *done, ymsg, zmsg = rest
    sides = [done[:1], done[1:]] if smooth else [done[:2], done[2:]]
    _, T, X, Y, _ = f.shape
    deep = 3 if smooth else 3 + sides[0][1].shape[0] // (4 * T)
    for side, halo in enumerate((halo_in.at[halo_base:], halo_out.at[halo_base:])):
        near = sides[side][0]
        high, has, layer, place = ends(info, side == 0, X, deep)
        sign = (jnp.where(high, scale, -scale) * has).astype(jnp.float32)
        weight = has.astype(jnp.float32)
        for t in range(T):
            for d in range(deep):
                at = layer(d)
                values = [f[c, t, at] for c in range(4)]
                if d < 3:
                    beyond = [[halo[3 * (c * T + t) + place(2 - e)] for e in range(3 - d)] for c in range(4)]
                    coefs = taps[1:] if smooth else deriv
                    parts = [sum(coefs[d + e] * value for e, value in enumerate(column)) for column in beyond]
                    if smooth:
                        values = [value - (filter_weight * weight) * part for value, part in zip(values, parts)]
                    else:
                        m, (gp, gu, gv, gw) = mach[at], parts
                        change = (m * gp + gu, m * gu + gp, m * gv, m * gw)
                        values = [value - sign * part for value, part in zip(values, change)]
                if not smooth:
                    index = jnp.where(high, deep - 1 - d, d)
                    for c in range(3):
                        term = terms[side][(c * T + t) * deep + index]
                        values[1 + c] = values[1 + c] - (scale * weight) * term
                for c in range(4):
                    if d < 3:
                        near[3 * (c * T + t) + place(d)] = values[c]
                    else:
                        sides[side][1][(deep - 3) * (c * T + t) + d - 3] = values[c]
    pack_sides(info, lambda c, t, i, rows: f[c, t, i, rows, :], ymsg, zmsg, ycomps, zcomps, X, Y, T, None)
    for side, (near, *far) in enumerate(sides):
        _, _, layer, place = ends(info, side == 0, X, deep)
        for d in range(deep):

            def get(c, t, i, rows):
                if d < 3:
                    return near[3 * (c * T + t) + place(d), rows, :]
                return far[0][(deep - 3) * (c * T + t) + d - 3, rows, :]

            pack_sides(info, get, ymsg, zmsg, ycomps, zcomps, X, Y, T, [layer(d)])


def pack_whole(info, f, o, near_in, near_out, start, ymsg, zmsg):
    _, T, X, Y, _ = o.shape

    def step(i, carry):
        for c in range(4):
            for t in range(T):
                o[c, t, i] = f[c, i, :, t * LANES : (t + 1) * LANES]
        return carry

    lax.fori_loop(0, X, step, 0, unroll=16)
    for side, near in enumerate((near_in, near_out)):
        _, _, layer, place = ends(info, side == 0, X, 3)
        for c in range(4):
            for t in range(T):
                for d in range(3):
                    near[start + 3 * (c * T + t) + place(d)] = o[c, t, layer(d)]
    pack_sides(info, lambda c, t, i, rows: o[c, t, i, rows, :], ymsg, zmsg, RATE_Y, RATE_Z, X, Y, T, None)


def pack_les(get, shape, inner, outer, ymsg, zmsg, info, base=0, ybase=0, zbase=0):
    pos, row, half = info[0], info[1], info[2]
    _, T, X, Y, _ = shape
    si = jnp.where(pos == 0, X - 1, 0)
    so = jnp.where(pos == 0, 0, X - 1)
    rows = lax.broadcasted_iota(jnp.int32, (8, LANES), 0)
    ys = pl.multiple_of(jnp.where(row == 0, Y - 8, 0), 8)
    turn = [jnp.where(row == 0, (r + 1) % 8, r) for r in range(8)]
    for c in range(3):
        for t in range(T):
            inner[base + c * T + t] = get(c, t, si, slice(None))
            outer[base + c * T + t] = get(c, t, so, slice(None))
            for n in range(X // 8):
                acc = jnp.zeros((8, LANES), jnp.float32)
                for r in range(8):
                    tile = get(c, t, 8 * n + r, pl.ds(ys, 8))
                    acc = jnp.where(rows == r, pltpu.roll(tile, turn[r], 0), acc)
                ymsg[ybase + (c * T + t) * (X // 8) + n] = acc

    def step(i, carry):
        for c in range(3):
            last, first = get(c, T - 1, i, slice(None)), get(c, 0, i, slice(None))
            zmsg[zbase + c * X + i] = jnp.where(half == 0, last, first)
        return carry

    lax.fori_loop(0, X, step, 0, unroll=16)


def getter(v):
    if len(v.shape) == 4:
        return lambda c, t, i, rows: v[i, c, rows, t * LANES : (t + 1) * LANES]
    return lambda c, t, i, rows: v[c, t, i, rows, :]


def pack_les_body(info, v, inner, outer, ymsg, zmsg):
    X, _, Y, Z = v.shape
    pack_les(getter(v), (3, Z // LANES, X, Y, LANES), inner, outer, ymsg, zmsg, info)


def les_body(info, offsets, v, inner, outer, ymsg, zmsg, tiles, *rest, base, ybase, zbase, advance):
    if advance:
        state, v1, own, n_in, n_out, f, ny, nz, V, LB, ACC, offset, sem = rest
    else:
        own, n_in, n_out, V, LB, ACC, offset, sem = rest
    copy_in = pltpu.make_async_copy(offsets, offset, sem)
    copy_in.start()
    pos, row, half = info[0], info[1], info[2]
    _, T, X, Y, _ = V.shape
    X, Y = X - 2, Y - 16
    get = getter(v)
    blocks = 2 * LB.shape[0]
    wide = X // blocks
    plane = wide * Y
    hi = jnp.where(pos == 0, X + 1, 0)
    ho = jnp.where(pos == 0, 0, X + 1)
    for c in range(3):
        for t in range(T):
            V[c, t, hi, 8 : 8 + Y, :] = inner[base + c * T + t]
            V[c, t, ho, 8 : 8 + Y, :] = known(outer[base + c * T + t], info[3])
            for n in range(X // 8):
                tile = ymsg[ybase + (c * T + t) * (X // 8) + n]
                zero = jnp.zeros_like(tile)
                for r in range(8):
                    low = pltpu.roll(tile, 7 - r, 0) if r < 7 else tile
                    high = pltpu.roll(tile, 8 - r, 0) if r else tile
                    V[c, t, 8 * n + r + 1, 0:8, :] = jnp.where(row == 1, low, zero)
                    V[c, t, 8 * n + r + 1, 8 + Y : 16 + Y, :] = jnp.where(row == 0, high, zero)

    def copy(i, carry):
        for c in range(3):
            for t in range(T):
                V[c, t, i + 1, 8 : 8 + Y, :] = get(c, t, i, slice(None))
        return carry

    lax.fori_loop(0, X, copy, 0, unroll=16)
    ACC[...] = jnp.zeros_like(ACC)
    lanes = lane_ids(Y)
    y = slice(8, 8 + Y)

    def step(i, carry):
        center = [[V[c, t, i + 1, y, :] for t in range(T)] for c in range(3)]
        ahead, behind = [], []
        for c in range(3 if advance else 2):
            left, right = side_tiles(zmsg[zbase + c * X + i], half)
            ahead.append(shift_tiles(center[c], left, right, 1, lanes))
            behind.append(shift_tiles(center[c], left, right, -1, lanes))
        at = lax.rem(i, 2 * wide) * Y
        at = at + jnp.where(at >= plane, plane, 0)
        b = i // (2 * wide)
        for t in range(T):
            xa = [V[c, t, i + 2, y, :] for c in range(3)]
            xb = [V[c, t, i, y, :] for c in range(3)]
            ya = [V[c, t, i + 1, 9 : 9 + Y, :] for c in range(3)]
            yb = [V[c, t, i + 1, 7 : 7 + Y, :] for c in range(3)]
            u, w, q = center[0][t], center[1][t], center[2][t]
            vx = 0.5 * ((ya[2] - yb[2]) - (ahead[1][t] - behind[1][t]))
            vy = 0.5 * ((ahead[0][t] - behind[0][t]) - (xa[2] - xb[2]))
            vz = 0.5 * ((xa[1] - xb[1]) - (ya[0] - yb[0]))
            lamb = [vy * q - vz * w, vz * u - vx * q, vx * w - vy * u]
            for c in range(3):
                high = lamb[c].astype(jnp.bfloat16)
                low = (lamb[c] - high.astype(jnp.float32)).astype(jnp.bfloat16)
                lane = slice((c * T + t) * LANES, (c * T + t + 1) * LANES)
                LB[b, pl.ds(pl.multiple_of(at, 16), Y), lane] = high
                LB[b, pl.ds(pl.multiple_of(plane + at, 16), Y), lane] = low
                if advance:
                    laplace = -6.0 * center[c][t] + ((xa[c] + xb[c]) + (ya[c] + yb[c]) + (ahead[c][t] + behind[c][t]))
                    v1[c, t, i] = center[c][t] + eddy_step * (viscosity * laplace - lamb[c])
        return carry

    lax.fori_loop(0, X, step, 0, unroll=16)

    copy_in.wait()
    for m in range(blocks // 2):
        a, b = [[tiles[2 * m + n, k] for k in (0, 1)] for n in (0, 1)]
        parts = [
            (jnp.concatenate([a[0], a[0], b[0], b[0]]), LB[m]),
            (jnp.concatenate([a[1], a[1]]), LB[m, : 2 * plane]),
            (jnp.concatenate([b[1], b[1]]), LB[m, 2 * plane :]),
        ]
        out = [
            lax.dot_general(w, x, (((0,), (0,)), ((), ())), preferred_element_type=jnp.float32) for w, x in parts
        ]
        at = (m + 1) * wide
        places = [at, at + offset[2 * m] * wide, at + offset[2 * m + 1] * wide]
        for c in range(3):
            for t in range(T):
                lane = slice((c * T + t) * LANES, (c * T + t + 1) * LANES)
                for to, value in zip(places, out):
                    for l in range(wide):
                        ACC[c, t, to + l] = ACC[c, t, to + l] + value[l * Y : (l + 1) * Y, lane]

    depth = own.shape[2]
    own[...] = ACC[:, :, wide : wide + depth]
    ti = jnp.where(pos == 0, depth + wide, 0)
    to = jnp.where(pos == 0, 0, depth + wide)
    for c in range(3):
        for t in range(T):
            for l in range(wide):
                n_in[(c * T + t) * wide + l] = ACC[c, t, ti + l]
                n_out[(c * T + t) * wide + l] = ACC[c, t, to + l]
    if advance:
        pack_whole(info, state, f, n_in, n_out, 3 * T * (wide + 1), ny, nz)
        pack_les(getter(v1), v1.shape, n_in, n_out, ny, nz, info, 3 * T * wide, T * f.shape[2], 2 * f.shape[2])


def solution(mesh):
    gx = mesh.shape["gx"]
    swap = [(0, 1), (1, 0)]
    even = [pair for k in range(gx // 2) for pair in ((2 * k, 2 * k + 1), (2 * k + 1, 2 * k))]
    odd = [pair for k in range(gx // 2 - 1) for pair in ((2 * k + 1, 2 * k + 2), (2 * k + 2, 2 * k + 1))]

    def flat(**at):
        index = 0
        for axis in mesh.axis_names:
            index = index * mesh.shape[axis] + at[axis]
        return index

    ends = [(0, 1), (1, 0)]
    hops = [
        (flat(gx=a, gy=y, grp=c), flat(gx=b, gy=y, grp=c)) for a, b in odd for y in range(mesh.shape["gy"]) for c in (0, 1)
    ] + [
        (flat(gx=g, gy=y, grp=a), flat(gx=g, gy=y, grp=b))
        for g in (0, gx - 1)
        for y in range(mesh.shape["gy"])
        for a, b in ends
    ]

    def send_in(message):
        return lax.ppermute(message, "gx", even)

    def send_out(message):
        return lax.ppermute(message, mesh.axis_names, hops)

    def send_sides(ymsg, zmsg):
        return lax.ppermute(ymsg, "gy", swap), lax.ppermute(zmsg, "grp", swap)

    def body(les_velocity, mean_mach, transfer_tiles, intersection_offset, acoustic_state):
        X2, Y, _, Z = les_velocity.shape
        X = acoustic_state.shape[0]
        T = Z // LANES
        blocks, plane = transfer_tiles.shape[0], transfer_tiles.shape[-1]
        wide = plane // Y
        v = les_velocity.transpose(0, 2, 1, 3)
        state = acoustic_state.transpose(2, 0, 1, 3)
        rate_z, smooth_z = (
            jnp.asarray(np.stack([banded(Z, weights, sign, h) for h in (0, 1)]))
            for weights, sign in ((deriv, -1), ([-filter_weight * w for w in taps[1:]], 1))
        )
        mach = jnp.broadcast_to(mean_mach[:, :, None], (X, Y, LANES))

        grid = (4, T, X, Y, LANES)
        source = (3, T, X, Y, LANES)
        near, far = (12 * T, Y, LANES), (4 * T * (wide - 3), Y, LANES)
        term = (3 * T * wide, Y, LANES)
        edge_y, edge_yy = (T * X, 8, LANES), (2 * T * X, 8, LANES)
        edge_z, edge_zz = (2 * X, Y, LANES), (4 * X, Y, LANES)
        les_x, les_y, les_z = (3 * T, Y, LANES), (3 * T * X2 // 8, 8, LANES), (3 * X2, Y, LANES)
        both_y, both_z = [(a[0] + b[0], *a[1:]) for a, b in ((edge_y, les_y), (edge_z, les_z))]
        F = pltpu.VMEM((4, T, X + 6, Y + 16, LANES), jnp.float32)
        G2 = pltpu.VMEM((2, T, X, Y, LANES), jnp.float32)
        G4 = pltpu.VMEM((4, T, X, Y, LANES), jnp.float32)
        les_scratch = [
            pltpu.VMEM((3, T, X2 + 2, Y + 16, LANES), jnp.float32),
            pltpu.VMEM((blocks // 2, 4 * plane, 3 * Z), jnp.bfloat16),
            pltpu.VMEM((3, T, X + 2 * wide, Y, LANES), jnp.float32),
            pltpu.SMEM((blocks,), jnp.int32),
            pltpu.SemaphoreType.DMA(()),
        ]
        def complete(part, halos, shared, scale, next_y, next_z, halo_base=0):
            smooth = not shared
            shapes = [near, near] if smooth else [near, far, near, far]
            sides = [edge_y, edge_z] if next_y == RATE_Y else [edge_yy, edge_zz]
            *done, ymsg, zmsg = call(
                functools.partial(
                    edge_body, smooth=smooth, scale=scale, ycomps=next_y, zcomps=next_z, halo_base=halo_base
                ),
                [*shapes, *sides],
                [part, *halos, *([shared[0], *shared[1]] if shared else [])],
            )
            nears, fars = (done, []) if smooth else (done[::2], done[1::2])
            return [part, *nears], fars, send_sides(ymsg, zmsg), (send_in(nears[0]), send_out(nears[1]))

        v_in, v_out, *sides = call(pack_les_body, [les_x, les_x, les_y, les_z], [v])
        les_edges = [send_in(v_in), send_out(v_out), *send_sides(*sides)]
        tiles = transfer_tiles[:, 0]
        at = term[0] + 3 * T
        joint = (at + near[0], Y, LANES)
        v1, S, *own, state, ym, zm = call(
            functools.partial(les_body, base=0, ybase=0, zbase=0, advance=True),
            [(3, T, X2, Y, LANES), source, joint, joint, grid, both_y, both_z],
            [intersection_offset, v, *les_edges, tiles, state],
            les_scratch,
            away=1,
            flops=4000000,
        )
        terms = (send_in(own[0]), send_out(own[1]))
        sides = send_sides(ym, zm)
        les_edges = [*terms, *sides]
        near_in, near_out = own
        halos = terms
        whole = [state, near_in, near_out]
        for step in range(STEPS):
            if step:
                whole[1], terms = lax.optimization_barrier((whole[1], terms))
            part, base = call(
                functools.partial(first_main, near_base=at if step == 0 else 0), [grid, grid], [*whole, *sides, rate_z, mach, S], [F, G2], flops=4000000
            )
            whole, fars, sides, halos = complete(
                part, halos, (mach, terms), wave_step, RATE_Y, RATE_Z, at if step == 0 else 0
            )
            if step + 1 < STEPS:
                S2, *terms2 = call(
                    functools.partial(les_body, base=term[0], ybase=edge_y[0], zbase=edge_z[0], advance=False),
                    [source, term, term],
                    [intersection_offset, v1, *les_edges, tiles],
                    les_scratch,
                    away=1,
                    flops=4000000,
                )
                whole[1], S2, *terms2 = lax.optimization_barrier((whole[1], S2, *terms2))
                terms2 = (send_in(terms2[0]), send_out(terms2[1]))
            (part,) = call(
                second_main, [grid], [*whole, *fars, *sides, rate_z, mach, S, base], [F, G2], flops=4000000
            )
            whole, fars, sides, halos = complete(part, halos, (mach, terms), 0.5 * wave_step, ALL, ALL)
            if step + 1 < STEPS:
                terms, S = terms2, S2
                (part,) = call(
                    functools.partial(smooth_main, last=False),
                    [grid],
                    [*whole, *fars, *sides, smooth_z],
                    [F, G4],
                    flops=4000000,
                )
                whole, _, sides, halos = complete(part, halos, None, 0.0, RATE_Y, RATE_Z)
        (part,) = call(
            functools.partial(smooth_main, last=True),
            [(4, X, Y, Z)],
            [*whole, *fars, *sides, smooth_z],
            [F, G4],
            flops=4000000,
        )
        (state,) = call(last_body, [(4, X, Y, Z)], [part, *halos])
        return state.transpose(1, 2, 0, 3)

    placed = (
        P("gx", "gy", None, "grp"),
        P("gx", "gy"),
        P("gx", "gy", None, None, None),
        P("gx"),
        P("gx", "gy", None, "grp"),
    )
    return jax.shard_map(body, mesh=mesh, in_specs=placed, out_specs=P("gx", "gy", None, "grp"), check_vma=False)
```

```python
import functools

import jax
import jax.numpy as jnp
import numpy as np
from jax import lax
from jax.experimental import pallas as pl
from jax.experimental.pallas import tpu as pltpu
from jax.sharding import PartitionSpec as P

STEPS = 2
eddy_step = 0.1
viscosity = 0.5
wave_step = 0.2
filter_weight = 0.2
deriv = (0.770882380518, -0.166705904415, 0.02084314277)
taps = (0.28739284246, -0.226146951809, 0.10630357877, -0.023853048191)

RATE_Y, RATE_Z = (0, 2), (0, 3)
ALL = (0, 1, 2, 3)
LANES = 128
VMEM = pl.BlockSpec(memory_space=pltpu.VMEM)
ANY = pl.BlockSpec(memory_space=pl.ANY)


def place():
    column = lax.axis_index("gx")
    inside = (column > 0) & (column < lax.axis_size("gx") - 1)
    return lax.rem(column, 2), lax.axis_index("gy"), lax.axis_index("grp"), inside.astype(jnp.int32)


def call(body, outs, ins, scratch=(), away=0, flops=1000000):
    shapes = [jax.ShapeDtypeStruct(s, jnp.float32) for s in outs]
    size = sum(o.size for o in shapes) + sum(i.size for i in ins)
    return pl.pallas_call(
        lambda *refs: body(place(), *refs),
        out_shape=shapes,
        in_specs=[ANY] * away + [VMEM] * (len(ins) - away),
        out_specs=[VMEM] * len(shapes),
        scratch_shapes=list(scratch),
        compiler_params=pltpu.CompilerParams(vmem_limit_bytes=12 * 1024 * 1024),
        cost_estimate=pl.CostEstimate(flops=flops, bytes_accessed=4 * size, transcendentals=0),
    )(*ins)


def banded(depth, weights, sign, half):
    matrix = np.zeros((depth + LANES, depth), np.float32)
    lane = np.arange(depth)
    for j, weight in enumerate(weights, 1):
        for to, factor in ((lane + j, weight), (lane - j, sign * weight)):
            ok = (to >= 0) & (to < depth)
            matrix[to[ok], lane[ok]] = factor
            beyond = to >= depth if half == 0 else to < 0
            matrix[depth + to[beyond] % LANES, lane[beyond]] = factor
    high = matrix.astype(jnp.bfloat16)
    low = (matrix - high.astype(np.float32)).astype(jnp.bfloat16)
    return np.concatenate([high, high, low])


def z_product(F, zmsg, zmat, comps, G, half):
    _, T, X, Y, _ = F.shape
    X, Y = X - 6, Y - 16
    for n, c in enumerate(comps):
        tiles = [F[c, t, 3 : 3 + X, 8 : 8 + Y, :].reshape(X * Y, LANES) for t in range(T)]
        tiles.append(zmsg[n * X : (n + 1) * X].reshape(X * Y, LANES))
        high = [tile.astype(jnp.bfloat16) for tile in tiles]
        low = [(tile - top.astype(jnp.float32)).astype(jnp.bfloat16) for tile, top in zip(tiles, high)]
        out = jnp.dot(jnp.concatenate(high + low + high, axis=1), zmat[half], preferred_element_type=jnp.float32)
        for t in range(T):
            G[n, t] = out[:, t * LANES : (t + 1) * LANES].reshape(X, Y, LANES)


def shift_tiles(tiles, left, right, by, lanes):
    out = []
    row = [left] + tiles + [right]
    for at in range(1, len(tiles) + 1):
        if by > 0:
            mixed = jnp.where(lanes < by, row[at + 1], row[at])
            out.append(pltpu.roll(mixed, LANES - by, 1))
        else:
            mixed = jnp.where(lanes >= LANES + by, row[at - 1], row[at])
            out.append(pltpu.roll(mixed, -by, 1))
    return out


def side_tiles(tile, half):
    zero = jnp.zeros_like(tile)
    return jnp.where(half == 1, tile, zero), jnp.where(half == 0, tile, zero)


def known(value, has):
    return jnp.where(has == 1, value, jnp.zeros_like(value))


def lane_ids(rows):
    return lax.broadcasted_iota(jnp.int32, (rows, LANES), 1)


def ends(info, inner, X, deep):
    high = (info[0] == 0) if inner else (info[0] == 1)
    has = jnp.int32(1) if inner else info[3]
    return high, has, lambda d: jnp.where(high, X - 1 - d, d), lambda d: jnp.where(high, 2 - d, d)


def pack_sides(info, get, ymsg, zmsg, ycomps, zcomps, X, Y, T, layers):
    row, half = info[1], info[2]
    rows = lax.broadcasted_iota(jnp.int32, (8, LANES), 0)
    ys = pl.multiple_of(jnp.where(row == 0, Y - 8, 0), 8)
    turn = jnp.where(row == 0, 4, 0)
    edge = jnp.where(half == 0, T - 1, 0)

    def one(i):
        for n in range(len(ycomps) // 2):
            for t in range(T):
                first = pltpu.roll(get(ycomps[2 * n], t, i, pl.ds(ys, 8)), turn, 0)
                second = pltpu.roll(get(ycomps[2 * n + 1], t, i, pl.ds(ys, 8)), 4 - turn, 0)
                ymsg[(n * T + t) * X + i] = jnp.where(rows < 4, first, second)
        for n, c in enumerate(zcomps):
            zmsg[n * X + i] = get(c, edge, i, slice(None))

    if layers is None:
        lax.fori_loop(0, X, lambda i, carry: (one(i), carry)[1], 0, unroll=16)
    else:
        for i in layers:
            one(i)


def fill(F, f, nears, fars, ymsg, ycomps, info):
    row = info[1]
    _, T, X, Y, _ = f.shape
    y = slice(8, 8 + Y)

    def step(i, carry):
        for t in range(T):
            for c in range(4):
                F[c, t, i + 3, y, :] = f[c, t, i]
            for n, c in enumerate(ycomps):
                tile = ymsg[(n // 2 * T + t) * X + i]
                turned = pltpu.roll(tile, 4, 0)
                if n % 2:
                    tile, turned = turned, tile
                zero = jnp.zeros_like(tile)
                F[c, t, i + 3, 0:8, :] = jnp.where(row == 1, turned, zero)
                F[c, t, i + 3, 8 + Y : 16 + Y, :] = jnp.where(row == 0, tile, zero)
        return carry

    lax.fori_loop(0, X, step, 0, unroll=16)
    zero = jnp.zeros((Y, LANES), jnp.float32)
    for side, near in enumerate(nears):
        high, _, layer, place = ends(info, side == 0, X, 3)
        for c in range(4):
            for t in range(T):
                for d in range(3):
                    F[c, t, 3 + layer(d), y, :] = near[3 * (c * T + t) + place(d)]
                    F[c, t, jnp.where(high, X + 3 + d, 2 - d), y, :] = zero
                if fars:
                    far = fars[side]
                    count = far.shape[0] // (4 * T)
                    for d in range(count):
                        F[c, t, 3 + layer(3 + d), y, :] = far[count * (c * T + t) + d]


def dx(F, c, t, i, Y):
    y = slice(8, 8 + Y)
    return sum(deriv[j - 1] * (F[c, t, i + 3 + j, y, :] - F[c, t, i + 3 - j, y, :]) for j in (1, 2, 3))


def dy(F, c, t, i, Y):
    return sum(
        deriv[j - 1] * (F[c, t, i + 3, 8 + j : 8 + Y + j, :] - F[c, t, i + 3, 8 - j : 8 + Y - j, :]) for j in (1, 2, 3)
    )


def rate_loop(F, G, mach, S, emit):
    T, X, Y = F.shape[1], F.shape[2] - 6, F.shape[3] - 16

    def step(i, carry):
        m = mach[i]
        for t in range(T):
            gp, gu, gv, gw = (dx(F, c, t, i, Y) for c in range(4))
            emit(0, t, i, -(m * gp + gu + dy(F, 2, t, i, Y) + G[1, t, i]))
            emit(1, t, i, -(m * gu + gp) - S[0, t, i])
            emit(2, t, i, -(m * gv + dy(F, 0, t, i, Y)) - S[1, t, i])
            emit(3, t, i, -(m * gw + G[0, t, i]) - S[2, t, i])
        return carry

    lax.fori_loop(0, X, step, 0, unroll=16)


def first_main(info, f, near_in, near_out, ymsg, zmsg, zmat, mach, S, o, base, F, G, *, near_base):
    Y = f.shape[3]
    fill(F, f, (near_in.at[near_base:], near_out.at[near_base:]), (), ymsg, RATE_Y, info)
    z_product(F, zmsg, zmat, RATE_Z, G, info[2])

    def emit(c, t, i, value):
        center = F[c, t, i + 3, 8 : 8 + Y, :]
        base[c, t, i] = center
        o[c, t, i] = center + wave_step * value

    rate_loop(F, G, mach, S, emit)


def second_main(info, f, near_in, near_out, far_in, far_out, ymsg, zmsg, zmat, mach, S, base, o, F, G):
    Y = f.shape[3]
    fill(F, f, (near_in, near_out), (far_in, far_out), ymsg, RATE_Y, info)
    z_product(F, zmsg, zmat, RATE_Z, G, info[2])

    def emit(c, t, i, value):
        o[c, t, i] = 0.5 * (base[c, t, i] + F[c, t, i + 3, 8 : 8 + Y, :]) + (0.5 * wave_step) * value

    rate_loop(F, G, mach, S, emit)


def smooth_main(info, f, near_in, near_out, far_in, far_out, ymsg, zmsg, zmat, o, F, G, *, last):
    _, T, X, Y, _ = f.shape
    fill(F, f, (near_in, near_out), (far_in, far_out), ymsg, ALL, info)
    z_product(F, zmsg, zmat, ALL, G, info[2])
    y = slice(8, 8 + Y)

    def step(i, carry):
        for c in range(4):
            for t in range(T):
                total = (1.0 - 3.0 * filter_weight * taps[0]) * F[c, t, i + 3, y, :] + G[c, t, i]
                for j in (1, 2, 3):
                    beside = (F[c, t, i + 3 + j, y, :] + F[c, t, i + 3 - j, y, :]) + (
                        F[c, t, i + 3, 8 + j : 8 + Y + j, :] + F[c, t, i + 3, 8 - j : 8 + Y - j, :]
                    )
                    total = total - (filter_weight * taps[j]) * beside
                if last:
                    o[c, i, :, t * LANES : (t + 1) * LANES] = total
                else:
                    o[c, t, i] = total
        return carry

    lax.fori_loop(0, X, step, 0, unroll=16)


def last_body(info, f, halo_in, halo_out, o):
    _, X, Y, Z = f.shape
    T = Z // LANES

    def copy(i, carry):
        for c in range(4):
            o[c, i] = f[c, i]
        return carry

    lax.fori_loop(0, X, copy, 0, unroll=16)
    for side, halo in enumerate((halo_in, halo_out)):
        _, has, layer, place = ends(info, side == 0, X, 3)
        weight = filter_weight * has.astype(jnp.float32)
        for c in range(4):
            for t in range(T):
                lane = slice(t * LANES, (t + 1) * LANES)
                beyond = [halo[3 * (c * T + t) + place(2 - e)] for e in range(3)]
                for d in range(3):
                    part = sum(taps[1 + d + e] * beyond[e] for e in range(3 - d))
                    o[c, layer(d), :, lane] = f[c, layer(d), :, lane] - weight * part


def edge_body(info, f, halo_in, halo_out, *rest, smooth, scale, ycomps, zcomps, halo_base):
    rest = list(rest)
    mach, *terms = (None, None, None) if smooth else [rest.pop(0) for _ in range(3)]
    *done, ymsg, zmsg = rest
    sides = [done[:1], done[1:]] if smooth else [done[:2], done[2:]]
    _, T, X, Y, _ = f.shape
    deep = 3 if smooth else 3 + sides[0][1].shape[0] // (4 * T)
    for side, halo in enumerate((halo_in.at[halo_base:], halo_out.at[halo_base:])):
        near = sides[side][0]
        high, has, layer, place = ends(info, side == 0, X, deep)
        sign = (jnp.where(high, scale, -scale) * has).astype(jnp.float32)
        weight = has.astype(jnp.float32)
        for t in range(T):
            for d in range(deep):
                at = layer(d)
                values = [f[c, t, at] for c in range(4)]
                if d < 3:
                    beyond = [[halo[3 * (c * T + t) + place(2 - e)] for e in range(3 - d)] for c in range(4)]
                    coefs = taps[1:] if smooth else deriv
                    parts = [sum(coefs[d + e] * value for e, value in enumerate(column)) for column in beyond]
                    if smooth:
                        values = [value - (filter_weight * weight) * part for value, part in zip(values, parts)]
                    else:
                        m, (gp, gu, gv, gw) = mach[at], parts
                        change = (m * gp + gu, m * gu + gp, m * gv, m * gw)
                        values = [value - sign * part for value, part in zip(values, change)]
                if not smooth:
                    index = jnp.where(high, deep - 1 - d, d)
                    for c in range(3):
                        term = terms[side][(c * T + t) * deep + index]
                        values[1 + c] = values[1 + c] - (scale * weight) * term
                for c in range(4):
                    if d < 3:
                        near[3 * (c * T + t) + place(d)] = values[c]
                    else:
                        sides[side][1][(deep - 3) * (c * T + t) + d - 3] = values[c]
    pack_sides(info, lambda c, t, i, rows: f[c, t, i, rows, :], ymsg, zmsg, ycomps, zcomps, X, Y, T, None)
    for side, (near, *far) in enumerate(sides):
        _, _, layer, place = ends(info, side == 0, X, deep)
        for d in range(deep):

            def get(c, t, i, rows):
                if d < 3:
                    return near[3 * (c * T + t) + place(d), rows, :]
                return far[0][(deep - 3) * (c * T + t) + d - 3, rows, :]

            pack_sides(info, get, ymsg, zmsg, ycomps, zcomps, X, Y, T, [layer(d)])


def pack_whole(info, f, o, near_in, near_out, start, ymsg, zmsg):
    _, T, X, Y, _ = o.shape

    def step(i, carry):
        for c in range(4):
            for t in range(T):
                o[c, t, i] = f[c, i, :, t * LANES : (t + 1) * LANES]
        return carry

    lax.fori_loop(0, X, step, 0, unroll=16)
    for side, near in enumerate((near_in, near_out)):
        _, _, layer, place = ends(info, side == 0, X, 3)
        for c in range(4):
            for t in range(T):
                for d in range(3):
                    near[start + 3 * (c * T + t) + place(d)] = o[c, t, layer(d)]
    pack_sides(info, lambda c, t, i, rows: o[c, t, i, rows, :], ymsg, zmsg, RATE_Y, RATE_Z, X, Y, T, None)


def pack_les(get, shape, inner, outer, ymsg, zmsg, info, base=0, ybase=0, zbase=0):
    pos, row, half = info[0], info[1], info[2]
    _, T, X, Y, _ = shape
    si = jnp.where(pos == 0, X - 1, 0)
    so = jnp.where(pos == 0, 0, X - 1)
    rows = lax.broadcasted_iota(jnp.int32, (8, LANES), 0)
    ys = pl.multiple_of(jnp.where(row == 0, Y - 8, 0), 8)
    turn = [jnp.where(row == 0, (r + 1) % 8, r) for r in range(8)]
    for c in range(3):
        for t in range(T):
            inner[base + c * T + t] = get(c, t, si, slice(None))
            outer[base + c * T + t] = get(c, t, so, slice(None))
            for n in range(X // 8):
                acc = jnp.zeros((8, LANES), jnp.float32)
                for r in range(8):
                    tile = get(c, t, 8 * n + r, pl.ds(ys, 8))
                    acc = jnp.where(rows == r, pltpu.roll(tile, turn[r], 0), acc)
                ymsg[ybase + (c * T + t) * (X // 8) + n] = acc

    def step(i, carry):
        for c in range(3):
            last, first = get(c, T - 1, i, slice(None)), get(c, 0, i, slice(None))
            zmsg[zbase + c * X + i] = jnp.where(half == 0, last, first)
        return carry

    lax.fori_loop(0, X, step, 0, unroll=16)


def getter(v):
    if len(v.shape) == 4:
        return lambda c, t, i, rows: v[i, c, rows, t * LANES : (t + 1) * LANES]
    return lambda c, t, i, rows: v[c, t, i, rows, :]


def pack_les_body(info, v, inner, outer, ymsg, zmsg):
    X, _, Y, Z = v.shape
    pack_les(getter(v), (3, Z // LANES, X, Y, LANES), inner, outer, ymsg, zmsg, info)


def les_body(info, offsets, v, inner, outer, ymsg, zmsg, tiles, *rest, base, ybase, zbase, advance):
    if advance:
        state, v1, own, n_in, n_out, f, ny, nz, V, LB, ACC, offset, sem = rest
    else:
        own, n_in, n_out, V, LB, ACC, offset, sem = rest
    copy_in = pltpu.make_async_copy(offsets, offset, sem)
    copy_in.start()
    pos, row, half = info[0], info[1], info[2]
    _, T, X, Y, _ = V.shape
    X, Y = X - 2, Y - 16
    get = getter(v)
    blocks = 2 * LB.shape[0]
    wide = X // blocks
    plane = wide * Y
    hi = jnp.where(pos == 0, X + 1, 0)
    ho = jnp.where(pos == 0, 0, X + 1)
    for c in range(3):
        for t in range(T):
            V[c, t, hi, 8 : 8 + Y, :] = inner[base + c * T + t]
            V[c, t, ho, 8 : 8 + Y, :] = known(outer[base + c * T + t], info[3])
            for n in range(X // 8):
                tile = ymsg[ybase + (c * T + t) * (X // 8) + n]
                zero = jnp.zeros_like(tile)
                for r in range(8):
                    low = pltpu.roll(tile, 7 - r, 0) if r < 7 else tile
                    high = pltpu.roll(tile, 8 - r, 0) if r else tile
                    V[c, t, 8 * n + r + 1, 0:8, :] = jnp.where(row == 1, low, zero)
                    V[c, t, 8 * n + r + 1, 8 + Y : 16 + Y, :] = jnp.where(row == 0, high, zero)

    def copy(i, carry):
        for c in range(3):
            for t in range(T):
                V[c, t, i + 1, 8 : 8 + Y, :] = get(c, t, i, slice(None))
        return carry

    lax.fori_loop(0, X, copy, 0, unroll=16)
    ACC[...] = jnp.zeros_like(ACC)
    lanes = lane_ids(Y)
    y = slice(8, 8 + Y)

    def step(i, carry):
        center = [[V[c, t, i + 1, y, :] for t in range(T)] for c in range(3)]
        ahead, behind = [], []
        for c in range(3 if advance else 2):
            left, right = side_tiles(zmsg[zbase + c * X + i], half)
            ahead.append(shift_tiles(center[c], left, right, 1, lanes))
            behind.append(shift_tiles(center[c], left, right, -1, lanes))
        at = lax.rem(i, 2 * wide) * Y
        at = at + jnp.where(at >= plane, plane, 0)
        b = i // (2 * wide)
        for t in range(T):
            xa = [V[c, t, i + 2, y, :] for c in range(3)]
            xb = [V[c, t, i, y, :] for c in range(3)]
            ya = [V[c, t, i + 1, 9 : 9 + Y, :] for c in range(3)]
            yb = [V[c, t, i + 1, 7 : 7 + Y, :] for c in range(3)]
            u, w, q = center[0][t], center[1][t], center[2][t]
            vx = 0.5 * ((ya[2] - yb[2]) - (ahead[1][t] - behind[1][t]))
            vy = 0.5 * ((ahead[0][t] - behind[0][t]) - (xa[2] - xb[2]))
            vz = 0.5 * ((xa[1] - xb[1]) - (ya[0] - yb[0]))
            lamb = [vy * q - vz * w, vz * u - vx * q, vx * w - vy * u]
            for c in range(3):
                high = lamb[c].astype(jnp.bfloat16)
                low = (lamb[c] - high.astype(jnp.float32)).astype(jnp.bfloat16)
                lane = slice((c * T + t) * LANES, (c * T + t + 1) * LANES)
                LB[b, pl.ds(pl.multiple_of(at, 16), Y), lane] = high
                LB[b, pl.ds(pl.multiple_of(plane + at, 16), Y), lane] = low
                if advance:
                    laplace = -6.0 * center[c][t] + ((xa[c] + xb[c]) + (ya[c] + yb[c]) + (ahead[c][t] + behind[c][t]))
                    v1[c, t, i] = center[c][t] + eddy_step * (viscosity * laplace - lamb[c])
        return carry

    lax.fori_loop(0, X, step, 0, unroll=16)

    copy_in.wait()
    for m in range(blocks // 2):
        a, b = [[tiles[2 * m + n, k] for k in (0, 1)] for n in (0, 1)]
        parts = [
            (jnp.concatenate([a[0], a[0], b[0], b[0]]), LB[m]),
            (jnp.concatenate([a[1], a[1]]), LB[m, : 2 * plane]),
            (jnp.concatenate([b[1], b[1]]), LB[m, 2 * plane :]),
        ]
        out = [
            lax.dot_general(w, x, (((0,), (0,)), ((), ())), preferred_element_type=jnp.float32) for w, x in parts
        ]
        at = (m + 1) * wide
        places = [at, at + offset[2 * m] * wide, at + offset[2 * m + 1] * wide]
        for c in range(3):
            for t in range(T):
                lane = slice((c * T + t) * LANES, (c * T + t + 1) * LANES)
                for to, value in zip(places, out):
                    for l in range(wide):
                        ACC[c, t, to + l] = ACC[c, t, to + l] + value[l * Y : (l + 1) * Y, lane]

    depth = own.shape[2]
    own[...] = ACC[:, :, wide : wide + depth]
    ti = jnp.where(pos == 0, depth + wide, 0)
    to = jnp.where(pos == 0, 0, depth + wide)
    for c in range(3):
        for t in range(T):
            for l in range(wide):
                n_in[(c * T + t) * wide + l] = ACC[c, t, ti + l]
                n_out[(c * T + t) * wide + l] = ACC[c, t, to + l]
    if advance:
        pack_whole(info, state, f, n_in, n_out, 3 * T * (wide + 1), ny, nz)
        pack_les(getter(v1), v1.shape, n_in, n_out, ny, nz, info, 3 * T * wide, T * f.shape[2], 2 * f.shape[2])


def solution(mesh):
    gx = mesh.shape["gx"]
    swap = [(0, 1), (1, 0)]
    even = [pair for k in range(gx // 2) for pair in ((2 * k, 2 * k + 1), (2 * k + 1, 2 * k))]
    odd = [pair for k in range(gx // 2 - 1) for pair in ((2 * k + 1, 2 * k + 2), (2 * k + 2, 2 * k + 1))]

    def flat(**at):
        index = 0
        for axis in mesh.axis_names:
            index = index * mesh.shape[axis] + at[axis]
        return index

    ends = [(0, 1), (1, 0)]
    hops = [
        (flat(gx=a, gy=y, grp=c), flat(gx=b, gy=y, grp=c)) for a, b in odd for y in range(mesh.shape["gy"]) for c in (0, 1)
    ] + [
        (flat(gx=g, gy=y, grp=a), flat(gx=g, gy=y, grp=b))
        for g in (0, gx - 1)
        for y in range(mesh.shape["gy"])
        for a, b in ends
    ]

    def send_in(message):
        return lax.ppermute(message, "gx", even)

    def send_out(message):
        return lax.ppermute(message, mesh.axis_names, hops)

    def send_sides(ymsg, zmsg):
        return lax.ppermute(ymsg, "gy", swap), lax.ppermute(zmsg, "grp", swap)

    def body(les_velocity, mean_mach, transfer_tiles, intersection_offset, acoustic_state):
        X2, Y, _, Z = les_velocity.shape
        X = acoustic_state.shape[0]
        T = Z // LANES
        blocks, plane = transfer_tiles.shape[0], transfer_tiles.shape[-1]
        wide = plane // Y
        v = les_velocity.transpose(0, 2, 1, 3)
        state = acoustic_state.transpose(2, 0, 1, 3)
        rate_z, smooth_z = (
            jnp.asarray(np.stack([banded(Z, weights, sign, h) for h in (0, 1)]))
            for weights, sign in ((deriv, -1), ([-filter_weight * w for w in taps[1:]], 1))
        )
        mach = jnp.broadcast_to(mean_mach[:, :, None], (X, Y, LANES))

        grid = (4, T, X, Y, LANES)
        source = (3, T, X, Y, LANES)
        near, far = (12 * T, Y, LANES), (4 * T * (wide - 3), Y, LANES)
        term = (3 * T * wide, Y, LANES)
        edge_y, edge_yy = (T * X, 8, LANES), (2 * T * X, 8, LANES)
        edge_z, edge_zz = (2 * X, Y, LANES), (4 * X, Y, LANES)
        les_x, les_y, les_z = (3 * T, Y, LANES), (3 * T * X2 // 8, 8, LANES), (3 * X2, Y, LANES)
        both_y, both_z = [(a[0] + b[0], *a[1:]) for a, b in ((edge_y, les_y), (edge_z, les_z))]
        F = pltpu.VMEM((4, T, X + 6, Y + 16, LANES), jnp.float32)
        G2 = pltpu.VMEM((2, T, X, Y, LANES), jnp.float32)
        G4 = pltpu.VMEM((4, T, X, Y, LANES), jnp.float32)
        les_scratch = [
            pltpu.VMEM((3, T, X2 + 2, Y + 16, LANES), jnp.float32),
            pltpu.VMEM((blocks // 2, 4 * plane, 3 * Z), jnp.bfloat16),
            pltpu.VMEM((3, T, X + 2 * wide, Y, LANES), jnp.float32),
            pltpu.SMEM((blocks,), jnp.int32),
            pltpu.SemaphoreType.DMA(()),
        ]
        def complete(part, halos, shared, scale, next_y, next_z, halo_base=0):
            smooth = not shared
            shapes = [near, near] if smooth else [near, far, near, far]
            sides = [edge_y, edge_z] if next_y == RATE_Y else [edge_yy, edge_zz]
            *done, ymsg, zmsg = call(
                functools.partial(
                    edge_body, smooth=smooth, scale=scale, ycomps=next_y, zcomps=next_z, halo_base=halo_base
                ),
                [*shapes, *sides],
                [part, *halos, *([shared[0], *shared[1]] if shared else [])],
            )
            nears, fars = (done, []) if smooth else (done[::2], done[1::2])
            return [part, *nears], fars, send_sides(ymsg, zmsg), (send_in(nears[0]), send_out(nears[1]))

        v_in, v_out, *sides = call(pack_les_body, [les_x, les_x, les_y, les_z], [v])
        les_edges = [send_in(v_in), send_out(v_out), *send_sides(*sides)]
        tiles = transfer_tiles[:, 0]
        at = term[0] + 3 * T
        joint = (at + near[0], Y, LANES)
        v1, S, *own, state, ym, zm = call(
            functools.partial(les_body, base=0, ybase=0, zbase=0, advance=True),
            [(3, T, X2, Y, LANES), source, joint, joint, grid, both_y, both_z],
            [intersection_offset, v, *les_edges, tiles, state],
            les_scratch,
            away=1,
            flops=4000000,
        )
        terms = (send_in(own[0]), send_out(own[1]))
        sides = send_sides(ym, zm)
        les_edges = [*terms, *sides]
        near_in, near_out = own
        halos = terms
        whole = [state, near_in, near_out]
        for step in range(STEPS):
            if step:
                terms = list(terms)
                whole[1], terms[0] = lax.optimization_barrier((whole[1], terms[0]))
            part, base = call(
                functools.partial(first_main, near_base=at if step == 0 else 0), [grid, grid], [*whole, *sides, rate_z, mach, S], [F, G2], flops=4000000
            )
            whole, fars, sides, halos = complete(
                part, halos, (mach, terms), wave_step, RATE_Y, RATE_Z, at if step == 0 else 0
            )
            if step + 1 < STEPS:
                S2, *terms2 = call(
                    functools.partial(les_body, base=term[0], ybase=edge_y[0], zbase=edge_z[0], advance=False),
                    [source, term, term],
                    [intersection_offset, v1, *les_edges, tiles],
                    les_scratch,
                    away=1,
                    flops=4000000,
                )
                whole[1], S2, *terms2 = lax.optimization_barrier((whole[1], S2, *terms2))
                terms2 = (send_in(terms2[0]), send_out(terms2[1]))
            (part,) = call(
                second_main, [grid], [*whole, *fars, *sides, rate_z, mach, S, base], [F, G2], flops=4000000
            )
            whole, fars, sides, halos = complete(part, halos, (mach, terms), 0.5 * wave_step, ALL, ALL)
            if step + 1 < STEPS:
                terms, S = terms2, S2
                (part,) = call(
                    functools.partial(smooth_main, last=False),
                    [grid],
                    [*whole, *fars, *sides, smooth_z],
                    [F, G4],
                    flops=4000000,
                )
                whole, _, sides, halos = complete(part, halos, None, 0.0, RATE_Y, RATE_Z)
        (part,) = call(
            functools.partial(smooth_main, last=True),
            [(4, X, Y, Z)],
            [*whole, *fars, *sides, smooth_z],
            [F, G4],
            flops=4000000,
        )
        (state,) = call(last_body, [(4, X, Y, Z)], [part, *halos])
        return state.transpose(1, 2, 0, 3)

    placed = (
        P("gx", "gy", None, "grp"),
        P("gx", "gy"),
        P("gx", "gy", None, None, None),
        P("gx"),
        P("gx", "gy", None, "grp"),
    )
    return jax.shard_map(body, mesh=mesh, in_specs=placed, out_specs=P("gx", "gy", None, "grp"), check_vma=False)
```
